32 devices in a mesh: exp: 4 (over z), dp: 8 (over y, x, core).
Axes of the slice: x: 2, y: 2, z: 4, core: 2. Of those that a mesh axis runs over, the one named last changes fastest.
Arguments:
- tokens: bfloat16 [8, 1024, 512], P('dp', 'exp'), may hold values from -6 to 6
- cotangent: bfloat16 [8, 1024, 512], P('dp', 'exp'), may hold values from -6 to 6
- routes: int32 [2, 8, 1024, 8], P(None, 'dp'), may hold values from 0 to 23, all different within a row; in each aligned block of 256 rows (0 to 255, 256 to 511, ..., all dimensions but the last counted through in order) at most 128 rows name the same one
- keep: int32 [8, 1024], P('dp'), may hold values 0 or 1
- lengths: int32 [8, 9], P('dp'), may hold values from 1 to 896, 1024 in all within a row
- norm1_gain: float32 [2, 512], replicated, may hold values from 0.1 to 1.9
- norm1_bias: float32 [2, 512], replicated, may hold values from -1 to 1
- w_kv: bfloat16 [2, 512, 128], replicated, may hold values from -0.25 to 0.25
- w_router: bfloat16 [2, 512, 24], replicated, may hold values from -0.125 to 0.125
- w_query: bfloat16 [2, 24, 512, 64], P(None, 'exp'), may hold values from -0.625 to 0.625
- w_out: bfloat16 [2, 24, 64, 512], P(None, 'exp'), may hold values from -2 to 2
- norm2_gain: float32 [2, 512], replicated, may hold values from 0.1 to 1.9
- norm2_bias: float32 [2, 512], replicated, may hold values from -1 to 1
- w_up: bfloat16 [2, 512, 2048], replicated, may hold values from -0.25 to 0.25
- w_down: bfloat16 [2, 2048, 512], replicated, may hold values from -0.125 to 0.125
Outputs:
- activations: bfloat16 [8, 1024, 512], P('dp', 'exp')
- input_grad: float32 [8, 1024, 512], P('dp', 'exp')
- norm1_gain_grad: float32 [2, 512], replicated
- norm1_bias_grad: float32 [2, 512], replicated
- w_kv_grad: float32 [2, 512, 128], replicated
- w_router_grad: float32 [2, 512, 24], replicated
- w_query_grad: float32 [2, 24, 512, 64], P(None, 'exp')
- w_out_grad: float32 [2, 24, 64, 512], P(None, 'exp')
- norm2_gain_grad: float32 [2, 512], replicated
- norm2_bias_grad: float32 [2, 512], replicated
- w_up_grad: float32 [2, 512, 2048], replicated
- w_down_grad: float32 [2, 2048, 512], replicated
- counts: float32 [2, 24], replicated
The draws below stay inside these ranges and needn't reach their ends.
Inputs may be any that keep to these rules, and one draw needn't show every extreme that they name: `routes`: in each layer, the rows of one device (aligned blocks of 256 rows of a group) name no head expert more than 128 times, a bound that some block reaches. Each group's lengths sum to 1024 and the largest is exactly 896.
All inputs are finite; a program needn't handle non-finite values. No bound on the sum of `keep` on one device may be relied on, other than what follows from the above.
Results may differ from the reference program's by a relative error of at most 0.025.
The reference program's roundings to bfloat16 on the way count: a program that leaves them out, or rounds other values in their place, can miss the bound.
Values may be sent and summed in bfloat16 or wider, within the bound.
A program may use at most 128 MiB of HBM per device.

```python
import math
import jax
import jax.numpy as jnp
import numpy as np
from jax import lax

D = 512
FF = 2048
HEADS = 24
HEAD = 64
TOPK = 8
LAYERS = 2
SEQS = 9
TOK_DEV = 256
CAP = 128
GROUP = 1024
GROUPS = 8
LONGEST = 896


def place_ends(values, own_key, low, largest):
    longest = values.shape.index(max(values.shape))
    spots = []
    for shift in (0, 1):
        where = [jax.random.randint(jax.random.fold_in(own_key, axis), (), 0, length) for axis, length in enumerate(values.shape)]
        where[longest] = (where[longest] + shift) % values.shape[longest]
        spots.append(tuple(where))
    return values.at[spots[0]].set(low).at[spots[1]].set(largest)


def block_levels(rng, shape, pieces, low, largest):
    factor_of, own = 1.0, jax.random.fold_in(rng, 6)
    for dim, parts in pieces:
        draws = jnp.exp(jax.random.uniform(jax.random.fold_in(own, dim), (parts,), jnp.float32, low / len(pieces), largest / len(pieces)))
        factor_of = factor_of * jnp.repeat(draws, shape[dim] // parts).reshape([-1 if axis == dim else 1 for axis in range(len(shape))])
    return factor_of


def split_up(count, total, bound, slope):
    portions = [(1 << 20) // math.isqrt(grade ** slope) + 1 for grade in range(2, count + 1)]
    surplus, holding = total - bound - (count - 1), [1] * (count - 1)
    while surplus > 0:
        movable = [i for i in range(count - 1) if holding[i] < bound]
        whole, remaining = sum([portions[i] for i in movable]), surplus
        for i in movable:
            more = min(bound - holding[i], max(1, remaining * portions[i] // whole), surplus)
            holding[i] = holding[i] + more
            surplus = surplus - more
    return np.array([bound] + holding)


def uneven(rng, count, total, most, skew):
    if count == 2:
        one = jax.random.randint(rng, (), max(1, total - most), min(most, total - 1) + 1)
        return jnp.stack([one, total - one])
    sizes = jnp.asarray(split_up(count, total, most, skew), jnp.int32)
    couples = (count - 1) // 2
    giver, taker = sizes[1:1 + 2 * couples:2], sizes[2:2 + 2 * couples:2]
    room = jnp.minimum(giver - 1, most - taker)
    moved = jax.random.randint(jax.random.fold_in(rng, 1), (couples,), 0, 1 << 20) % (room + 1)
    sizes = sizes.at[1:1 + 2 * couples:2].set(giver - moved).at[2:2 + 2 * couples:2].set(taker + moved)
    return sizes[jax.random.permutation(jax.random.fold_in(rng, 2), count)]


def deal_out(key, own, number, rows, amount, top, limit, skew):
    order = jax.random.permutation(key, amount)
    packed, usual = portions_of(amount, rows * top, limit, skew, True), portions_of(amount, rows * top, limit, skew, False)
    places = jnp.arange(amount)

    def named(sizes, rotation):
        used = int((sizes > 0).sum())
        fixed = max(1, used // 4)
        shifted = fixed + (places - fixed + rotation * (used - fixed)) % max(1, amount - fixed)
        return jnp.zeros((amount,), jnp.int32).at[order[jnp.where(places < fixed, places, shifted)]].set(jnp.asarray(sizes, jnp.int32))

    sizes = jnp.where(number % 4 == 0, named(packed, number // 4), named(usual, number - number // 4 - 1))
    mixed = jax.random.permutation(jax.random.fold_in(own, 3), amount)
    donor, sink = mixed[0:amount // 2 * 2:2], mixed[1:amount // 2 * 2:2]
    room = jnp.minimum(sizes[donor] - 1, limit - sizes[sink]) // 2
    room = jnp.where((donor == order[0]) | (sink == order[0]) | (sizes[sink] == 0), 0, jnp.maximum(room, 0))
    shifted = jax.random.randint(jax.random.fold_in(own, 4), (amount // 2,), 0, 1 << 20) % (room + 1)
    sizes = sizes.at[donor].add(-shifted).at[sink].add(shifted)
    items = jnp.searchsorted(jnp.cumsum(sizes), jnp.arange(rows * top), side="right").astype(jnp.int32)
    listing = items.reshape(top, rows).T
    listing = listing[jax.random.permutation(jax.random.fold_in(own, 1), rows)]
    rotation = jax.random.randint(jax.random.fold_in(own, 2), (rows, 1), 0, top)
    return jnp.take_along_axis(listing, (jnp.arange(top)[None, :] + rotation) % top, axis=1)


def portions_of(number_of, total, most, lean, full):
    weights = [(1 << 20) // math.isqrt(standing ** lean) + 1 for standing in range(1, number_of + 1)]
    largest = most if full else min(most, max(-(-total // number_of), total * weights[0] // sum(weights)))
    least = 1 if total - largest >= number_of - 1 else 0
    holding, spare = [largest] + [least] * (number_of - 1), total - largest - least * (number_of - 1)
    while spare > 0:
        movable = [i for i in range(1, number_of) if holding[i] < largest] or [i for i in range(1, number_of) if holding[i] < most]
        pool, remaining = sum([weights[i] for i in movable]), spare
        for i in movable:
            more = min(most - holding[i], max(1, remaining * weights[i] // pool), spare)
            holding[i] = holding[i] + more
            spare = spare - more
    return np.array(holding)


def noise(own_key, dims, scale, limit, split=(), kind=jnp.bfloat16):
    values = scale * jax.random.normal(own_key, dims, jnp.float32)
    if split:
        values = values * block_levels(own_key, dims, split, -0.22, 0.18)
    return jnp.clip(values, -limit, limit).astype(kind)


def setup_inputs(seed: int = 0) -> dict:
    seeds = jax.random.split(jax.random.key(seed), 16)
    tokens = noise(seeds[0], (GROUPS, GROUP, D), 1.0, 6.0, ((0, 8), (1, 4)))
    cotangent = noise(seeds[1], (GROUPS, GROUP, D), 1.0, 6.0, ((0, 8), (1, 4)))
    routes_keys = jax.random.split(jax.random.fold_in(seeds[2], 1), LAYERS * GROUPS * GROUP // TOK_DEV)
    routes_turns = jax.random.permutation(jax.random.fold_in(seeds[2], 3), LAYERS * GROUPS * GROUP // TOK_DEV)
    routes = jax.vmap(lambda own, number: deal_out(jax.random.fold_in(seeds[2], 2), own, number, TOK_DEV, HEADS, TOPK, CAP, 1))(routes_keys, routes_turns).reshape((LAYERS, GROUPS, GROUP, TOPK))
    keep = place_ends((jax.random.randint(seeds[3], (GROUPS, GROUP), 0, 8) < 7).astype(jnp.int32), jax.random.fold_in(seeds[3], 1), 0, 1)
    lengths = jax.vmap(lambda own: uneven(own, SEQS, GROUP, LONGEST, 2))(jax.random.split(seeds[4], GROUPS)).reshape((GROUPS, SEQS)).astype(jnp.int32)
    norm1_gain = jnp.clip(1.0 + 0.18 * jax.random.normal(seeds[5], (LAYERS, D), jnp.float32), 0.1, 1.9)
    norm1_bias = noise(seeds[6], (LAYERS, D), 0.2, 1.0, (), jnp.float32)
    w_kv = noise(seeds[7], (LAYERS, D, 2 * HEAD), D ** -0.5, 0.25)
    w_router = noise(seeds[8], (LAYERS, D, HEADS), (4 * D) ** -0.5, 0.125)
    w_query = noise(seeds[9], (LAYERS, HEADS, D, HEAD), (D // 6) ** -0.5, 0.625, ((1, 4),))
    w_out = noise(seeds[10], (LAYERS, HEADS, HEAD, D), (HEAD // 8) ** -0.5, 2.0, ((1, 4),))
    norm2_gain = jnp.clip(1.0 + 0.18 * jax.random.normal(seeds[11], (LAYERS, D), jnp.float32), 0.1, 1.9)
    norm2_bias = noise(seeds[12], (LAYERS, D), 0.2, 1.0, (), jnp.float32)
    w_up = noise(seeds[13], (LAYERS, D, FF), D ** -0.5, 0.25)
    w_down = noise(seeds[14], (LAYERS, FF, D), FF ** -0.5, 0.125)
    return {"tokens": tokens, "cotangent": cotangent, "routes": routes, "keep": keep, "lengths": lengths, "norm1_gain": norm1_gain, "norm1_bias": norm1_bias, "w_kv": w_kv, "w_router": w_router, "w_query": w_query, "w_out": w_out, "norm2_gain": norm2_gain, "norm2_bias": norm2_bias, "w_up": w_up, "w_down": w_down}


@jax.custom_vjp
def low(v):
    return lax.optimization_barrier(v.astype(jnp.bfloat16)).astype(jnp.float32)

@jax.custom_vjp
def low_back(v):
    return v

def low_keep(v):
    return (low(v), None)

def low_pass(kept, grad):
    return (grad,)

def back_keep(v):
    return (v, None)

def back_low(kept, grad):
    return (low(grad),)
low.defvjp(low_keep, low_pass)
low_back.defvjp(back_keep, back_low)
epsilon = 1e-05
neg_big = -1e+30

def product(left, right):
    return jnp.dot(left, right, precision=lax.Precision.HIGHEST, preferred_element_type=jnp.float32)

def normalize(values, gain, bias):
    center = values - lax.optimization_barrier(jnp.mean(values, axis=-1, keepdims=True))
    spread = lax.optimization_barrier(jnp.mean(center * center, axis=-1, keepdims=True))
    return center * lax.rsqrt(spread + epsilon) * gain + bias

def attend(queries, keyval, segment, keep_keys):
    group = queries.shape[0]
    block = min(512, group)
    keys = keyval[:, :HEAD]
    values = keyval[:, HEAD:]
    where = jnp.arange(group, dtype=jnp.int32)

    @jax.checkpoint
    def one_block(item):
        block_rows, first = item
        position = first + jnp.arange(block, dtype=jnp.int32)
        scores = low_back(product(block_rows, keys.T) * 0.125)
        same = segment[position][:, None] == segment[None, :]
        causal = where[None, :] <= position[:, None]
        usable = (keep_keys[None, :] > 0) | (where[None, :] == position[:, None])
        allowed = same & causal & usable
        masked = jnp.where(allowed, scores, neg_big)
        top = lax.optimization_barrier(jnp.max(masked, axis=1, keepdims=True))
        spread = jnp.where(allowed, jnp.exp(masked - top), 0.0)
        shares = spread / lax.optimization_barrier(jnp.sum(spread, axis=1, keepdims=True))
        return product(low(shares), values)
    starts = (jnp.arange(group // block) * block).astype(jnp.int32)
    out = lax.map(one_block, (queries.reshape(group // block, block, HEAD), starts))
    return out.reshape(group, HEAD)

def layer(stream, params, chosen, segment, keep_keys):
    gain1, bias1, w_kv, w_router, w_query, w_out, gain2, bias2, w_up, w_down = params
    normed = low(normalize(stream, gain1, bias1))
    keyval = low_back(low(product(normed, w_kv)))
    logits = low_back(product(normed, w_router))
    picked = jnp.take_along_axis(logits, chosen, axis=1)
    picked = jnp.exp(picked - lax.optimization_barrier(jnp.max(picked, axis=1, keepdims=True)))
    gates = picked / lax.optimization_barrier(jnp.sum(picked, axis=1, keepdims=True))
    one_hot = (chosen[:, :, None] == jnp.arange(HEADS, dtype=jnp.int32)[None, None, :]).astype(stream.dtype)
    dense = jnp.einsum('tk,tke->te', gates, one_hot, precision=lax.Precision.HIGHEST)

    def expert(carry, item):
        query_weight, out_weight, gate = item
        queries = low_back(low(product(low_back(normed), query_weight)))
        attended = low_back(low(attend(queries, keyval, segment, keep_keys)))
        result = low_back(low(product(attended, out_weight)))
        return (carry + gate[:, None] * result, None)
    mix, _ = lax.scan(expert, jnp.zeros_like(stream), (w_query, w_out, dense.T))
    middle = stream + mix
    normed2 = low(normalize(middle, gain2, bias2))
    upper = low_back(product(normed2, w_up))
    active = low(jax.nn.gelu(upper, approximate=True))
    return middle + low_back(product(active, w_down))

def reference(tokens, cotangent, routes, keep, lengths, norm1_gain, norm1_bias, w_kv, w_router, w_query, w_out, norm2_gain, norm2_bias, w_up, w_down):
    weights = tuple((w.astype(jnp.float32) for w in (norm1_gain, norm1_bias, w_kv, w_router, w_query, w_out, norm2_gain, norm2_bias, w_up, w_down)))
    zero_grads = tuple((jnp.zeros(w.shape, jnp.float32) for w in weights))
    zero_counts = jnp.zeros((LAYERS, HEADS), jnp.float32)

    def per_group(carry, item):
        sums, count_sum = carry
        group_in, group_cot, group_routes, keep_group, group_lengths = item
        ends = jnp.cumsum(group_lengths).astype(jnp.int32)
        where = jnp.arange(GROUP, dtype=jnp.int32)
        segment = lax.optimization_barrier(jnp.sum((where[:, None] >= ends[None, :-1]).astype(jnp.int32), axis=1))

        def forward(stream, params):
            for layer_no in range(LAYERS):
                stream = layer(stream, tuple((p[layer_no] for p in params)), group_routes[layer_no], segment, keep_group)
            return stream
        out, pullback = jax.vjp(forward, group_in.astype(jnp.float32), weights)
        keep_float = keep_group.astype(jnp.float32)
        grad_in, grad_weights = pullback(group_cot.astype(jnp.float32) * keep_float[:, None])
        hits = (group_routes[..., None] == jnp.arange(HEADS, dtype=jnp.int32)).astype(jnp.float32)
        counted = lax.optimization_barrier(jnp.sum(hits * keep_float[None, :, None, None], axis=(1, 2)))
        sums = tuple((a + b for a, b in zip(sums, grad_weights)))
        return ((sums, count_sum + counted), (out.astype(jnp.bfloat16), grad_in))
    (sums, count_sum), (outs, grads_in) = lax.scan(per_group, (zero_grads, zero_counts), (tokens, cotangent, jnp.moveaxis(routes, 1, 0), keep, lengths))
    return (outs, grads_in, sums[0], sums[1], sums[2], sums[3], sums[4], sums[5], sums[6], sums[7], sums[8], sums[9], count_sum)
```

```python
from functools import partial
import math

import jax
import jax.numpy as jnp
from jax import lax
from jax.experimental import pallas as pl
from jax.experimental.pallas import tpu as pltpu
from jax.sharding import PartitionSpec as P

F32 = jnp.float32
BF16 = jnp.bfloat16
LANES = 128
epsilon = 1e-05
neg_big = -1e30
never = 1 << 30
gelu_c = 0.7978845608028654
gelu_a = 0.044715
VMEM_LIMIT = 56 << 20


def nn(a, b):
    return jnp.dot(a, b, preferred_element_type=F32)


def nt(a, b):
    return lax.dot_general(a, b, (((1,), (1,)), ((), ())), preferred_element_type=F32)


def tn(a, b):
    return lax.dot_general(a, b, (((0,), (0,)), ((), ())), preferred_element_type=F32)


def iota(shape, axis):
    return lax.broadcasted_iota(jnp.int32, shape, axis)


def norm_parts(values):
    center = values - jnp.mean(values, axis=-1, keepdims=True)
    spread = jnp.mean(center * center, axis=-1, keepdims=True)
    scale = lax.rsqrt(spread + epsilon)
    return center * scale, scale


def norm_back(hat, scale, gain, grad):
    scaled = grad * gain
    first = jnp.mean(scaled, axis=-1, keepdims=True)
    second = jnp.mean(scaled * hat, axis=-1, keepdims=True)
    back = scale * (scaled - first - hat * second)
    return back, jnp.sum(grad * hat, axis=0, keepdims=True), jnp.sum(grad, axis=0, keepdims=True)


def gelu_parts(v):
    inner = jnp.tanh(gelu_c * (v + gelu_a * v * v * v))
    half = 0.5 * (1.0 + inner)
    return v * half, half + 0.5 * v * (1.0 - inner * inner) * gelu_c * (1.0 + 3.0 * gelu_a * v * v)


def lane_half(shape):
    return (iota(shape, 1) >= LANES // 2).astype(jnp.int32)


def select_tiles(dense, chosen):
    out = jnp.zeros(chosen.shape, F32)
    for tile in range(dense.shape[1] // LANES):
        out = jnp.where(chosen == 2 * tile, dense[:, tile * LANES : (tile + 1) * LANES], out)
    return out


def place_tiles(dense, chosen, values):
    for tile in range(dense.shape[1] // LANES):
        where = slice(tile * LANES, (tile + 1) * LANES)
        dense[:, where] = jnp.where(chosen == 2 * tile, values, dense[:, where])


def own_columns(ref, count):
    start = lax.axis_index("exp") * count
    return ref[:, pl.ds(pl.multiple_of(start, count), count)]


def spread_routes(routes, spread):
    topk, count, lanes = spread.shape
    own = own_columns(routes, count)
    for k in range(topk):
        spread[k] = jnp.broadcast_to(own[k : k + 1, :], (lanes, count)).T


def fill_mask(lengths, keep, mask):
    group, count = mask.shape
    start = lax.axis_index("exp") * count
    position = start + iota((1, count), 1)
    low = jnp.zeros((1, count), jnp.int32)
    end = 0
    for s in range(lengths.shape[1] - 1):
        end = end + lengths[0, s]
        low = jnp.where(position >= end, end, low)
    kept = jnp.broadcast_to(keep[...], (LANES, group)).T
    kept = jnp.concatenate([kept] * (count // LANES), axis=1)
    key = iota((group, count), 0)
    usable = jnp.where(kept > 0, key, never)
    allowed = ((usable >= low) & (usable <= position)) | (key == position)
    mask[...] = jnp.where(allowed, 0.0, neg_big)


def split_keyval(keyval):
    both = keyval.astype(F32)
    swapped = pltpu.roll(both, LANES // 2, 1)
    first = iota(both.shape, 1) < LANES // 2
    return jnp.where(first, both, swapped), jnp.where(first, swapped, both)


def pre_layer(x, gain1, bias1, w_kv, normed, keyval_own):
    hat, _ = norm_parts(x)
    normed[...] = (hat * gain1 + bias1).astype(BF16)
    keyval_own[...] = nn(normed[...], w_kv).astype(BF16)


def make_gates(normed, w_router, spread):
    logits = nt(normed, w_router)
    experts = logits.shape[1]
    lanes = iota(logits.shape, 1)
    picked = spread[0][:, :experts] == lanes
    for k in range(1, spread.shape[0]):
        picked = picked | (spread[k][:, :experts] == lanes)
    top = jnp.max(jnp.where(picked, logits, neg_big), axis=1, keepdims=True)
    shares = jnp.where(picked, jnp.exp(jnp.minimum(logits - top, 0.0)), 0.0)
    return shares / jnp.sum(shares, axis=1, keepdims=True), picked


def gate_column(gates, spread_k):
    lanes = iota(gates.shape, 1)
    return jnp.sum(
        jnp.where(spread_k[:, : gates.shape[1]] == lanes, gates, 0.0), axis=1, keepdims=True
    )


def layer_forward(x, normed, weights, mask, spread, dense, gated, kept):
    count = normed.shape[0]
    gates, picked = make_gates(normed[...], weights.w_router[...], spread)
    kept.gates[...] = gates
    dense[...] = nt(normed[...], weights.w_query[...]).astype(BF16).astype(F32) * 0.125
    gated[...] = jnp.zeros(gated.shape, F32)
    keys, values = split_keyval(kept.keyval[...])
    keys = keys.astype(BF16)
    values_t = values.T.astype(BF16)

    def slot(k, carry):
        which = spread[k]
        chosen = which - lane_half((count, LANES))
        query = select_tiles(dense, chosen).astype(BF16)
        kept.query[k] = query
        scores = nt(keys, query) + mask[...]
        top = jnp.max(scores, axis=0, keepdims=True)
        shares = jnp.exp(scores - top)
        total = jnp.sum(shares, axis=0, keepdims=True)
        kept.lse[k] = jnp.broadcast_to(top + jnp.log(total), kept.lse.shape[1:])
        shares = (shares * (1.0 / total)).astype(BF16)
        attended = nn(values_t, shares).T.astype(BF16)
        kept.attended[k] = attended
        gate = gate_column(kept.gates[...], which)
        place_tiles(gated, chosen, gate * attended.astype(F32))
        return carry

    lax.fori_loop(0, spread.shape[0], slot, 0)
    kept.gated[...] = gated[...].astype(BF16)
    middle = x + nn(kept.gated[...], weights.w_out[...])
    kept.middle[...] = middle
    hat, _ = norm_parts(middle)
    normed2 = (hat * weights.gain2[...] + weights.bias2[...]).astype(BF16)
    active = gelu_parts(nn(normed2, weights.w_up[...]))[0].astype(BF16)
    return middle + nn(active, weights.w_down[...]), picked


def layer_back(stream_grad, normed, weights, mask, spread, dense, gated, kept, sums, out):
    count, width = normed.shape
    hidden = weights.w_up.shape[1]
    branch = stream_grad.astype(BF16)
    hat2, scale2 = norm_parts(kept.middle[...])
    normed2 = (hat2 * weights.gain2[...] + weights.bias2[...]).astype(BF16)
    normed2_t = normed2.astype(F32).T.astype(BF16)
    sums.wide[...] = jnp.zeros(sums.wide.shape, F32)

    blocks = out.up.shape[0]
    piece = hidden // blocks
    own = weights.w_query.shape[0] // blocks

    def part(c, carry):
        cols = pl.ds(pl.multiple_of(c * piece, piece), piece)
        active, slope = gelu_parts(nn(normed2, weights.w_up[:, cols]))
        out.down[c, 0:piece, :] = nn(active.T.astype(BF16), branch).astype(BF16)
        upper_grad = (nt(branch, weights.w_down[cols, :]) * slope).astype(BF16)
        out.up[c, 0:width, :] = nn(normed2_t, upper_grad).astype(BF16)
        sums.wide[...] += nt(upper_grad, weights.w_up[:, cols])
        return carry

    lax.fori_loop(0, blocks, part, 0)
    back, gain2_grad, bias2_grad = norm_back(hat2, scale2, weights.gain2[...], sums.wide[...])
    out.small[2:3, :] = gain2_grad
    out.small[3:4, :] = bias2_grad
    middle_grad = stream_grad + back
    out.middle_grad[...] = middle_grad
    rounded = middle_grad.astype(BF16)
    gated_t = kept.gated[...].astype(F32).T.astype(BF16)
    for block in range(blocks):
        rows = slice(block * own, (block + 1) * own)
        out.w_out[block, 0:own, :] = nn(gated_t[rows], rounded).astype(BF16)
    dense[...] = nt(rounded, weights.w_out[...])
    gated[...] = jnp.zeros(gated.shape, F32)
    keys, values = split_keyval(kept.keyval[...])
    keys_t = keys.T.astype(BF16)
    keys = keys.astype(BF16)
    values = values.astype(BF16)
    sums.keys[...] = jnp.zeros(sums.keys.shape, F32)
    sums.values[...] = jnp.zeros(sums.values.shape, F32)
    sums.gates[...] = jnp.zeros(sums.gates.shape, F32)
    lanes = iota(sums.gates.shape, 1)

    def slot(k, carry):
        which = spread[k]
        chosen = which - lane_half((count, LANES))
        grad = select_tiles(dense, chosen)
        gate = gate_column(kept.gates[...], which)
        gate_grad = jnp.sum(grad * kept.attended[k].astype(F32), axis=1, keepdims=True)
        sums.gates[...] += jnp.where(which[:, : lanes.shape[1]] == lanes, gate * gate_grad, 0.0)
        att_grad = (gate * grad).astype(BF16)
        query = kept.query[k]
        shares = jnp.exp(nt(keys, query) + mask[...] - kept.lse[k, 0:1, :])
        sums.values[...] += nn(shares.astype(BF16), att_grad)
        share_grad = nt(values, att_grad)
        score_grad = shares * (share_grad - jnp.sum(share_grad * shares, axis=0, keepdims=True))
        score_grad = score_grad.astype(BF16)
        sums.keys[...] += nn(score_grad, query)
        query_grad = nn(keys_t, score_grad).T * 0.125
        place_tiles(gated, chosen, query_grad.astype(BF16).astype(F32))
        return carry

    lax.fori_loop(0, kept.query.shape[0], slot, 0)
    both_keys = sums.keys[...] + pltpu.roll(sums.keys[...], LANES // 2, 1)
    both_values = sums.values[...] + pltpu.roll(sums.values[...], LANES // 2, 1)
    first = iota(both_keys.shape, 1) < LANES // 2
    out.keyval[...] = jnp.where(first, both_keys, both_values).astype(BF16)
    weighted = sums.gates[...]
    logit_grad = weighted - kept.gates[...] * jnp.sum(weighted, axis=1, keepdims=True)
    logit_grad = logit_grad.astype(BF16)
    out.router[...] = tn(logit_grad, normed[...])
    query_grad = gated[...].astype(BF16)
    query_grad_t = gated[...].T.astype(BF16)
    for block in range(blocks):
        rows = slice(block * own, (block + 1) * own)
        out.w_query[block, 0:own, :] = nn(query_grad_t[rows], normed[...]).astype(BF16)
    out.normed_grad[...] = nn(query_grad, weights.w_query[...]) + nn(logit_grad, weights.w_router[...])


def layer_finish(x, normed, received, gain1, w_kv, middle_grad, normed_grad, keyval_out, small):
    total = received[0].astype(F32)
    for j in range(1, received.shape[0]):
        total = total + received[j].astype(F32)
    total = total.astype(BF16)
    keyval_out[...] = nn(total.astype(F32).T.astype(BF16), normed[...]).astype(BF16)
    grad = normed_grad[...] + nt(total, w_kv)
    hat, scale = norm_parts(x)
    back, gain1_grad, bias1_grad = norm_back(hat, scale, gain1, grad)
    small[0:1, :] = gain1_grad
    small[1:2, :] = bias1_grad
    return middle_grad[...] + back


def count_chosen(picked, keep, small):
    count, experts = picked.shape
    kept = jnp.broadcast_to(own_columns(keep, count).astype(F32), (LANES, count)).T[:, :experts]
    small[4:5, 0:experts] = jnp.sum(jnp.where(picked, kept, 0.0), axis=0, keepdims=True)


class Refs:
    def __init__(self, **refs):
        self.__dict__.update(refs)


def named(names, refs):
    return Refs(**dict(zip(names, refs[: len(names)]))), refs[len(names) :]


def weights_of(layer, refs):
    weights, refs = named(WEIGHTS, refs)
    for name in ("gain1", "bias1", "gain2", "bias2"):
        setattr(weights, name, getattr(weights, name).at[pl.ds(layer, 1), :])
    return weights, refs


WEIGHTS = ("gain1", "bias1", "w_kv", "w_router", "w_query", "w_out", "gain2", "bias2", "w_up", "w_down")
KEPT = ("keyval", "gates", "query", "lse", "attended", "gated", "middle")
SUMS = ("wide", "keys", "values", "gates")
OUT = ("up", "down", "w_out", "w_query", "router", "keyval", "small", "middle_grad", "normed_grad")
LATER = ("x", "normed", "received", "gain1", "w_kv", "middle_grad", "normed_grad", "small")


def pre_kernel(x, gain1, bias1, w_kv, normed, keyval_own):
    pre_layer(x[...].astype(F32), gain1[0:1, :], bias1[0:1, :], w_kv[...], normed, keyval_own)


def first_kernel(*refs):
    weights, refs = weights_of(0, refs)
    (x, normed, keyval, routes, lengths, keep, next_gain1, next_bias1, next_w_kv), refs = refs[:9], refs[9:]
    kept, refs = named(KEPT[1:], refs)
    kept.keyval = keyval
    (stream, next_normed, next_keyval, small), refs = refs[:4], refs[4:]
    mask, spread, dense, gated = refs
    fill_mask(lengths, keep, mask)
    spread_routes(routes, spread)
    result, picked = layer_forward(
        x[...].astype(F32), normed, weights, mask, spread, dense, gated, kept
    )
    small[...] = jnp.zeros(small.shape, F32)
    count_chosen(picked, keep, small)
    stream[...] = result
    pre_layer(result, next_gain1[1:2, :], next_bias1[1:2, :], next_w_kv[...], next_normed, next_keyval)


def turn_kernel(*refs):
    weights, refs = weights_of(1, refs)
    (x, normed, keyval, routes, lengths, keep, cotangent), refs = refs[:7], refs[7:]
    (activations,), refs = refs[:1], refs[1:]
    out, refs = named(OUT, refs)
    kept, refs = named(KEPT[1:], refs)
    kept.keyval = keyval
    sums, refs = named(SUMS, refs)
    mask, spread, dense, gated = refs
    fill_mask(lengths, keep, mask)
    spread_routes(routes, spread)
    result, picked = layer_forward(x[...], normed, weights, mask, spread, dense, gated, kept)
    activations[...] = result.astype(BF16)
    count = x.shape[0]
    kept_col = jnp.broadcast_to(own_columns(keep, count).astype(F32), (LANES, count)).T
    kept_col = jnp.concatenate([kept_col] * (x.shape[1] // LANES), axis=1)
    out.small[...] = jnp.zeros(out.small.shape, F32)
    count_chosen(picked, keep, out.small)
    stream_grad = cotangent[...].astype(F32) * kept_col
    layer_back(stream_grad, normed, weights, mask, spread, dense, gated, kept, sums, out)


def back_kernel(*refs):
    weights, refs = weights_of(0, refs)
    later, refs = named(LATER, refs)
    (normed, routes, lengths, keep, small), refs = refs[:5], refs[5:]
    kept, refs = named(KEPT, refs)
    (later_keyval, later_small), refs = refs[:2], refs[2:]
    out, refs = named(OUT, refs)
    sums, refs = named(SUMS, refs)
    mask, spread, dense, gated = refs
    later_small[...] = later.small[...]
    out.small[...] = small[...]
    stream_grad = layer_finish(
        later.x[...], later.normed, later.received, later.gain1[1:2, :], later.w_kv[...],
        later.middle_grad, later.normed_grad, later_keyval, later_small,
    )
    fill_mask(lengths, keep, mask)
    spread_routes(routes, spread)
    layer_back(stream_grad, normed, weights, mask, spread, dense, gated, kept, sums, out)


def end_kernel(x, normed, received, gain1, w_kv, middle_grad, normed_grad, small_in, keyval_out, small, grad):
    small[...] = small_in[...]
    grad[...] = layer_finish(
        x[...].astype(F32), normed, received, gain1[0:1, :], w_kv[...], middle_grad, normed_grad,
        keyval_out, small,
    )


def share_kernel(n, scatter, mine, everyones, send_sem, recv_sem):
    me = lax.axis_index("exp")
    rows = everyones.shape[1]
    barrier = pltpu.get_barrier_semaphore()
    others = [lax.rem(me + step, n) for step in range(1, n)]
    for other in others:
        pl.semaphore_signal(
            barrier, inc=1, device_id={"exp": other}, device_id_type=pl.DeviceIdType.MESH
        )

    def part(owner):
        return mine.at[pl.ds(pl.multiple_of(owner * rows, rows), rows)] if scatter else mine

    pl.semaphore_wait(barrier, n - 1)
    copies = []
    for step, other in enumerate(others):
        copy = pltpu.make_async_remote_copy(
            src_ref=part(other),
            dst_ref=everyones.at[me],
            send_sem=send_sem.at[step],
            recv_sem=recv_sem.at[step],
            device_id={"exp": other},
            device_id_type=pl.DeviceIdType.MESH,
        )
        copy.start()
        copies.append(copy)
    everyones[me] = part(me)[...]
    for copy in copies:
        copy.wait()


def vmem():
    return pl.BlockSpec(memory_space=pltpu.VMEM)


def axis_sizes():
    chips = lax.axis_size("dp") // 2
    across = math.isqrt(chips)
    across = across if across * across == chips else chips
    return {"c": 2, "x": across, "y": chips // across, "z": lax.axis_size("exp")}


def place_of():
    size = axis_sizes()
    d = lax.axis_index("dp")
    at = {"c": lax.rem(d, 2), "x": lax.rem(d // 2, size["x"]), "y": d // (2 * size["x"]), "z": lax.axis_index("exp")}
    return at, size


def peers_of(axis, at, size):
    out = []
    for step in range(1, size[axis]):
        where = dict(at)
        where[axis] = lax.rem(at[axis] + step, size[axis])
        out.append((where[axis], {"exp": where["z"], "dp": (where["y"] * size["x"] + where["x"]) * 2 + where["c"]}))
    return out


def greet(axes, at, size):
    barrier = pltpu.get_barrier_semaphore()
    total = 0
    for axis in axes:
        for _, device in peers_of(axis, at, size):
            pl.semaphore_signal(barrier, inc=1, device_id=device, device_id_type=pl.DeviceIdType.MESH)
            total += 1
    pl.semaphore_wait(barrier, total)


class Chunk:
    def __init__(self, array, first, rows, order, kind, result, layer, held_here):
        self.array, self.first, self.rows, self.order = array, first, rows, order
        self.kind, self.result, self.layer, self.held_here = kind, result, layer, held_here

    def shapes(self, blocks, width, size):
        own = (blocks, self.rows // size[self.order[0]], width)
        z, rows = blocks, self.rows
        got = []
        for axis in self.order:
            if axis == "z":
                z = 1
            else:
                rows = rows // size[axis]
            got.append((size[axis] - 1, z, rows, width))
        return ([] if self.held_here else [own]) + got


class Sums:
    def __init__(self, chunks, sources, results, scratch, sems):
        self.chunks, self.sources, self.results = chunks, sources, results
        self.down_send, self.down_recv, self.up_send, self.up_recv, self.own_sem = sems
        self.at, self.size = place_of()
        self.waiting = {}
        self.own, self.base, self.got = [], [], []
        scratch = list(scratch)
        for chunk in chunks:
            part = chunk.rows // self.size[chunk.order[0]]
            if chunk.held_here:
                self.own.append(sources[chunk.array])
                self.base.append(chunk.first + self.at[chunk.order[0]] * part)
            else:
                self.own.append(scratch.pop(0))
                self.base.append(0)
            self.got.append([scratch.pop(0) for _ in chunk.order])

    def region(self, i, stages):
        chunk = self.chunks[i]
        first, rows, z = 0, chunk.rows, None
        for k, axis in enumerate(chunk.order[:stages]):
            if axis == "z":
                z = self.at["z"]
            else:
                rows = rows // self.size[axis]
                if k > 0:
                    first = first + self.at[axis] * rows
        return z, first, rows

    def copy_to(self, source, target, send, recv, device):
        copy = pltpu.make_async_remote_copy(
            src_ref=source, dst_ref=target, send_sem=send, recv_sem=recv, device_id=device,
            device_id_type=pl.DeviceIdType.MESH,
        )
        copy.start()
        return copy

    def send_down(self, i, s):
        chunk, axis = self.chunks[i], self.chunks[i].order[s]
        copies = []
        z, first, rows = self.region(i, s)
        part = rows if axis == "z" else rows // self.size[axis]
        for step, (place, device) in enumerate(peers_of(axis, self.at, self.size)):
            if s == 0:
                start = chunk.first + place * part
                source = self.sources[chunk.array].at[:, pl.ds(pl.multiple_of(start, 16), part), :]
            elif axis == "z":
                start = self.base[i] + first
                source = self.own[i].at[pl.ds(place, 1), pl.ds(pl.multiple_of(start, 16), part), :]
            else:
                start = pl.multiple_of(self.base[i] + first + place * part, 16)
                blocks = slice(None) if z is None else pl.ds(z, 1)
                source = self.own[i].at[blocks, pl.ds(start, part), :]
            index = (i, s, step)
            copies.append(
                self.copy_to(source, self.got[i][s].at[step], self.down_send.at[index], self.down_recv.at[index], device)
            )
        if s == 0 and not chunk.held_here:
            start = pl.multiple_of(chunk.first + self.at[axis] * part, 16)
            load = pltpu.make_async_copy(
                self.sources[chunk.array].at[:, pl.ds(start, part), :], self.own[i], self.own_sem.at[i]
            )
            load.start()
            copies.append(load)
        self.waiting[i] = copies

    def add_up(self, i, s):
        chunk, axis = self.chunks[i], self.chunks[i].order[s]
        for copy in self.waiting[i]:
            copy.wait()
        z, first, rows = self.region(i, s + 1)
        blocks = self.got[i][s].shape[1]
        piece = math.gcd(rows, 64)
        own, got = self.own[i], self.got[i][s]

        def one(t, carry):
            block, row = t // (rows // piece), lax.rem(t, rows // piece) * piece
            where = pl.ds(pl.multiple_of(self.base[i] + first + row, 16), piece)
            arrived = pl.ds(pl.multiple_of(row, 16), piece)
            held = block if z is None else z
            total = own[held, where, :].astype(F32)
            for step in range(self.size[axis] - 1):
                total = total + got[step, block, arrived, :].astype(F32)
            own[held, where, :] = total.astype(BF16)
            return carry

        lax.fori_loop(0, blocks * (rows // piece), one, 0)

    def target(self, i, stages):
        chunk = self.chunks[i]
        z, first, rows = self.region(i, stages)
        start = chunk.first + self.at[chunk.order[0]] * (chunk.rows // self.size[chunk.order[0]]) + first
        where = pl.ds(pl.multiple_of(start, 16), rows)
        result = self.results[chunk.result].at[chunk.layer]
        if chunk.kind == "own":
            return result.at[where, :]
        if chunk.kind == "stack":
            return result.at[:, where, :] if z is None else result.at[z, where, :]
        width = self.own[i].shape[2]
        return result.at[where, :] if z is None else result.at[where, pl.ds(pl.multiple_of(z * width, width), width)]

    def send_up(self, i, s):
        chunk, axis = self.chunks[i], self.chunks[i].order[s]
        target = self.target(i, s + 1)
        copies = []
        source = target
        if s == len(chunk.order) - 1:
            z, first, rows = self.region(i, s + 1)
            where = pl.ds(pl.multiple_of(self.base[i] + first, 16), rows)
            source = self.own[i].at[z, where, :]
            keep = pltpu.make_async_copy(source, target, self.own_sem.at[i])
            keep.start()
            copies.append(keep)
        if axis != "z" or chunk.kind != "own":
            for step, (_, device) in enumerate(peers_of(axis, self.at, self.size)):
                index = (i, s, step)
                copies.append(self.copy_to(source, target, self.up_send.at[index], self.up_recv.at[index], device))
        self.waiting[i] = copies

    def stages(self, i):
        return 2 * len(self.chunks[i].order)

    def advance(self, i, stage):
        depth = len(self.chunks[i].order)
        if stage < depth:
            self.add_up(i, stage)
            if stage + 1 < depth:
                self.send_down(i, stage + 1)
            else:
                self.send_up(i, depth - 1)
        else:
            for copy in self.waiting[i]:
                copy.wait()
            if stage + 1 < 2 * depth:
                self.send_up(i, 2 * depth - 2 - stage)


class SmallSum:
    def __init__(self, array, result, got, send, recv):
        self.array, self.result, self.got, self.send, self.recv = array, result, got, send, recv
        self.at, self.size = place_of()

    def start(self, s):
        axis = "cxyz"[s]
        source = self.array if s == 0 else self.result
        self.copies = []
        for step, (_, device) in enumerate(peers_of(axis, self.at, self.size)):
            copy = pltpu.make_async_remote_copy(
                src_ref=source, dst_ref=self.got[s].at[self.at[axis]], send_sem=self.send.at[s, step],
                recv_sem=self.recv.at[s, step], device_id=device, device_id_type=pl.DeviceIdType.MESH,
            )
            copy.start()
            self.copies.append(copy)
        self.got[s][self.at[axis]] = source[...]

    def advance(self, s):
        for copy in self.copies:
            copy.wait()
        total = self.got[s][0]
        for j in range(1, self.size["cxyz"[s]]):
            total = total + self.got[s][j]
        self.result[...] = total
        if s < 3:
            self.start(s + 1)


def sum_scratch(chunks, shapes, size):
    scratch = []
    for chunk in chunks:
        blocks, _, width = shapes[chunk.array]
        scratch += [pltpu.VMEM(shape, BF16) for shape in chunk.shapes(blocks, width, size)]
    most = max(size.values()) - 1
    sems = pltpu.SemaphoreType.DMA((len(chunks), 4, most))
    return scratch, [sems] * 4 + [pltpu.SemaphoreType.DMA((len(chunks),))]


def small_scratch(shape, size):
    most = max(size.values()) - 1
    sems = pltpu.SemaphoreType.DMA((4, most))
    return [pltpu.VMEM((size[axis],) + shape, F32) for axis in "cxyz"] + [sems] * 2


def reduce_kernel(chunks, starts, counts, *refs):
    sources, refs = refs[: counts[0]], refs[counts[0] :]
    small_in, refs = refs[0], refs[1:]
    results, refs = refs[: counts[1]], refs[counts[1] :]
    small_out, refs = refs[0], refs[1:]
    scratch, sems, refs = refs[: counts[2]], refs[counts[2] : counts[2] + 5], refs[counts[2] + 5 :]
    small = SmallSum(small_in, small_out, refs[:4], refs[4], refs[5])
    sums = Sums(chunks, sources, results, scratch, sems)
    greet("cxyz", sums.at, sums.size)
    ahead = AHEAD
    for i, start in enumerate(starts):
        if start < ahead:
            sums.send_down(i, 0)
    small.start(0)
    for t in range(max(start + sums.stages(i) for i, start in enumerate(starts))):
        order = range(len(chunks))
        for i in (reversed(order) if NEWEST else order):
            if 0 <= t - starts[i] < sums.stages(i):
                sums.advance(i, t - starts[i])
        for i, start in enumerate(starts):
            if start == t + ahead:
                sums.send_down(i, 0)
        if t < 4:
            small.advance(t)


AHEAD = 2
NEWEST = False


def pieces(rows, unit):
    units = rows // unit
    if units < 2 or not HALVES:
        return [(0, rows)]
    return [(0, -(-units // 2) * unit), (-(-units // 2) * unit, units // 2 * unit)]


HALVES = False


def sum_plan(n, up_rows, down_rows, own_rows, dp, tail_rows):
    unit = 16 * dp
    chunks, starts = [], []

    def pad(rows):
        return -(-rows // unit) * unit

    def add(pair, rows_pair):
        cuts = [pieces(pad(rows), unit) for rows in rows_pair]
        for k in range(max(len(cut) for cut in cuts)):
            start = starts[-1] + 1 if starts else 0
            for (array, kind, result, layer, order), cut in zip(pair, cuts):
                if k < len(cut):
                    chunks.append(Chunk(array, cut[k][0], cut[k][1], order, kind, result, layer, False))
                    starts.append(start)

    add([(0, "wide", 0, 1, "cxyz"), (1, "stack", 1, 1, "cyxz")], (up_rows, down_rows))
    add([(4, "wide", 0, 0, "cxyz"), (5, "stack", 1, 0, "cyxz")], (up_rows, down_rows))
    add([(2, "own", 2, 1, "cxyz"), (3, "own", 3, 1, "cyxz")], (own_rows, own_rows))
    add([(6, "own", 2, 0, "cxyz"), (7, "own", 3, 0, "cyxz")], (own_rows, own_rows))
    chunks.append(Chunk(8, 0, tail_rows, "cxyz", "stack", 4, 0, False))
    starts.append(0)
    return chunks, starts


def reduce_all(arrays, chunks, starts, result_shapes, small, sizes, collective_id):
    scratch, sems = sum_scratch(chunks, [array.shape for array in arrays], sizes)
    counts = (len(arrays), len(result_shapes), len(scratch))
    anywhere = pl.BlockSpec(memory_space=pl.ANY)
    return pl.pallas_call(
        partial(reduce_kernel, chunks, starts, counts),
        out_shape=[jax.ShapeDtypeStruct(shape, BF16) for shape in result_shapes] + [jax.ShapeDtypeStruct(small.shape, F32)],
        in_specs=[anywhere] * len(arrays) + [vmem()],
        out_specs=[anywhere] * len(result_shapes) + [vmem()],
        scratch_shapes=scratch + sems + small_scratch(small.shape, sizes),
        compiler_params=pltpu.CompilerParams(
            collective_id=collective_id, has_side_effects=True, vmem_limit_bytes=VMEM_LIMIT
        ),
        name="sum_gradients",
    )(*arrays, small)


def gather_kernel(orders, *refs):
    count = len(orders)
    mine, results, sems = refs[:2], refs[2 : 2 + count], refs[2 + count :]
    mine = [mine[i % 2].at[i // 2] for i in range(count)]
    send_sem, recv_sem, own_sem = sems
    at, size = place_of()
    greet("cxyz", at, size)
    waiting = {}

    def region(i, s):
        first, rows = 0, mine[i].shape[0]
        for axis in reversed(orders[i][s:]):
            rows = rows // size[axis]
            first = first + at[axis] * rows
        return pl.ds(pl.multiple_of(first, rows), rows)

    def send(i, s):
        axis = orders[i][s]
        copies = []
        if s == 0:
            where = region(i, 1)
            own = pltpu.make_async_copy(mine[i], results[i].at[at["z"]], own_sem.at[i])
            own.start()
            copies.append(own)
        else:
            where = region(i, s)
        for step, (_, device) in enumerate(peers_of(axis, at, size)):
            for other in range(1 if s == 0 else size["z"] - 1):
                block = at["z"] if s == 0 else lax.rem(at["z"] + 1 + other, size["z"])
                source = mine[i].at[where, :] if s == 0 else results[i].at[block, where, :]
                copy = pltpu.make_async_remote_copy(
                    src_ref=source,
                    dst_ref=results[i].at[block, where, :],
                    send_sem=send_sem.at[i, s, step, other],
                    recv_sem=recv_sem.at[i, s, step, other],
                    device_id=device,
                    device_id_type=pl.DeviceIdType.MESH,
                )
                copy.start()
                copies.append(copy)
        waiting[i] = copies

    for t in range(count // 2 + max(len(order) for order in orders)):
        for i in range(count):
            stage = t - i // 2
            if 0 <= stage <= len(orders[i]):
                if stage > 0:
                    for copy in waiting[i]:
                        copy.wait()
                if stage < len(orders[i]):
                    send(i, stage)


def gather_all(arrays, sizes, collective_id):
    layers, rows, width = arrays[0].shape
    n = sizes["z"]
    orders = []
    for i in range(2 * layers):
        left, axes = rows // 16, ""
        for axis in "cxy" if i % 2 else "cyx":
            if left % sizes[axis] == 0:
                left, axes = left // sizes[axis], axis + axes
        orders.append("z" + axes)
    anywhere = pl.BlockSpec(memory_space=pl.ANY)
    most = max(sizes.values()) - 1
    sems = pltpu.SemaphoreType.DMA((len(orders), 4, most, n - 1))
    return pl.pallas_call(
        partial(gather_kernel, orders),
        out_shape=[jax.ShapeDtypeStruct((n, rows, width), BF16) for _ in orders],
        in_specs=[vmem()] * 2,
        out_specs=[vmem()] * len(orders),
        scratch_shapes=[sems, sems, pltpu.SemaphoreType.DMA((len(orders),))],
        compiler_params=pltpu.CompilerParams(collective_id=collective_id, has_side_effects=True),
        name="gather_experts",
    )(*arrays)


def layer_spec(array, layer):
    block = (None,) + array.shape[1:]
    return pl.BlockSpec(block, lambda *_: (layer,) + (0,) * (array.ndim - 1), pipeline_mode=pl.Buffered(1))


def share(mine, n, scatter, collective_id, name):
    rows = mine.shape[0] // n if scatter else mine.shape[0]
    return pl.pallas_call(
        partial(share_kernel, n, scatter),
        out_shape=jax.ShapeDtypeStruct((n, rows, mine.shape[1]), mine.dtype),
        in_specs=[vmem()],
        out_specs=vmem(),
        scratch_shapes=[pltpu.SemaphoreType.DMA((n - 1,)), pltpu.SemaphoreType.DMA((n - 1,))],
        compiler_params=pltpu.CompilerParams(collective_id=collective_id, has_side_effects=True),
        name=name,
    )(mine)


def call(kernel, args, outs, scratch, name):
    specs, arrays = [], []
    for array, layer in args:
        arrays.append(array)
        if layer == "smem":
            specs.append(pl.BlockSpec(memory_space=pltpu.SMEM))
        elif layer is None:
            specs.append(pl.BlockSpec(array.shape, lambda *_, nd=array.ndim: (0,) * nd, pipeline_mode=pl.Buffered(1)))
        else:
            specs.append(layer_spec(array, layer))
    return pl.pallas_call(
        kernel,
        out_shape=[jax.ShapeDtypeStruct(shape, dtype) for shape, dtype in outs],
        grid=(1,),
        in_specs=specs,
        out_specs=[pl.BlockSpec(shape, lambda *_, nd=len(shape): (0,) * nd, pipeline_mode=pl.Buffered(1)) for shape, _ in outs],
        scratch_shapes=[pltpu.VMEM(shape, dtype) for shape, dtype in scratch],
        compiler_params=pltpu.CompilerParams(vmem_limit_bytes=VMEM_LIMIT),
        name=name,
    )(*arrays)


def body(
    tokens, cotangent, routes, keep, lengths, norm1_gain, norm1_bias, w_kv, w_router, w_query, w_out,
    norm2_gain, norm2_bias, w_up, w_down,
):
    n = lax.axis_size("exp")
    dp = lax.axis_size("dp")
    layers, width, pair = w_kv.shape
    count = tokens.shape[1]
    group = routes.shape[2]
    topk = routes.shape[3]
    experts = w_router.shape[2]
    head = w_query.shape[3]
    local = w_query.shape[1]
    hidden = w_up.shape[2]
    flat = experts * head
    own = local * head
    x0 = tokens[0]
    routes_t = jnp.swapaxes(routes[:, 0], 1, 2)
    router_t = jnp.swapaxes(w_router, 1, 2)
    gain1, bias1, gain2, bias2 = norm1_gain, norm1_bias, norm2_gain, norm2_bias
    queries_t = jnp.swapaxes(w_query, 2, 3).reshape(layers, own, width)
    outs = w_out.reshape(layers, own, width)
    sizes = axis_sizes()
    gathered = [array.reshape(flat, width) for array in gather_all((queries_t, outs), sizes, 2)]
    wq, wo = gathered[0::2], gathered[1::2]

    def rows_of(least):
        return -(-least // (16 * dp)) * 16 * dp

    def weights(l):
        return [(gain1, None), (bias1, None), (w_kv, l), (router_t, l), (wq[l], None), (wo[l], None), (gain2, None), (bias2, None), (w_up, l), (w_down, l)]

    kept_shapes = [
        ((count, experts), F32), ((topk, count, LANES), BF16), ((topk, 8, count), F32),
        ((topk, count, LANES), BF16), ((count, flat), BF16), ((count, width), F32),
    ]
    work = [((group, count), F32), ((topk, count, LANES), jnp.int32), ((count, flat), F32), ((count, flat), F32)]
    sum_shapes = [((count, width), F32), ((group, pair), F32), ((group, pair), F32), ((count, experts), F32)]
    out_shapes = [
        ((n, rows_of(width), hidden // n), BF16), ((n, rows_of(hidden // n), width), BF16),
        ((n, rows_of(own), width), BF16), ((n, rows_of(own), width), BF16),
        ((experts, width), F32), ((group, pair), BF16), ((8, width), F32), ((count, width), F32), ((count, width), F32),
    ]
    normed0, keyval0 = call(
        pre_kernel, [(x0, None), (gain1, None), (bias1, None), (w_kv, 0)],
        [((count, width), BF16), ((count, pair), BF16)], [], "pre",
    )
    keyval0 = share(keyval0, n, False, 0, "gather_keyval").reshape(group, pair)
    *kept0, x1, normed1, keyval1, small0 = call(
        first_kernel,
        weights(0) + [(x0, None), (normed0, None), (keyval0, None), (routes_t, 0), (lengths, "smem"), (keep, None), (gain1, None), (bias1, None), (w_kv, 1)],
        kept_shapes + [((count, width), F32), ((count, width), BF16), ((count, pair), BF16), ((8, width), F32)],
        work, "first_block",
    )
    keyval1 = share(keyval1, n, False, 0, "gather_keyval").reshape(group, pair)
    activations, up1, down1, out1, query1, router1, part1, small1, mid1, ngrad1 = call(
        turn_kernel,
        weights(1) + [(x1, None), (normed1, None), (keyval1, None), (routes_t, 1), (lengths, "smem"), (keep, None), (cotangent[0], None)],
        [((count, width), BF16)] + out_shapes, kept_shapes + sum_shapes + work, "second_block",
    )
    received1 = share(part1, n, True, 1, "scatter_keyval")
    kv1, small1, up0, down0, out0, query0, router0, part0, small0, mid0, ngrad0 = call(
        back_kernel,
        weights(0) + [(x1, None), (normed1, None), (received1, None), (gain1, None), (w_kv, 1), (mid1, None), (ngrad1, None), (small1, None),
         (normed0, None), (routes_t, 0), (lengths, "smem"), (keep, None), (small0, None), (keyval0, None)] + [(v, None) for v in kept0],
        [((pair, width), BF16), ((8, width), F32)] + out_shapes, sum_shapes + work, "first_block_back",
    )
    received0 = share(part0, n, True, 1, "scatter_keyval")
    kv0, small0, input_grad = call(
        end_kernel,
        [(x0, None), (normed0, None), (received0, None), (gain1, None), (w_kv, 0), (mid0, None), (ngrad0, None), (small0, None)],
        [((pair, width), BF16), ((8, width), F32), ((count, width), F32)], [], "end",
    )
    kv_rows = experts + pair
    tail = jnp.concatenate([kv0, router0.astype(BF16), kv1, router1.astype(BF16)])
    tail_rows = rows_of(-(-tail.shape[0] // n))
    tail = jnp.pad(tail, ((0, n * tail_rows - tail.shape[0]), (0, 0))).reshape(n, tail_rows, width)
    chunks, starts = sum_plan(n, width, hidden // n, own, dp, tail_rows)
    arrays = [up1, down1, query1, out1, up0, down0, query0, out0, tail]
    up, down, expert_query, expert_out, tail, small = reduce_all(
        arrays, chunks, starts,
        [(layers,) + up1.shape[1:2] + (hidden,), (layers,) + down1.shape, (layers,) + query1.shape[1:], (layers,) + out1.shape[1:], (1,) + tail.shape],
        jnp.concatenate([small0, small1]), sizes, 3,
    )
    down = down[:, :, : hidden // n].reshape(layers, hidden, width).astype(F32)
    tail = tail.reshape(n * tail_rows, width)[: layers * kv_rows].reshape(layers, kv_rows, width).astype(F32)
    kv = jnp.swapaxes(tail[:, :pair], 1, 2)
    router = jnp.swapaxes(tail[:, pair:], 1, 2)
    norms = small.reshape(layers, -1, width)
    expert_query = jnp.swapaxes(expert_query[:, :own].reshape(layers, local, head, width), 2, 3).astype(F32)
    expert_out = expert_out[:, :own].reshape(layers, local, head, width).astype(F32)
    return (
        activations[None], input_grad[None], norms[:, 0], norms[:, 1], kv, router, expert_query, expert_out,
        norms[:, 2], norms[:, 3], up[:, :width].astype(F32), down, norms[:, 4, :experts],
    )


def solution(mesh):
    return jax.shard_map(
        body,
        mesh=mesh,
        in_specs=(
            P("dp", "exp", None), P("dp", "exp", None), P(None, "dp", None, None), P("dp", None), P("dp", None),
            P(), P(), P(), P(), P(None, "exp", None, None), P(None, "exp", None, None), P(), P(), P(), P(),
        ),
        out_specs=(
            P("dp", "exp", None), P("dp", "exp", None), P(), P(), P(), P(),
            P(None, "exp", None, None), P(None, "exp", None, None), P(), P(), P(), P(), P(),
        ),
        check_vma=False,
    )
```

```python
from functools import partial
import math

import jax
import jax.numpy as jnp
from jax import lax
from jax.experimental import pallas as pl
from jax.experimental.pallas import tpu as pltpu
from jax.sharding import PartitionSpec as P

F32 = jnp.float32
BF16 = jnp.bfloat16
LANES = 128
epsilon = 1e-05
neg_big = -1e30
never = 1 << 30
gelu_c = 0.7978845608028654
gelu_a = 0.044715
VMEM_LIMIT = 56 << 20


def nn(a, b):
    return jnp.dot(a, b, preferred_element_type=F32)


def nt(a, b):
    return lax.dot_general(a, b, (((1,), (1,)), ((), ())), preferred_element_type=F32)


def tn(a, b):
    return lax.dot_general(a, b, (((0,), (0,)), ((), ())), preferred_element_type=F32)


def iota(shape, axis):
    return lax.broadcasted_iota(jnp.int32, shape, axis)


def norm_parts(values):
    center = values - jnp.mean(values, axis=-1, keepdims=True)
    spread = jnp.mean(center * center, axis=-1, keepdims=True)
    scale = lax.rsqrt(spread + epsilon)
    return center * scale, scale


def norm_back(hat, scale, gain, grad):
    scaled = grad * gain
    first = jnp.mean(scaled, axis=-1, keepdims=True)
    second = jnp.mean(scaled * hat, axis=-1, keepdims=True)
    back = scale * (scaled - first - hat * second)
    return back, jnp.sum(grad * hat, axis=0, keepdims=True), jnp.sum(grad, axis=0, keepdims=True)


def gelu_parts(v):
    inner = jnp.tanh(gelu_c * (v + gelu_a * v * v * v))
    half = 0.5 * (1.0 + inner)
    return v * half, half + 0.5 * v * (1.0 - inner * inner) * gelu_c * (1.0 + 3.0 * gelu_a * v * v)


def lane_half(shape):
    return (iota(shape, 1) >= LANES // 2).astype(jnp.int32)


def select_tiles(dense, chosen):
    out = jnp.zeros(chosen.shape, F32)
    for tile in range(dense.shape[1] // LANES):
        out = jnp.where(chosen == 2 * tile, dense[:, tile * LANES : (tile + 1) * LANES], out)
    return out


def place_tiles(dense, chosen, values):
    for tile in range(dense.shape[1] // LANES):
        where = slice(tile * LANES, (tile + 1) * LANES)
        dense[:, where] = jnp.where(chosen == 2 * tile, values, dense[:, where])


def own_columns(ref, count):
    start = lax.axis_index("exp") * count
    return ref[:, pl.ds(pl.multiple_of(start, count), count)]


def spread_routes(routes, spread):
    topk, count, lanes = spread.shape
    own = own_columns(routes, count)
    for k in range(topk):
        spread[k] = jnp.broadcast_to(own[k : k + 1, :], (lanes, count)).T


def fill_mask(lengths, keep, mask):
    group, count = mask.shape
    start = lax.axis_index("exp") * count
    position = start + iota((1, count), 1)
    low = jnp.zeros((1, count), jnp.int32)
    end = 0
    for s in range(lengths.shape[1] - 1):
        end = end + lengths[0, s]
        low = jnp.where(position >= end, end, low)
    kept = jnp.broadcast_to(keep[...], (LANES, group)).T
    kept = jnp.concatenate([kept] * (count // LANES), axis=1)
    key = iota((group, count), 0)
    usable = jnp.where(kept > 0, key, never)
    allowed = ((usable >= low) & (usable <= position)) | (key == position)
    mask[...] = jnp.where(allowed, 0.0, neg_big)


def split_keyval(keyval):
    both = keyval.astype(F32)
    swapped = pltpu.roll(both, LANES // 2, 1)
    first = iota(both.shape, 1) < LANES // 2
    return jnp.where(first, both, swapped), jnp.where(first, swapped, both)


def pre_layer(x, gain1, bias1, w_kv, normed, keyval_own):
    hat, _ = norm_parts(x)
    normed[...] = (hat * gain1 + bias1).astype(BF16)
    keyval_own[...] = nn(normed[...], w_kv).astype(BF16)


def make_gates(normed, w_router, spread):
    logits = nt(normed, w_router)
    experts = logits.shape[1]
    lanes = iota(logits.shape, 1)
    picked = spread[0][:, :experts] == lanes
    for k in range(1, spread.shape[0]):
        picked = picked | (spread[k][:, :experts] == lanes)
    top = jnp.max(jnp.where(picked, logits, neg_big), axis=1, keepdims=True)
    shares = jnp.where(picked, jnp.exp(jnp.minimum(logits - top, 0.0)), 0.0)
    return shares / jnp.sum(shares, axis=1, keepdims=True), picked


def gate_column(gates, spread_k):
    lanes = iota(gates.shape, 1)
    return jnp.sum(
        jnp.where(spread_k[:, : gates.shape[1]] == lanes, gates, 0.0), axis=1, keepdims=True
    )


def layer_forward(x, normed, weights, mask, spread, dense, gated, kept):
    count = normed.shape[0]
    gates, picked = make_gates(normed[...], weights.w_router[...], spread)
    kept.gates[...] = gates
    dense[...] = nt(normed[...], weights.w_query[...]).astype(BF16).astype(F32) * 0.125
    gated[...] = jnp.zeros(gated.shape, F32)
    keys, values = split_keyval(kept.keyval[...])
    keys = keys.astype(BF16)
    values_t = values.T.astype(BF16)

    def slot(k, carry):
        which = spread[k]
        chosen = which - lane_half((count, LANES))
        query = select_tiles(dense, chosen).astype(BF16)
        kept.query[k] = query
        scores = nt(keys, query) + mask[...]
        top = jnp.max(scores, axis=0, keepdims=True)
        shares = jnp.exp(scores - top)
        total = jnp.sum(shares, axis=0, keepdims=True)
        kept.lse[k] = jnp.broadcast_to(top + jnp.log(total), kept.lse.shape[1:])
        shares = (shares * (1.0 / total)).astype(BF16)
        attended = nn(values_t, shares).T.astype(BF16)
        kept.attended[k] = attended
        gate = gate_column(kept.gates[...], which)
        place_tiles(gated, chosen, gate * attended.astype(F32))
        return carry

    lax.fori_loop(0, spread.shape[0], slot, 0)
    kept.gated[...] = gated[...].astype(BF16)
    middle = x + nn(kept.gated[...], weights.w_out[...])
    kept.middle[...] = middle
    hat, _ = norm_parts(middle)
    normed2 = (hat * weights.gain2[...] + weights.bias2[...]).astype(BF16)
    active = gelu_parts(nn(normed2, weights.w_up[...]))[0].astype(BF16)
    return middle + nn(active, weights.w_down[...]), picked


def layer_back(stream_grad, normed, weights, mask, spread, dense, gated, kept, sums, out, between=None):
    between = between or (lambda *place: None)
    count, width = normed.shape
    hidden = weights.w_up.shape[1]
    branch = stream_grad.astype(BF16)
    hat2, scale2 = norm_parts(kept.middle[...])
    normed2 = (hat2 * weights.gain2[...] + weights.bias2[...]).astype(BF16)
    normed2_t = normed2.astype(F32).T.astype(BF16)
    sums.wide[...] = jnp.zeros(sums.wide.shape, F32)

    blocks = out.up.shape[0]
    piece = hidden // blocks
    own = weights.w_query.shape[0] // blocks

    def part(c, carry):
        cols = pl.ds(pl.multiple_of(c * piece, piece), piece)
        active, slope = gelu_parts(nn(normed2, weights.w_up[:, cols]))
        out.down[c, 0:piece, :] = nn(active.T.astype(BF16), branch).astype(BF16)
        upper_grad = (nt(branch, weights.w_down[cols, :]) * slope).astype(BF16)
        out.up[c, 0:width, :] = nn(normed2_t, upper_grad).astype(BF16)
        sums.wide[...] += nt(upper_grad, weights.w_up[:, cols])
        return carry

    lax.fori_loop(0, blocks, part, 0)
    between("hidden")
    back, gain2_grad, bias2_grad = norm_back(hat2, scale2, weights.gain2[...], sums.wide[...])
    out.small[2:3, :] = gain2_grad
    out.small[3:4, :] = bias2_grad
    middle_grad = stream_grad + back
    out.middle_grad[...] = middle_grad
    rounded = middle_grad.astype(BF16)
    gated_t = kept.gated[...].astype(F32).T.astype(BF16)
    for block in range(blocks):
        rows = slice(block * own, (block + 1) * own)
        out.w_out[block, 0:own, :] = nn(gated_t[rows], rounded).astype(BF16)
    dense[...] = nt(rounded, weights.w_out[...])
    gated[...] = jnp.zeros(gated.shape, F32)
    keys, values = split_keyval(kept.keyval[...])
    keys_t = keys.T.astype(BF16)
    keys = keys.astype(BF16)
    values = values.astype(BF16)
    sums.keys[...] = jnp.zeros(sums.keys.shape, F32)
    sums.values[...] = jnp.zeros(sums.values.shape, F32)
    sums.gates[...] = jnp.zeros(sums.gates.shape, F32)
    lanes = iota(sums.gates.shape, 1)

    def slot(k, carry):
        which = spread[k]
        chosen = which - lane_half((count, LANES))
        grad = select_tiles(dense, chosen)
        gate = gate_column(kept.gates[...], which)
        gate_grad = jnp.sum(grad * kept.attended[k].astype(F32), axis=1, keepdims=True)
        sums.gates[...] += jnp.where(which[:, : lanes.shape[1]] == lanes, gate * gate_grad, 0.0)
        att_grad = (gate * grad).astype(BF16)
        query = kept.query[k]
        shares = jnp.exp(nt(keys, query) + mask[...] - kept.lse[k, 0:1, :])
        sums.values[...] += nn(shares.astype(BF16), att_grad)
        share_grad = nt(values, att_grad)
        score_grad = shares * (share_grad - jnp.sum(share_grad * shares, axis=0, keepdims=True))
        score_grad = score_grad.astype(BF16)
        sums.keys[...] += nn(score_grad, query)
        query_grad = nn(keys_t, score_grad).T * 0.125
        place_tiles(gated, chosen, query_grad.astype(BF16).astype(F32))
        between("slot", k)
        return carry

    lax.fori_loop(0, kept.query.shape[0], slot, 0)
    both_keys = sums.keys[...] + pltpu.roll(sums.keys[...], LANES // 2, 1)
    both_values = sums.values[...] + pltpu.roll(sums.values[...], LANES // 2, 1)
    first = iota(both_keys.shape, 1) < LANES // 2
    out.keyval[...] = jnp.where(first, both_keys, both_values).astype(BF16)
    between("keyval")
    weighted = sums.gates[...]
    logit_grad = weighted - kept.gates[...] * jnp.sum(weighted, axis=1, keepdims=True)
    logit_grad = logit_grad.astype(BF16)
    out.router[...] = tn(logit_grad, normed[...])
    query_grad = gated[...].astype(BF16)
    query_grad_t = gated[...].T.astype(BF16)
    for block in range(blocks):
        rows = slice(block * own, (block + 1) * own)
        out.w_query[block, 0:own, :] = nn(query_grad_t[rows], normed[...]).astype(BF16)
    out.normed_grad[...] = nn(query_grad, weights.w_query[...]) + nn(logit_grad, weights.w_router[...])


def add_received(received):
    total = received[0].astype(F32)
    for j in range(1, received.shape[0]):
        total = total + received[j].astype(F32)
    return total.astype(BF16)


def layer_finish(x, normed, total, gain1, w_kv, middle_grad, normed_grad, keyval_out, small):
    keyval_out[...] = nn(total.astype(F32).T.astype(BF16), normed[...]).astype(BF16)
    grad = normed_grad[...] + nt(total, w_kv)
    hat, scale = norm_parts(x)
    back, gain1_grad, bias1_grad = norm_back(hat, scale, gain1, grad)
    small[0:1, :] = gain1_grad
    small[1:2, :] = bias1_grad
    return middle_grad[...] + back


def count_chosen(picked, keep, small):
    count, experts = picked.shape
    kept = jnp.broadcast_to(own_columns(keep, count).astype(F32), (LANES, count)).T[:, :experts]
    small[4:5, 0:experts] = jnp.sum(jnp.where(picked, kept, 0.0), axis=0, keepdims=True)


class Refs:
    def __init__(self, **refs):
        self.__dict__.update(refs)


def named(names, refs):
    return Refs(**dict(zip(names, refs[: len(names)]))), refs[len(names) :]


def weights_of(layer, refs):
    weights, refs = named(WEIGHTS, refs)
    for name in ("gain1", "bias1", "gain2", "bias2"):
        setattr(weights, name, getattr(weights, name).at[pl.ds(layer, 1), :])
    return weights, refs


WEIGHTS = ("gain1", "bias1", "w_kv", "w_router", "w_query", "w_out", "gain2", "bias2", "w_up", "w_down")
KEPT = ("keyval", "gates", "query", "lse", "attended", "gated", "middle")
SUMS = ("wide", "keys", "values", "gates")
OUT = ("up", "down", "w_out", "w_query", "router", "keyval", "small", "middle_grad", "normed_grad")
LATER = ("x", "normed", "received", "gain1", "w_kv", "middle_grad", "normed_grad", "small")


def pre_kernel(x, gain1, bias1, w_kv, normed, keyval_own):
    pre_layer(x[...].astype(F32), gain1[0:1, :], bias1[0:1, :], w_kv[...], normed, keyval_own)


def first_kernel(*refs):
    weights, refs = weights_of(0, refs)
    (x, normed, keyval, routes, lengths, keep, next_gain1, next_bias1, next_w_kv), refs = refs[:9], refs[9:]
    kept, refs = named(KEPT[1:], refs)
    kept.keyval = keyval
    (stream, next_normed, next_keyval, small), refs = refs[:4], refs[4:]
    mask, spread, dense, gated = refs
    fill_mask(lengths, keep, mask)
    spread_routes(routes, spread)
    result, picked = layer_forward(
        x[...].astype(F32), normed, weights, mask, spread, dense, gated, kept
    )
    small[...] = jnp.zeros(small.shape, F32)
    count_chosen(picked, keep, small)
    stream[...] = result
    pre_layer(result, next_gain1[1:2, :], next_bias1[1:2, :], next_w_kv[...], next_normed, next_keyval)


def turn_kernel(*refs):
    weights, refs = weights_of(1, refs)
    (x, normed, keyval, routes, lengths, keep, cotangent), refs = refs[:7], refs[7:]
    (activations,), refs = refs[:1], refs[1:]
    out, refs = named(OUT, refs)
    kept, refs = named(KEPT[1:], refs)
    kept.keyval = keyval
    sums, refs = named(SUMS, refs)
    mask, spread, dense, gated = refs
    fill_mask(lengths, keep, mask)
    spread_routes(routes, spread)
    result, picked = layer_forward(x[...], normed, weights, mask, spread, dense, gated, kept)
    activations[...] = result.astype(BF16)
    count = x.shape[0]
    kept_col = jnp.broadcast_to(own_columns(keep, count).astype(F32), (LANES, count)).T
    kept_col = jnp.concatenate([kept_col] * (x.shape[1] // LANES), axis=1)
    out.small[...] = jnp.zeros(out.small.shape, F32)
    count_chosen(picked, keep, out.small)
    stream_grad = cotangent[...].astype(F32) * kept_col
    layer_back(stream_grad, normed, weights, mask, spread, dense, gated, kept, sums, out)


def back_kernel(*refs):
    weights, refs = weights_of(0, refs)
    later, refs = named(LATER, refs)
    (normed, routes, lengths, keep, small), refs = refs[:5], refs[5:]
    kept, refs = named(KEPT, refs)
    (later_keyval, later_small), refs = refs[:2], refs[2:]
    out, refs = named(OUT, refs)
    sums, refs = named(SUMS, refs)
    mask, spread, dense, gated = refs
    later_small[...] = later.small[...]
    out.small[...] = small[...]
    stream_grad = layer_finish(
        later.x[...], later.normed, add_received(later.received), later.gain1[1:2, :], later.w_kv[...],
        later.middle_grad, later.normed_grad, later_keyval, later_small,
    )
    fill_mask(lengths, keep, mask)
    spread_routes(routes, spread)
    layer_back(stream_grad, normed, weights, mask, spread, dense, gated, kept, sums, out)


def end_kernel(x, normed, received, gain1, w_kv, middle_grad, normed_grad, small_in, keyval_out, small, grad):
    small[...] = small_in[...]
    grad[...] = layer_finish(
        x[...].astype(F32), normed, add_received(received), gain1[0:1, :], w_kv[...], middle_grad, normed_grad,
        keyval_out, small,
    )


def share_kernel(n, scatter, mine, everyones, send_sem, recv_sem):
    me = lax.axis_index("exp")
    rows = everyones.shape[1]
    barrier = pltpu.get_barrier_semaphore()
    others = [lax.rem(me + step, n) for step in range(1, n)]
    for other in others:
        pl.semaphore_signal(
            barrier, inc=1, device_id={"exp": other}, device_id_type=pl.DeviceIdType.MESH
        )

    def part(owner):
        return mine.at[pl.ds(pl.multiple_of(owner * rows, rows), rows)] if scatter else mine

    pl.semaphore_wait(barrier, n - 1)
    copies = []
    for step, other in enumerate(others):
        copy = pltpu.make_async_remote_copy(
            src_ref=part(other),
            dst_ref=everyones.at[me],
            send_sem=send_sem.at[step],
            recv_sem=recv_sem.at[step],
            device_id={"exp": other},
            device_id_type=pl.DeviceIdType.MESH,
        )
        copy.start()
        copies.append(copy)
    everyones[me] = part(me)[...]
    for copy in copies:
        copy.wait()


def vmem():
    return pl.BlockSpec(memory_space=pltpu.VMEM)


def axis_sizes():
    chips = lax.axis_size("dp") // 2
    across = math.isqrt(chips)
    across = across if across * across == chips else chips
    return {"c": 2, "x": across, "y": chips // across, "z": lax.axis_size("exp")}


def place_of():
    size = axis_sizes()
    d = lax.axis_index("dp")
    at = {"c": lax.rem(d, 2), "x": lax.rem(d // 2, size["x"]), "y": d // (2 * size["x"]), "z": lax.axis_index("exp")}
    return at, size


def peers_of(axis, at, size):
    out = []
    for step in range(1, size[axis]):
        where = dict(at)
        where[axis] = lax.rem(at[axis] + step, size[axis])
        out.append((where[axis], {"exp": where["z"], "dp": (where["y"] * size["x"] + where["x"]) * 2 + where["c"]}))
    return out


def greet(axes, at, size):
    barrier = pltpu.get_barrier_semaphore()
    total = 0
    for axis in axes:
        for _, device in peers_of(axis, at, size):
            pl.semaphore_signal(barrier, inc=1, device_id=device, device_id_type=pl.DeviceIdType.MESH)
            total += 1
    pl.semaphore_wait(barrier, total)


class Chunk:
    def __init__(self, array, first, rows, order, kind, result, layer, held_here):
        self.array, self.first, self.rows, self.order = array, first, rows, order
        self.kind, self.result, self.layer, self.held_here = kind, result, layer, held_here

    def shapes(self, blocks, width, size):
        own = (blocks, self.rows // size[self.order[0]], width)
        z, rows = blocks, self.rows
        got = []
        for axis in self.order:
            if axis == "z":
                z = 1
            else:
                rows = rows // size[axis]
            got.append((size[axis] - 1, z, rows, width))
        return ([] if self.held_here else [own]) + got


class Sums:
    def __init__(self, chunks, sources, results, scratch, sems):
        self.chunks, self.sources, self.results = chunks, sources, results
        self.down_send, self.down_recv, self.up_send, self.up_recv, self.own_sem = sems
        self.at, self.size = place_of()
        self.own, self.base, self.got = [], [], []
        scratch = list(scratch)
        for chunk in chunks:
            part = chunk.rows // self.size[chunk.order[0]]
            if chunk.held_here:
                self.own.append(sources[chunk.array])
                self.base.append(chunk.first + self.at[chunk.order[0]] * part)
            else:
                self.own.append(scratch.pop(0))
                self.base.append(0)
            self.got.append([scratch.pop(0) for _ in chunk.order])

    def region(self, i, stages):
        chunk = self.chunks[i]
        first, rows, z = 0, chunk.rows, None
        for k, axis in enumerate(chunk.order[:stages]):
            if axis == "z":
                z = self.at["z"]
            else:
                rows = rows // self.size[axis]
                if k > 0:
                    first = first + self.at[axis] * rows
        return z, first, rows

    def copy_to(self, source, target, send, recv, device):
        copy = pltpu.make_async_remote_copy(
            src_ref=source, dst_ref=target, send_sem=send, recv_sem=recv, device_id=device,
            device_id_type=pl.DeviceIdType.MESH,
        )
        return copy

    def send_down(self, i, s):
        for copy in self.down_copies(i, s):
            copy.start()

    def down_copies(self, i, s):
        chunk, axis = self.chunks[i], self.chunks[i].order[s]
        copies = []
        z, first, rows = self.region(i, s)
        part = rows if axis == "z" else rows // self.size[axis]
        for step, (place, device) in enumerate(peers_of(axis, self.at, self.size)):
            if s == 0:
                start = chunk.first + place * part
                source = self.sources[chunk.array].at[:, pl.ds(pl.multiple_of(start, 16), part), :]
            elif axis == "z":
                start = self.base[i] + first
                source = self.own[i].at[pl.ds(place, 1), pl.ds(pl.multiple_of(start, 16), part), :]
            else:
                start = pl.multiple_of(self.base[i] + first + place * part, 16)
                blocks = slice(None) if z is None else pl.ds(z, 1)
                source = self.own[i].at[blocks, pl.ds(start, part), :]
            index = (i, s, step)
            copies.append(
                self.copy_to(source, self.got[i][s].at[step], self.down_send.at[index], self.down_recv.at[index], device)
            )
        if s == 0 and not chunk.held_here:
            start = pl.multiple_of(chunk.first + self.at[axis] * part, 16)
            load = pltpu.make_async_copy(
                self.sources[chunk.array].at[:, pl.ds(start, part), :], self.own[i], self.own_sem.at[i]
            )
            copies.append(load)
        return copies

    def add_up(self, i, s):
        chunk, axis = self.chunks[i], self.chunks[i].order[s]
        for copy in self.down_copies(i, s):
            copy.wait()
        z, first, rows = self.region(i, s + 1)
        blocks = self.got[i][s].shape[1]
        piece = math.gcd(rows, 64)
        own, got = self.own[i], self.got[i][s]

        def one(t, carry):
            block, row = t // (rows // piece), lax.rem(t, rows // piece) * piece
            where = pl.ds(pl.multiple_of(self.base[i] + first + row, 16), piece)
            arrived = pl.ds(pl.multiple_of(row, 16), piece)
            held = block if z is None else z
            total = own[held, where, :].astype(F32)
            for step in range(self.size[axis] - 1):
                total = total + got[step, block, arrived, :].astype(F32)
            own[held, where, :] = total.astype(BF16)
            return carry

        lax.fori_loop(0, blocks * (rows // piece), one, 0)

    def target(self, i, stages):
        chunk = self.chunks[i]
        z, first, rows = self.region(i, stages)
        start = chunk.first + self.at[chunk.order[0]] * (chunk.rows // self.size[chunk.order[0]]) + first
        where = pl.ds(pl.multiple_of(start, 16), rows)
        result = self.results[chunk.result].at[chunk.layer]
        if chunk.kind == "own":
            return result.at[where, :]
        if chunk.kind == "stack":
            return result.at[:, where, :] if z is None else result.at[z, where, :]
        width = self.own[i].shape[2]
        return result.at[where, :] if z is None else result.at[where, pl.ds(pl.multiple_of(z * width, width), width)]

    def send_up(self, i, s):
        for copy in self.up_copies(i, s):
            copy.start()

    def up_copies(self, i, s):
        chunk, axis = self.chunks[i], self.chunks[i].order[s]
        target = self.target(i, s + 1)
        copies = []
        source = target
        if s == len(chunk.order) - 1:
            z, first, rows = self.region(i, s + 1)
            where = pl.ds(pl.multiple_of(self.base[i] + first, 16), rows)
            source = self.own[i].at[z, where, :]
            copies.append(pltpu.make_async_copy(source, target, self.own_sem.at[i]))
        if axis != "z" or chunk.kind != "own":
            for step, (_, device) in enumerate(peers_of(axis, self.at, self.size)):
                index = (i, s, step)
                copies.append(self.copy_to(source, target, self.up_send.at[index], self.up_recv.at[index], device))
        return copies

    def stages(self, i):
        return 2 * len(self.chunks[i].order)

    def advance(self, i, stage):
        depth = len(self.chunks[i].order)
        if stage < depth:
            self.add_up(i, stage)
            if stage + 1 < depth:
                self.send_down(i, stage + 1)
            else:
                self.send_up(i, depth - 1)
        else:
            for copy in self.up_copies(i, 2 * depth - 1 - stage):
                copy.wait()
            if stage + 1 < 2 * depth:
                self.send_up(i, 2 * depth - 2 - stage)


class SmallSum:
    def __init__(self, array, result, got, send, recv):
        self.array, self.result, self.got, self.send, self.recv = array, result, got, send, recv
        self.at, self.size = place_of()

    def start(self, s):
        axis = "cxyz"[s]
        source = self.array if s == 0 else self.result
        self.copies = []
        for step, (_, device) in enumerate(peers_of(axis, self.at, self.size)):
            copy = pltpu.make_async_remote_copy(
                src_ref=source, dst_ref=self.got[s].at[self.at[axis]], send_sem=self.send.at[s, step],
                recv_sem=self.recv.at[s, step], device_id=device, device_id_type=pl.DeviceIdType.MESH,
            )
            copy.start()
            self.copies.append(copy)
        self.got[s][self.at[axis]] = source[...]

    def advance(self, s):
        for copy in self.copies:
            copy.wait()
        total = self.got[s][0]
        for j in range(1, self.size["cxyz"[s]]):
            total = total + self.got[s][j]
        self.result[...] = total
        if s < 3:
            self.start(s + 1)


def sum_scratch(chunks, shapes, size):
    scratch = []
    for chunk in chunks:
        blocks, _, width = shapes[chunk.array]
        scratch += [pltpu.VMEM(shape, BF16) for shape in chunk.shapes(blocks, width, size)]
    most = max(size.values()) - 1
    sems = pltpu.SemaphoreType.DMA((len(chunks), 4, most))
    return scratch, [sems] * 4 + [pltpu.SemaphoreType.DMA((len(chunks),))]


def small_scratch(shape, size):
    most = max(size.values()) - 1
    sems = pltpu.SemaphoreType.DMA((4, most))
    return [pltpu.VMEM((size[axis],) + shape, F32) for axis in "cxyz"] + [sems] * 2


def reduce_kernel(chunks, starts, counts, *refs):
    sources, refs = refs[: counts[0]], refs[counts[0] :]
    small_in, refs = refs[0], refs[1:]
    results, refs = refs[: counts[1]], refs[counts[1] :]
    small_out, refs = refs[0], refs[1:]
    scratch, sems, refs = refs[: counts[2]], refs[counts[2] : counts[2] + 5], refs[counts[2] + 5 :]
    small = SmallSum(small_in, small_out, refs[:4], refs[4], refs[5])
    sums = Sums(chunks, sources, results, scratch, sems)
    greet("cxyz", sums.at, sums.size)
    ahead = AHEAD
    for i, start in enumerate(starts):
        if start < ahead:
            sums.send_down(i, 0)
    small.start(0)
    for t in range(max(start + sums.stages(i) for i, start in enumerate(starts))):
        order = range(len(chunks))
        for i in (reversed(order) if NEWEST else order):
            if 0 <= t - starts[i] < sums.stages(i):
                sums.advance(i, t - starts[i])
        for i, start in enumerate(starts):
            if start == t + ahead:
                sums.send_down(i, 0)
        if t < 4:
            small.advance(t)


AHEAD = 2
NEWEST = False


def pieces(rows, unit):
    units = rows // unit
    if units < 2 or not HALVES:
        return [(0, rows)]
    return [(0, -(-units // 2) * unit), (-(-units // 2) * unit, units // 2 * unit)]


HALVES = False


def sum_plan(n, up_rows, down_rows, own_rows, dp, tail_rows):
    unit = 16 * dp
    chunks, starts = [], []

    def pad(rows):
        return -(-rows // unit) * unit

    def add(pair, rows_pair):
        cuts = [pieces(pad(rows), unit) for rows in rows_pair]
        for k in range(max(len(cut) for cut in cuts)):
            start = starts[-1] + 1 if starts else 0
            for (array, kind, result, layer, order), cut in zip(pair, cuts):
                if k < len(cut):
                    chunks.append(Chunk(array, cut[k][0], cut[k][1], order, kind, result, layer, False))
                    starts.append(start)

    add([(0, "wide", 0, 1, "cxyz"), (1, "stack", 1, 1, "cyxz")], (up_rows, down_rows))
    add([(4, "wide", 0, 0, "cxyz"), (5, "stack", 1, 0, "cyxz")], (up_rows, down_rows))
    add([(2, "own", 2, 1, "cxyz"), (3, "own", 3, 1, "cyxz")], (own_rows, own_rows))
    add([(6, "own", 2, 0, "cxyz"), (7, "own", 3, 0, "cyxz")], (own_rows, own_rows))
    chunks.append(Chunk(8, 0, tail_rows, "cxyz", "stack", 4, 0, False))
    starts.append(0)
    return chunks, starts


def reduce_all(arrays, chunks, starts, result_shapes, small, sizes, collective_id):
    scratch, sems = sum_scratch(chunks, [array.shape for array in arrays], sizes)
    counts = (len(arrays), len(result_shapes), len(scratch))
    anywhere = pl.BlockSpec(memory_space=pl.ANY)
    return pl.pallas_call(
        partial(reduce_kernel, chunks, starts, counts),
        out_shape=[jax.ShapeDtypeStruct(shape, BF16) for shape in result_shapes] + [jax.ShapeDtypeStruct(small.shape, F32)],
        in_specs=[anywhere] * len(arrays) + [vmem()],
        out_specs=[anywhere] * len(result_shapes) + [vmem()],
        scratch_shapes=scratch + sems + small_scratch(small.shape, sizes),
        compiler_params=pltpu.CompilerParams(
            collective_id=collective_id, has_side_effects=True, vmem_limit_bytes=VMEM_LIMIT
        ),
        name="sum_gradients",
    )(*arrays, small)


def gather_kernel(orders, *refs):
    count = len(orders)
    mine, results, sems = refs[:2], refs[2 : 2 + count], refs[2 + count :]
    mine = [mine[i % 2].at[i // 2] for i in range(count)]
    send_sem, recv_sem, own_sem = sems
    at, size = place_of()
    greet("cxyz", at, size)
    waiting = {}

    def region(i, s):
        first, rows = 0, mine[i].shape[0]
        for axis in reversed(orders[i][s:]):
            rows = rows // size[axis]
            first = first + at[axis] * rows
        return pl.ds(pl.multiple_of(first, rows), rows)

    def send(i, s):
        axis = orders[i][s]
        copies = []
        if s == 0:
            where = region(i, 1)
            own = pltpu.make_async_copy(mine[i], results[i].at[at["z"]], own_sem.at[i])
            own.start()
            copies.append(own)
        else:
            where = region(i, s)
        for step, (_, device) in enumerate(peers_of(axis, at, size)):
            for other in range(1 if s == 0 else size["z"] - 1):
                block = at["z"] if s == 0 else lax.rem(at["z"] + 1 + other, size["z"])
                source = mine[i].at[where, :] if s == 0 else results[i].at[block, where, :]
                copy = pltpu.make_async_remote_copy(
                    src_ref=source,
                    dst_ref=results[i].at[block, where, :],
                    send_sem=send_sem.at[i, s, step, other],
                    recv_sem=recv_sem.at[i, s, step, other],
                    device_id=device,
                    device_id_type=pl.DeviceIdType.MESH,
                )
                copy.start()
                copies.append(copy)
        waiting[i] = copies

    for t in range(count // 2 + max(len(order) for order in orders)):
        for i in range(count):
            stage = t - i // 2
            if 0 <= stage <= len(orders[i]):
                if stage > 0:
                    for copy in waiting[i]:
                        copy.wait()
                if stage < len(orders[i]):
                    send(i, stage)


def gather_all(arrays, sizes, collective_id):
    layers, rows, width = arrays[0].shape
    n = sizes["z"]
    orders = []
    for i in range(2 * layers):
        left, axes = rows // 16, ""
        for axis in "cxy" if i % 2 else "cyx":
            if left % sizes[axis] == 0:
                left, axes = left // sizes[axis], axis + axes
        orders.append("z" + axes)
    anywhere = pl.BlockSpec(memory_space=pl.ANY)
    most = max(sizes.values()) - 1
    sems = pltpu.SemaphoreType.DMA((len(orders), 4, most, n - 1))
    return pl.pallas_call(
        partial(gather_kernel, orders),
        out_shape=[jax.ShapeDtypeStruct((n, rows, width), BF16) for _ in orders],
        in_specs=[vmem()] * 2,
        out_specs=[vmem()] * len(orders),
        scratch_shapes=[sems, sems, pltpu.SemaphoreType.DMA((len(orders),))],
        compiler_params=pltpu.CompilerParams(collective_id=collective_id, has_side_effects=True),
        name="gather_experts",
    )(*arrays)


def layer_spec(array, layer):
    block = (None,) + array.shape[1:]
    return pl.BlockSpec(block, lambda *_: (layer,) + (0,) * (array.ndim - 1), pipeline_mode=pl.Buffered(1))


def share(mine, n, scatter, collective_id, name):
    rows = mine.shape[0] // n if scatter else mine.shape[0]
    return pl.pallas_call(
        partial(share_kernel, n, scatter),
        out_shape=jax.ShapeDtypeStruct((n, rows, mine.shape[1]), mine.dtype),
        in_specs=[vmem()],
        out_specs=vmem(),
        scratch_shapes=[pltpu.SemaphoreType.DMA((n - 1,)), pltpu.SemaphoreType.DMA((n - 1,))],
        compiler_params=pltpu.CompilerParams(collective_id=collective_id, has_side_effects=True),
        name=name,
    )(mine)


class KeyvalSum:
    def __init__(self, mine, got, send, recv):
        self.mine, self.got, self.send, self.recv = mine, got, send, recv
        self.at, self.size = place_of()

    def part(self, place):
        rows = self.got.shape[1]
        return self.mine.at[pl.ds(pl.multiple_of(place * rows, rows), rows), :]

    def start(self):
        self.copies = []
        for step, (place, device) in enumerate(peers_of("z", self.at, self.size)):
            copy = pltpu.make_async_remote_copy(
                src_ref=self.part(place), dst_ref=self.got.at[step], send_sem=self.send.at[step],
                recv_sem=self.recv.at[step], device_id=device, device_id_type=pl.DeviceIdType.MESH,
            )
            copy.start()
            self.copies.append(copy)

    def total(self):
        for copy in self.copies:
            copy.wait()
        total = self.part(self.at["z"])[...].astype(F32)
        for step in range(self.got.shape[0]):
            total = total + self.got[step].astype(F32)
        return total.astype(BF16)


def finish_chunks(n, up_rows, down_rows, own_rows, tail_rows):
    groups = [
        [Chunk(0, 0, up_rows, "cxyz", "wide", 0, 1, False), Chunk(1, 0, down_rows, "cyxz", "stack", 1, 1, False)],
        [Chunk(2, 0, own_rows, "cxyz", "own", 2, 1, False), Chunk(3, 0, own_rows, "cyxz", "own", 3, 1, False)],
        [Chunk(4, 0, up_rows, "cxyz", "wide", 0, 0, True), Chunk(5, 0, down_rows, "cyxz", "stack", 1, 0, True)],
        [Chunk(6, 0, own_rows, "cxyz", "own", 2, 0, True), Chunk(7, 0, own_rows, "cyxz", "own", 3, 0, True)],
        [Chunk(8, 0, tail_rows, "cxyz", "stack", 4, 0, True)],
    ]
    chunks, numbers = [], []
    for group in groups:
        numbers.append(list(range(len(chunks), len(chunks) + len(group))))
        chunks += group
    return chunks, numbers


def finish_kernel(chunks, groups, counts, *refs):
    weights, refs = weights_of(0, refs)
    later, refs = named(LATER[:2] + ("part",) + LATER[3:] + ("router",), refs)
    (x, normed, routes, lengths, keep, small), refs = refs[:6], refs[6:]
    kept, refs = named(KEPT, refs)
    last_grads, refs = refs[:4], refs[4:]
    input_grad, refs = refs[0], refs[1:]
    results, refs = refs[:5], refs[5:]
    small_out, refs = refs[0], refs[1:]
    out, refs = named(OUT, refs)
    sums, refs = named(SUMS, refs)
    (mask, spread, dense, gated), refs = refs[:4], refs[4:]
    (tail, small_in, got1, got0), refs = refs[:4], refs[4:]
    scratch, refs = refs[:counts], refs[counts:]
    small_got, refs = refs[:4], refs[4:]
    sems, small_sems, (send1, recv1, send0, recv0) = refs[:5], refs[5:7], refs[7:]
    sources = list(last_grads) + [out.up, out.down, out.w_query, out.w_out, tail]
    total = Sums(chunks, sources, results, scratch, sems)
    little = SmallSum(small_in, small_out, small_got, *small_sems)
    keyval1 = KeyvalSum(later.part, got1, send1, recv1)
    keyval0 = KeyvalSum(out.keyval, got0, send0, recv0)
    done = [0] * len(groups)

    def begin(group):
        for i in groups[group]:
            total.send_down(i, 0)

    def advance(group):
        if done[group] < total.stages(groups[group][0]):
            for i in groups[group]:
                total.advance(i, done[group])
            done[group] += 1

    greet("cxyz", total.at, total.size)
    keyval1.start()
    begin(0)
    begin(1)
    fill_mask(lengths, keep, mask)
    spread_routes(routes, spread)
    tail[...] = jnp.zeros(tail.shape, BF16)
    rows = small.shape[0]
    experts = weights.w_router.shape[0]
    small_in[0:rows, :] = small[...]
    small_in[rows : 2 * rows, :] = later.small[...]
    small0, small1 = small_in.at[0:rows, :], small_in.at[rows : 2 * rows, :]
    out.small = small0
    tail[3, 0:experts, :] = later.router[...].astype(BF16)
    advance(0)
    stream_grad = layer_finish(
        later.x[...], later.normed, keyval1.total(), later.gain1[1:2, :], later.w_kv[...],
        later.middle_grad, later.normed_grad, tail.at[2, 0 : later.w_kv.shape[1]], small1,
    )

    def between(place, k=None):
        if place == "hidden":
            begin(2)
            advance(0)
            advance(1)
        elif place == "slot":

            @pl.when(k == 2)
            def _():
                advance(0)

            @pl.when(k == 5)
            def _():
                advance(1)
                advance(2)

        elif place == "keyval":
            keyval0.start()
            advance(0)

    layer_back(stream_grad, normed, weights, mask, spread, dense, gated, kept, sums, out, between)
    tail[1, 0:experts, :] = out.router[...].astype(BF16)
    begin(3)
    advance(1)
    input_grad[...] = layer_finish(
        x[...].astype(F32), normed, keyval0.total(), weights.gain1[...], weights.w_kv[...],
        out.middle_grad, out.normed_grad, tail.at[0, 0 : weights.w_kv.shape[1]], small0,
    )
    begin(4)
    little.start(0)
    for step in range(2 * len(chunks[-1].order)):
        for group in range(len(groups)):
            advance(group)
        if step < 4:
            little.advance(step)


def finish_all(args, last_grads, out_shapes, work, result_shapes, sizes):
    specs, arrays = specs_of(args)
    n, up_rows, _ = last_grads[0].shape
    tail_shape = result_shapes[4][1:]
    chunks, groups = finish_chunks(n, up_rows, last_grads[1].shape[1], last_grads[2].shape[1], tail_shape[1])
    shapes = [array.shape for array in last_grads] * 2 + [tail_shape]
    scratch, sems = sum_scratch(chunks, shapes, sizes)
    count, width = out_shapes[-1][0]
    small_shape = (2 * out_shapes[6][0][0], width)
    group, pair = out_shapes[5][0]
    got = pltpu.VMEM((n - 1, group // n, pair), BF16)
    anywhere = pl.BlockSpec(memory_space=pl.ANY)
    return pl.pallas_call(
        partial(finish_kernel, chunks, groups, len(scratch)),
        out_shape=[jax.ShapeDtypeStruct((count, width), F32)]
        + [jax.ShapeDtypeStruct(shape, BF16) for shape in result_shapes]
        + [jax.ShapeDtypeStruct(small_shape, F32)],
        grid=(1,),
        in_specs=specs + [anywhere] * len(last_grads),
        out_specs=[vmem()] + [anywhere] * len(result_shapes) + [vmem()],
        scratch_shapes=[pltpu.VMEM(shape, dtype) for shape, dtype in out_shapes + work]
        + [pltpu.VMEM(tail_shape, BF16), pltpu.VMEM(small_shape, F32), got, got]
        + scratch + small_scratch(small_shape, sizes)[:4] + sems + small_scratch(small_shape, sizes)[4:]
        + [pltpu.SemaphoreType.DMA((n - 1,))] * 4,
        compiler_params=pltpu.CompilerParams(
            collective_id=4, has_side_effects=True, vmem_limit_bytes=62 << 20
        ),
        name="first_block_back_and_sums",
    )(*arrays, *last_grads)


FUSED = True


def specs_of(args):
    specs, arrays = [], []
    for array, layer in args:
        arrays.append(array)
        if layer == "smem":
            specs.append(pl.BlockSpec(memory_space=pltpu.SMEM))
        elif layer is None:
            specs.append(pl.BlockSpec(array.shape, lambda *_, nd=array.ndim: (0,) * nd, pipeline_mode=pl.Buffered(1)))
        else:
            specs.append(layer_spec(array, layer))
    return specs, arrays


def call(kernel, args, outs, scratch, name):
    specs, arrays = specs_of(args)
    return pl.pallas_call(
        kernel,
        out_shape=[jax.ShapeDtypeStruct(shape, dtype) for shape, dtype in outs],
        grid=(1,),
        in_specs=specs,
        out_specs=[pl.BlockSpec(shape, lambda *_, nd=len(shape): (0,) * nd, pipeline_mode=pl.Buffered(1)) for shape, _ in outs],
        scratch_shapes=[pltpu.VMEM(shape, dtype) for shape, dtype in scratch],
        compiler_params=pltpu.CompilerParams(vmem_limit_bytes=VMEM_LIMIT),
        name=name,
    )(*arrays)


def body(
    tokens, cotangent, routes, keep, lengths, norm1_gain, norm1_bias, w_kv, w_router, w_query, w_out,
    norm2_gain, norm2_bias, w_up, w_down,
):
    n = lax.axis_size("exp")
    dp = lax.axis_size("dp")
    layers, width, pair = w_kv.shape
    count = tokens.shape[1]
    group = routes.shape[2]
    topk = routes.shape[3]
    experts = w_router.shape[2]
    head = w_query.shape[3]
    local = w_query.shape[1]
    hidden = w_up.shape[2]
    flat = experts * head
    own = local * head
    x0 = tokens[0]
    routes_t = jnp.swapaxes(routes[:, 0], 1, 2)
    router_t = jnp.swapaxes(w_router, 1, 2)
    gain1, bias1, gain2, bias2 = norm1_gain, norm1_bias, norm2_gain, norm2_bias
    queries_t = jnp.swapaxes(w_query, 2, 3).reshape(layers, own, width)
    outs = w_out.reshape(layers, own, width)
    sizes = axis_sizes()
    gathered = [array.reshape(flat, width) for array in gather_all((queries_t, outs), sizes, 2)]
    wq, wo = gathered[0::2], gathered[1::2]

    def rows_of(least):
        return -(-least // (16 * dp)) * 16 * dp

    def weights(l):
        return [(gain1, None), (bias1, None), (w_kv, l), (router_t, l), (wq[l], None), (wo[l], None), (gain2, None), (bias2, None), (w_up, l), (w_down, l)]

    kept_shapes = [
        ((count, experts), F32), ((topk, count, LANES), BF16), ((topk, 8, count), F32),
        ((topk, count, LANES), BF16), ((count, flat), BF16), ((count, width), F32),
    ]
    work = [((group, count), F32), ((topk, count, LANES), jnp.int32), ((count, flat), F32), ((count, flat), F32)]
    sum_shapes = [((count, width), F32), ((group, pair), F32), ((group, pair), F32), ((count, experts), F32)]
    out_shapes = [
        ((n, rows_of(width), hidden // n), BF16), ((n, rows_of(hidden // n), width), BF16),
        ((n, rows_of(own), width), BF16), ((n, rows_of(own), width), BF16),
        ((experts, width), F32), ((group, pair), BF16), ((8, width), F32), ((count, width), F32), ((count, width), F32),
    ]
    normed0, keyval0 = call(
        pre_kernel, [(x0, None), (gain1, None), (bias1, None), (w_kv, 0)],
        [((count, width), BF16), ((count, pair), BF16)], [], "pre",
    )
    keyval0 = share(keyval0, n, False, 0, "gather_keyval").reshape(group, pair)
    *kept0, x1, normed1, keyval1, small0 = call(
        first_kernel,
        weights(0) + [(x0, None), (normed0, None), (keyval0, None), (routes_t, 0), (lengths, "smem"), (keep, None), (gain1, None), (bias1, None), (w_kv, 1)],
        kept_shapes + [((count, width), F32), ((count, width), BF16), ((count, pair), BF16), ((8, width), F32)],
        work, "first_block",
    )
    keyval1 = share(keyval1, n, False, 0, "gather_keyval").reshape(group, pair)
    activations, up1, down1, out1, query1, router1, part1, small1, mid1, ngrad1 = call(
        turn_kernel,
        weights(1) + [(x1, None), (normed1, None), (keyval1, None), (routes_t, 1), (lengths, "smem"), (keep, None), (cotangent[0], None)],
        [((count, width), BF16)] + out_shapes, kept_shapes + sum_shapes + work, "second_block",
    )
    tail_rows = rows_of(pair)
    result_shapes = [
        (layers,) + up1.shape[1:2] + (hidden,), (layers,) + down1.shape, (layers,) + query1.shape[1:],
        (layers,) + out1.shape[1:], (1, n, tail_rows, width),
    ]
    fused = FUSED and n * dp == 32
    if fused:
        last = [(x1, None), (normed1, None), (part1, None), (gain1, None), (w_kv, 1), (mid1, None), (ngrad1, None), (small1, None), (router1, None)]
        first = [(x0, None), (normed0, None), (routes_t, 0), (lengths, "smem"), (keep, None), (small0, None), (keyval0, None)]
        input_grad, up, down, expert_query, expert_out, tail, small = finish_all(
            weights(0) + last + first + [(v, None) for v in kept0], [up1, down1, query1, out1],
            out_shapes, sum_shapes + work, result_shapes, sizes,
        )
    else:
        received1 = share(part1, n, True, 1, "scatter_keyval")
        kv1, small1, up0, down0, out0, query0, router0, part0, small0, mid0, ngrad0 = call(
            back_kernel,
            weights(0) + [(x1, None), (normed1, None), (received1, None), (gain1, None), (w_kv, 1), (mid1, None), (ngrad1, None), (small1, None),
             (normed0, None), (routes_t, 0), (lengths, "smem"), (keep, None), (small0, None), (keyval0, None)] + [(v, None) for v in kept0],
            [((pair, width), BF16), ((8, width), F32)] + out_shapes, sum_shapes + work, "first_block_back",
        )
        received0 = share(part0, n, True, 1, "scatter_keyval")
        kv0, small0, input_grad = call(
            end_kernel,
            [(x0, None), (normed0, None), (received0, None), (gain1, None), (w_kv, 0), (mid0, None), (ngrad0, None), (small0, None)],
            [((pair, width), BF16), ((8, width), F32), ((count, width), F32)], [], "end",
        )
        tail = jnp.zeros((n, tail_rows, width), BF16)
        for block, rows in enumerate((kv0, router0, kv1, router1)):
            tail = tail.at[block, : rows.shape[0]].set(rows.astype(BF16))
        chunks, starts = sum_plan(n, width, hidden // n, own, dp, tail_rows)
        arrays = [up1, down1, query1, out1, up0, down0, query0, out0, tail]
        up, down, expert_query, expert_out, tail, small = reduce_all(
            arrays, chunks, starts,
            result_shapes,
            jnp.concatenate([small0, small1]), sizes, 3,
        )
    down = down[:, :, : hidden // n].reshape(layers, hidden, width).astype(F32)
    kv = jnp.swapaxes(tail[0, 0:4:2, :pair].astype(F32), 1, 2)
    router = jnp.swapaxes(tail[0, 1:4:2, :experts].astype(F32), 1, 2)
    norms = small.reshape(layers, -1, width)
    expert_query = jnp.swapaxes(expert_query[:, :own].reshape(layers, local, head, width), 2, 3).astype(F32)
    expert_out = expert_out[:, :own].reshape(layers, local, head, width).astype(F32)
    return (
        activations[None], input_grad[None], norms[:, 0], norms[:, 1], kv, router, expert_query, expert_out,
        norms[:, 2], norms[:, 3], up[:, :width].astype(F32), down, norms[:, 4, :experts],
    )


def solution(mesh):
    return jax.shard_map(
        body,
        mesh=mesh,
        in_specs=(
            P("dp", "exp", None), P("dp", "exp", None), P(None, "dp", None, None), P("dp", None), P("dp", None),
            P(), P(), P(), P(), P(None, "exp", None, None), P(None, "exp", None, None), P(), P(), P(), P(),
        ),
        out_specs=(
            P("dp", "exp", None), P("dp", "exp", None), P(), P(), P(), P(),
            P(None, "exp", None, None), P(None, "exp", None, None), P(), P(), P(), P(), P(),
        ),
        check_vma=False,
    )
```

```python
from functools import partial
import math

import jax
import jax.numpy as jnp
from jax import lax
from jax.experimental import pallas as pl
from jax.experimental.pallas import tpu as pltpu
from jax.sharding import PartitionSpec as P

F32 = jnp.float32
BF16 = jnp.bfloat16
LANES = 128
epsilon = 1e-05
neg_big = -1e30
never = 1 << 30
gelu_c = 0.7978845608028654
gelu_a = 0.044715
VMEM_LIMIT = 56 << 20


def nn(a, b):
    return jnp.dot(a, b, preferred_element_type=F32)


def nt(a, b):
    return lax.dot_general(a, b, (((1,), (1,)), ((), ())), preferred_element_type=F32)


def tn(a, b):
    return lax.dot_general(a, b, (((0,), (0,)), ((), ())), preferred_element_type=F32)


def iota(shape, axis):
    return lax.broadcasted_iota(jnp.int32, shape, axis)


def norm_parts(values):
    center = values - jnp.mean(values, axis=-1, keepdims=True)
    spread = jnp.mean(center * center, axis=-1, keepdims=True)
    scale = lax.rsqrt(spread + epsilon)
    return center * scale, scale


def norm_back(hat, scale, gain, grad):
    scaled = grad * gain
    first = jnp.mean(scaled, axis=-1, keepdims=True)
    second = jnp.mean(scaled * hat, axis=-1, keepdims=True)
    back = scale * (scaled - first - hat * second)
    return back, jnp.sum(grad * hat, axis=0, keepdims=True), jnp.sum(grad, axis=0, keepdims=True)


def gelu_parts(v):
    inner = jnp.tanh(gelu_c * (v + gelu_a * v * v * v))
    half = 0.5 * (1.0 + inner)
    return v * half, half + 0.5 * v * (1.0 - inner * inner) * gelu_c * (1.0 + 3.0 * gelu_a * v * v)


def lane_half(shape):
    return (iota(shape, 1) >= LANES // 2).astype(jnp.int32)


def select_tiles(dense, chosen):
    out = jnp.zeros(chosen.shape, F32)
    for tile in range(dense.shape[1] // LANES):
        out = jnp.where(chosen == 2 * tile, dense[:, tile * LANES : (tile + 1) * LANES], out)
    return out


def place_tiles(dense, chosen, values):
    for tile in range(dense.shape[1] // LANES):
        where = slice(tile * LANES, (tile + 1) * LANES)
        dense[:, where] = jnp.where(chosen == 2 * tile, values, dense[:, where])


def own_columns(ref, count):
    start = lax.axis_index("exp") * count
    return ref[:, pl.ds(pl.multiple_of(start, count), count)]


def spread_routes(routes, spread):
    topk, count, lanes = spread.shape
    own = own_columns(routes, count)
    for k in range(topk):
        spread[k] = jnp.broadcast_to(own[k : k + 1, :], (lanes, count)).T


def fill_mask(lengths, keep, mask):
    group, count = mask.shape
    start = lax.axis_index("exp") * count
    position = start + iota((1, count), 1)
    low = jnp.zeros((1, count), jnp.int32)
    end = 0
    for s in range(lengths.shape[1] - 1):
        end = end + lengths[0, s]
        low = jnp.where(position >= end, end, low)
    kept = jnp.broadcast_to(keep[...], (LANES, group)).T
    kept = jnp.concatenate([kept] * (count // LANES), axis=1)
    key = iota((group, count), 0)
    usable = jnp.where(kept > 0, key, never)
    allowed = ((usable >= low) & (usable <= position)) | (key == position)
    mask[...] = jnp.where(allowed, 0.0, neg_big)


def split_keyval(keyval):
    both = keyval.astype(F32)
    swapped = pltpu.roll(both, LANES // 2, 1)
    first = iota(both.shape, 1) < LANES // 2
    return jnp.where(first, both, swapped), jnp.where(first, swapped, both)


def pre_layer(x, gain1, bias1, w_kv, normed, keyval_own):
    hat, _ = norm_parts(x)
    normed[...] = (hat * gain1 + bias1).astype(BF16)
    keyval_own[...] = nn(normed[...], w_kv).astype(BF16)


def make_gates(normed, w_router, spread):
    logits = nt(normed, w_router)
    experts = logits.shape[1]
    lanes = iota(logits.shape, 1)
    picked = spread[0][:, :experts] == lanes
    for k in range(1, spread.shape[0]):
        picked = picked | (spread[k][:, :experts] == lanes)
    top = jnp.max(jnp.where(picked, logits, neg_big), axis=1, keepdims=True)
    shares = jnp.where(picked, jnp.exp(jnp.minimum(logits - top, 0.0)), 0.0)
    return shares / jnp.sum(shares, axis=1, keepdims=True), picked


def gate_column(gates, spread_k):
    lanes = iota(gates.shape, 1)
    return jnp.sum(
        jnp.where(spread_k[:, : gates.shape[1]] == lanes, gates, 0.0), axis=1, keepdims=True
    )


def layer_forward(x, normed, weights, mask, spread, dense, gated, kept, between=None):
    between = between or (lambda *place: None)
    count = normed.shape[0]
    gates, picked = make_gates(normed[...], weights.w_router[...], spread)
    kept.gates[...] = gates
    dense[...] = nt(normed[...], weights.w_query[...]).astype(BF16).astype(F32) * 0.125
    gated[...] = jnp.zeros(gated.shape, F32)
    between("queries")
    keys, values = split_keyval(kept.keyval[...])
    keys = keys.astype(BF16)
    values_t = values.T.astype(BF16)

    def slot(k, carry):
        which = spread[k]
        chosen = which - lane_half((count, LANES))
        query = select_tiles(dense, chosen).astype(BF16)
        kept.query[k] = query
        scores = nt(keys, query) + mask[...]
        top = jnp.max(scores, axis=0, keepdims=True)
        shares = jnp.exp(scores - top)
        total = jnp.sum(shares, axis=0, keepdims=True)
        kept.lse[k] = jnp.broadcast_to(top + jnp.log(total), kept.lse.shape[1:])
        shares = (shares * (1.0 / total)).astype(BF16)
        attended = nn(values_t, shares).T.astype(BF16)
        kept.attended[k] = attended
        gate = gate_column(kept.gates[...], which)
        place_tiles(gated, chosen, gate * attended.astype(F32))
        between("slot", k)
        return carry

    lax.fori_loop(0, spread.shape[0], slot, 0)
    kept.gated[...] = gated[...].astype(BF16)
    between("attended")
    middle = x + nn(kept.gated[...], weights.w_out[...])
    kept.middle[...] = middle
    between("middle")
    hat, _ = norm_parts(middle)
    normed2 = (hat * weights.gain2[...] + weights.bias2[...]).astype(BF16)
    active = gelu_parts(nn(normed2, weights.w_up[...]))[0].astype(BF16)
    return middle + nn(active, weights.w_down[...]), picked


def layer_back(stream_grad, normed, weights, mask, spread, dense, gated, kept, sums, out, between=None):
    between = between or (lambda *place: None)
    count, width = normed.shape
    hidden = weights.w_up.shape[1]
    branch = stream_grad.astype(BF16)
    hat2, scale2 = norm_parts(kept.middle[...])
    normed2 = (hat2 * weights.gain2[...] + weights.bias2[...]).astype(BF16)
    normed2_t = normed2.astype(F32).T.astype(BF16)
    sums.wide[...] = jnp.zeros(sums.wide.shape, F32)

    blocks = out.up.shape[0]
    piece = hidden // blocks
    own = weights.w_query.shape[0] // blocks

    def part(c, carry):
        cols = pl.ds(pl.multiple_of(c * piece, piece), piece)
        active, slope = gelu_parts(nn(normed2, weights.w_up[:, cols]))
        out.down[c, 0:piece, :] = nn(active.T.astype(BF16), branch).astype(BF16)
        upper_grad = (nt(branch, weights.w_down[cols, :]) * slope).astype(BF16)
        out.up[c, 0:width, :] = nn(normed2_t, upper_grad).astype(BF16)
        sums.wide[...] += nt(upper_grad, weights.w_up[:, cols])
        return carry

    lax.fori_loop(0, blocks, part, 0)
    between("hidden")
    back, gain2_grad, bias2_grad = norm_back(hat2, scale2, weights.gain2[...], sums.wide[...])
    out.small[2:3, :] = gain2_grad
    out.small[3:4, :] = bias2_grad
    middle_grad = stream_grad + back
    out.middle_grad[...] = middle_grad
    rounded = middle_grad.astype(BF16)
    between("out")
    gated_t = kept.gated[...].astype(F32).T.astype(BF16)
    for block in range(blocks):
        rows = slice(block * own, (block + 1) * own)
        out.w_out[block, 0:own, :] = nn(gated_t[rows], rounded).astype(BF16)
    dense[...] = nt(rounded, weights.w_out[...])
    gated[...] = jnp.zeros(gated.shape, F32)
    keys, values = split_keyval(kept.keyval[...])
    keys_t = keys.T.astype(BF16)
    keys = keys.astype(BF16)
    values = values.astype(BF16)
    sums.keys[...] = jnp.zeros(sums.keys.shape, F32)
    sums.values[...] = jnp.zeros(sums.values.shape, F32)
    sums.gates[...] = jnp.zeros(sums.gates.shape, F32)
    lanes = iota(sums.gates.shape, 1)

    def slot(k, carry):
        which = spread[k]
        chosen = which - lane_half((count, LANES))
        grad = select_tiles(dense, chosen)
        gate = gate_column(kept.gates[...], which)
        gate_grad = jnp.sum(grad * kept.attended[k].astype(F32), axis=1, keepdims=True)
        sums.gates[...] += jnp.where(which[:, : lanes.shape[1]] == lanes, gate * gate_grad, 0.0)
        att_grad = (gate * grad).astype(BF16)
        query = kept.query[k]
        shares = jnp.exp(nt(keys, query) + mask[...] - kept.lse[k, 0:1, :])
        sums.values[...] += nn(shares.astype(BF16), att_grad)
        share_grad = nt(values, att_grad)
        score_grad = shares * (share_grad - jnp.sum(share_grad * shares, axis=0, keepdims=True))
        score_grad = score_grad.astype(BF16)
        sums.keys[...] += nn(score_grad, query)
        query_grad = nn(keys_t, score_grad).T * 0.125
        place_tiles(gated, chosen, query_grad.astype(BF16).astype(F32))
        between("slot", k)
        return carry

    lax.fori_loop(0, kept.query.shape[0], slot, 0)
    both_keys = sums.keys[...] + pltpu.roll(sums.keys[...], LANES // 2, 1)
    both_values = sums.values[...] + pltpu.roll(sums.values[...], LANES // 2, 1)
    first = iota(both_keys.shape, 1) < LANES // 2
    out.keyval[...] = jnp.where(first, both_keys, both_values).astype(BF16)
    between("keyval")
    weighted = sums.gates[...]
    logit_grad = weighted - kept.gates[...] * jnp.sum(weighted, axis=1, keepdims=True)
    logit_grad = logit_grad.astype(BF16)
    out.router[...] = tn(logit_grad, normed[...])
    query_grad = gated[...].astype(BF16)
    query_grad_t = gated[...].T.astype(BF16)
    for block in range(blocks):
        rows = slice(block * own, (block + 1) * own)
        out.w_query[block, 0:own, :] = nn(query_grad_t[rows], normed[...]).astype(BF16)
    out.normed_grad[...] = nn(query_grad, weights.w_query[...]) + nn(logit_grad, weights.w_router[...])


def add_received(received):
    total = received[0].astype(F32)
    for j in range(1, received.shape[0]):
        total = total + received[j].astype(F32)
    return total.astype(BF16)


def layer_finish(x, normed, total, gain1, w_kv, middle_grad, normed_grad, keyval_out, small):
    keyval_out[...] = nn(total.astype(F32).T.astype(BF16), normed[...]).astype(BF16)
    grad = normed_grad[...] + nt(total, w_kv)
    hat, scale = norm_parts(x)
    back, gain1_grad, bias1_grad = norm_back(hat, scale, gain1, grad)
    small[0:1, :] = gain1_grad
    small[1:2, :] = bias1_grad
    return middle_grad[...] + back


def count_chosen(picked, keep, small):
    count, experts = picked.shape
    kept = jnp.broadcast_to(own_columns(keep, count).astype(F32), (LANES, count)).T[:, :experts]
    small[4:5, 0:experts] = jnp.sum(jnp.where(picked, kept, 0.0), axis=0, keepdims=True)


class Refs:
    def __init__(self, **refs):
        self.__dict__.update(refs)


def named(names, refs):
    return Refs(**dict(zip(names, refs[: len(names)]))), refs[len(names) :]


def weights_of(layer, refs):
    weights, refs = named(WEIGHTS, refs)
    for name in ("gain1", "bias1", "gain2", "bias2"):
        setattr(weights, name, getattr(weights, name).at[pl.ds(layer, 1), :])
    return weights, refs


WEIGHTS = ("gain1", "bias1", "w_kv", "w_router", "w_query", "w_out", "gain2", "bias2", "w_up", "w_down")
KEPT = ("keyval", "gates", "query", "lse", "attended", "gated", "middle")
SUMS = ("wide", "keys", "values", "gates")
OUT = ("up", "down", "w_out", "w_query", "router", "keyval", "small", "middle_grad", "normed_grad")
LATER = ("x", "normed", "received", "gain1", "w_kv", "middle_grad", "normed_grad", "small")


def pre_kernel(x, gain1, bias1, w_kv, normed, keyval_own):
    pre_layer(x[...].astype(F32), gain1[0:1, :], bias1[0:1, :], w_kv[...], normed, keyval_own)


def first_kernel(*refs):
    weights, refs = weights_of(0, refs)
    (x, normed, keyval, routes, lengths, keep, next_gain1, next_bias1, next_w_kv), refs = refs[:9], refs[9:]
    kept, refs = named(KEPT[1:], refs)
    kept.keyval = keyval
    (stream, next_normed, next_keyval, small), refs = refs[:4], refs[4:]
    mask, spread, dense, gated = refs
    fill_mask(lengths, keep, mask)
    spread_routes(routes, spread)
    result, picked = layer_forward(
        x[...].astype(F32), normed, weights, mask, spread, dense, gated, kept
    )
    small[...] = jnp.zeros(small.shape, F32)
    count_chosen(picked, keep, small)
    stream[...] = result
    pre_layer(result, next_gain1[1:2, :], next_bias1[1:2, :], next_w_kv[...], next_normed, next_keyval)


def turn_kernel(*refs):
    weights, refs = weights_of(1, refs)
    (x, normed, keyval, routes, lengths, keep, cotangent), refs = refs[:7], refs[7:]
    (activations,), refs = refs[:1], refs[1:]
    out, refs = named(OUT, refs)
    kept, refs = named(KEPT[1:], refs)
    kept.keyval = keyval
    sums, refs = named(SUMS, refs)
    mask, spread, dense, gated = refs
    fill_mask(lengths, keep, mask)
    spread_routes(routes, spread)
    result, picked = layer_forward(x[...], normed, weights, mask, spread, dense, gated, kept)
    activations[...] = result.astype(BF16)
    count = x.shape[0]
    kept_col = jnp.broadcast_to(own_columns(keep, count).astype(F32), (LANES, count)).T
    kept_col = jnp.concatenate([kept_col] * (x.shape[1] // LANES), axis=1)
    out.small[...] = jnp.zeros(out.small.shape, F32)
    count_chosen(picked, keep, out.small)
    stream_grad = cotangent[...].astype(F32) * kept_col
    layer_back(stream_grad, normed, weights, mask, spread, dense, gated, kept, sums, out)


def back_kernel(*refs):
    weights, refs = weights_of(0, refs)
    later, refs = named(LATER, refs)
    (normed, routes, lengths, keep, small), refs = refs[:5], refs[5:]
    kept, refs = named(KEPT, refs)
    (later_keyval, later_small), refs = refs[:2], refs[2:]
    out, refs = named(OUT, refs)
    sums, refs = named(SUMS, refs)
    mask, spread, dense, gated = refs
    later_small[...] = later.small[...]
    out.small[...] = small[...]
    stream_grad = layer_finish(
        later.x[...], later.normed, add_received(later.received), later.gain1[1:2, :], later.w_kv[...],
        later.middle_grad, later.normed_grad, later_keyval, later_small,
    )
    fill_mask(lengths, keep, mask)
    spread_routes(routes, spread)
    layer_back(stream_grad, normed, weights, mask, spread, dense, gated, kept, sums, out)


def end_kernel(x, normed, received, gain1, w_kv, middle_grad, normed_grad, small_in, keyval_out, small, grad):
    small[...] = small_in[...]
    grad[...] = layer_finish(
        x[...].astype(F32), normed, add_received(received), gain1[0:1, :], w_kv[...], middle_grad, normed_grad,
        keyval_out, small,
    )


def share_kernel(n, scatter, mine, everyones, send_sem, recv_sem):
    me = lax.axis_index("exp")
    rows = everyones.shape[1]
    barrier = pltpu.get_barrier_semaphore()
    others = [lax.rem(me + step, n) for step in range(1, n)]
    for other in others:
        pl.semaphore_signal(
            barrier, inc=1, device_id={"exp": other}, device_id_type=pl.DeviceIdType.MESH
        )

    def part(owner):
        return mine.at[pl.ds(pl.multiple_of(owner * rows, rows), rows)] if scatter else mine

    pl.semaphore_wait(barrier, n - 1)
    copies = []
    for step, other in enumerate(others):
        copy = pltpu.make_async_remote_copy(
            src_ref=part(other),
            dst_ref=everyones.at[me],
            send_sem=send_sem.at[step],
            recv_sem=recv_sem.at[step],
            device_id={"exp": other},
            device_id_type=pl.DeviceIdType.MESH,
        )
        copy.start()
        copies.append(copy)
    everyones[me] = part(me)[...]
    for copy in copies:
        copy.wait()


def vmem():
    return pl.BlockSpec(memory_space=pltpu.VMEM)


def axis_sizes():
    chips = lax.axis_size("dp") // 2
    across = math.isqrt(chips)
    across = across if across * across == chips else chips
    return {"c": 2, "x": across, "y": chips // across, "z": lax.axis_size("exp")}


def place_of():
    size = axis_sizes()
    d = lax.axis_index("dp")
    at = {"c": lax.rem(d, 2), "x": lax.rem(d // 2, size["x"]), "y": d // (2 * size["x"]), "z": lax.axis_index("exp")}
    return at, size


def peers_of(axis, at, size):
    out = []
    for step in range(1, size[axis]):
        where = dict(at)
        where[axis] = lax.rem(at[axis] + step, size[axis])
        out.append((where[axis], {"exp": where["z"], "dp": (where["y"] * size["x"] + where["x"]) * 2 + where["c"]}))
    return out


def greet(axes, at, size):
    barrier = pltpu.get_barrier_semaphore()
    total = 0
    for axis in axes:
        for _, device in peers_of(axis, at, size):
            pl.semaphore_signal(barrier, inc=1, device_id=device, device_id_type=pl.DeviceIdType.MESH)
            total += 1
    pl.semaphore_wait(barrier, total)


class Chunk:
    def __init__(self, array, first, rows, order, kind, result, layer, held_here):
        self.array, self.first, self.rows, self.order = array, first, rows, order
        self.kind, self.result, self.layer, self.held_here = kind, result, layer, held_here

    def shapes(self, blocks, width, size):
        own = (blocks, self.rows // size[self.order[0]], width)
        z, rows = blocks, self.rows
        got = []
        for axis in self.order:
            if axis == "z":
                z = 1
            else:
                rows = rows // size[axis]
            got.append((size[axis] - 1, z, rows, width))
        return ([] if self.held_here else [own]) + got


class Sums:
    def __init__(self, chunks, sources, results, scratch, sems):
        self.chunks, self.sources, self.results = chunks, sources, results
        self.down_send, self.down_recv, self.up_send, self.up_recv, self.own_sem = sems
        self.at, self.size = place_of()
        self.own, self.base, self.got = [], [], []
        scratch = list(scratch)
        for chunk in chunks:
            part = chunk.rows // self.size[chunk.order[0]]
            if chunk.held_here:
                self.own.append(sources[chunk.array])
                self.base.append(chunk.first + self.at[chunk.order[0]] * part)
            else:
                self.own.append(scratch.pop(0))
                self.base.append(0)
            self.got.append([scratch.pop(0) for _ in chunk.order])

    def region(self, i, stages):
        chunk = self.chunks[i]
        first, rows, z = 0, chunk.rows, None
        for k, axis in enumerate(chunk.order[:stages]):
            if axis == "z":
                z = self.at["z"]
            else:
                rows = rows // self.size[axis]
                if k > 0:
                    first = first + self.at[axis] * rows
        return z, first, rows

    def copy_to(self, source, target, send, recv, device):
        copy = pltpu.make_async_remote_copy(
            src_ref=source, dst_ref=target, send_sem=send, recv_sem=recv, device_id=device,
            device_id_type=pl.DeviceIdType.MESH,
        )
        return copy

    def send_down(self, i, s):
        for copy in self.down_copies(i, s):
            copy.start()

    def down_copies(self, i, s):
        chunk, axis = self.chunks[i], self.chunks[i].order[s]
        copies = []
        z, first, rows = self.region(i, s)
        part = rows if axis == "z" else rows // self.size[axis]
        for step, (place, device) in enumerate(peers_of(axis, self.at, self.size)):
            if s == 0:
                start = chunk.first + place * part
                source = self.sources[chunk.array].at[:, pl.ds(pl.multiple_of(start, 16), part), :]
            elif axis == "z":
                start = self.base[i] + first
                source = self.own[i].at[pl.ds(place, 1), pl.ds(pl.multiple_of(start, 16), part), :]
            else:
                start = pl.multiple_of(self.base[i] + first + place * part, 16)
                blocks = slice(None) if z is None else pl.ds(z, 1)
                source = self.own[i].at[blocks, pl.ds(start, part), :]
            index = (i, s, step)
            copies.append(
                self.copy_to(source, self.got[i][s].at[step], self.down_send.at[index], self.down_recv.at[index], device)
            )
        if s == 0 and not chunk.held_here:
            start = pl.multiple_of(chunk.first + self.at[axis] * part, 16)
            load = pltpu.make_async_copy(
                self.sources[chunk.array].at[:, pl.ds(start, part), :], self.own[i], self.own_sem.at[i]
            )
            copies.append(load)
        return copies

    def add_up(self, i, s):
        chunk, axis = self.chunks[i], self.chunks[i].order[s]
        for copy in self.down_copies(i, s):
            copy.wait()
        z, first, rows = self.region(i, s + 1)
        blocks = self.got[i][s].shape[1]
        piece = math.gcd(rows, 64)
        own, got = self.own[i], self.got[i][s]

        def one(t, carry):
            block, row = t // (rows // piece), lax.rem(t, rows // piece) * piece
            where = pl.ds(pl.multiple_of(self.base[i] + first + row, 16), piece)
            arrived = pl.ds(pl.multiple_of(row, 16), piece)
            held = block if z is None else z
            total = own[held, where, :].astype(F32)
            for step in range(self.size[axis] - 1):
                total = total + got[step, block, arrived, :].astype(F32)
            own[held, where, :] = total.astype(BF16)
            return carry

        lax.fori_loop(0, blocks * (rows // piece), one, 0)

    def target(self, i, stages):
        chunk = self.chunks[i]
        z, first, rows = self.region(i, stages)
        start = chunk.first + self.at[chunk.order[0]] * (chunk.rows // self.size[chunk.order[0]]) + first
        where = pl.ds(pl.multiple_of(start, 16), rows)
        result = self.results[chunk.result].at[chunk.layer]
        if chunk.kind == "own":
            return result.at[where, :]
        if chunk.kind == "stack":
            return result.at[:, where, :] if z is None else result.at[z, where, :]
        width = self.own[i].shape[2]
        return result.at[where, :] if z is None else result.at[where, pl.ds(pl.multiple_of(z * width, width), width)]

    def send_up(self, i, s):
        for copy in self.up_copies(i, s):
            copy.start()

    def up_copies(self, i, s):
        chunk, axis = self.chunks[i], self.chunks[i].order[s]
        target = self.target(i, s + 1)
        copies = []
        source = target
        if s == len(chunk.order) - 1:
            z, first, rows = self.region(i, s + 1)
            where = pl.ds(pl.multiple_of(self.base[i] + first, 16), rows)
            source = self.own[i].at[z, where, :]
            copies.append(pltpu.make_async_copy(source, target, self.own_sem.at[i]))
        if axis != "z" or chunk.kind != "own":
            for step, (_, device) in enumerate(peers_of(axis, self.at, self.size)):
                index = (i, s, step)
                copies.append(self.copy_to(source, target, self.up_send.at[index], self.up_recv.at[index], device))
        return copies

    def stages(self, i):
        return 2 * len(self.chunks[i].order)

    def advance(self, i, stage):
        depth = len(self.chunks[i].order)
        if stage < depth:
            self.add_up(i, stage)
            if stage + 1 < depth:
                self.send_down(i, stage + 1)
            else:
                self.send_up(i, depth - 1)
        else:
            for copy in self.up_copies(i, 2 * depth - 1 - stage):
                copy.wait()
            if stage + 1 < 2 * depth:
                self.send_up(i, 2 * depth - 2 - stage)


class SmallSum:
    def __init__(self, array, result, got, send, recv):
        self.array, self.result, self.got, self.send, self.recv = array, result, got, send, recv
        self.at, self.size = place_of()

    def start(self, s):
        axis = "cxyz"[s]
        source = self.array if s == 0 else self.result
        self.copies = []
        for step, (_, device) in enumerate(peers_of(axis, self.at, self.size)):
            copy = pltpu.make_async_remote_copy(
                src_ref=source, dst_ref=self.got[s].at[self.at[axis]], send_sem=self.send.at[s, step],
                recv_sem=self.recv.at[s, step], device_id=device, device_id_type=pl.DeviceIdType.MESH,
            )
            copy.start()
            self.copies.append(copy)
        self.got[s][self.at[axis]] = source[...]

    def advance(self, s):
        for copy in self.copies:
            copy.wait()
        total = self.got[s][0]
        for j in range(1, self.size["cxyz"[s]]):
            total = total + self.got[s][j]
        self.result[...] = total
        if s < 3:
            self.start(s + 1)


def sum_scratch(chunks, shapes, size):
    scratch = []
    for chunk in chunks:
        blocks, _, width = shapes[chunk.array]
        scratch += [pltpu.VMEM(shape, BF16) for shape in chunk.shapes(blocks, width, size)]
    most = max(size.values()) - 1
    sems = pltpu.SemaphoreType.DMA((len(chunks), 4, most))
    return scratch, [sems] * 4 + [pltpu.SemaphoreType.DMA((len(chunks),))]


def small_scratch(shape, size):
    most = max(size.values()) - 1
    sems = pltpu.SemaphoreType.DMA((4, most))
    return [pltpu.VMEM((size[axis],) + shape, F32) for axis in "cxyz"] + [sems] * 2


def reduce_kernel(chunks, starts, counts, *refs):
    sources, refs = refs[: counts[0]], refs[counts[0] :]
    small_in, refs = refs[0], refs[1:]
    results, refs = refs[: counts[1]], refs[counts[1] :]
    small_out, refs = refs[0], refs[1:]
    scratch, sems, refs = refs[: counts[2]], refs[counts[2] : counts[2] + 5], refs[counts[2] + 5 :]
    small = SmallSum(small_in, small_out, refs[:4], refs[4], refs[5])
    sums = Sums(chunks, sources, results, scratch, sems)
    greet("cxyz", sums.at, sums.size)
    ahead = AHEAD
    for i, start in enumerate(starts):
        if start < ahead:
            sums.send_down(i, 0)
    small.start(0)
    for t in range(max(start + sums.stages(i) for i, start in enumerate(starts))):
        order = range(len(chunks))
        for i in (reversed(order) if NEWEST else order):
            if 0 <= t - starts[i] < sums.stages(i):
                sums.advance(i, t - starts[i])
        for i, start in enumerate(starts):
            if start == t + ahead:
                sums.send_down(i, 0)
        if t < 4:
            small.advance(t)


AHEAD = 2
NEWEST = False


def pieces(rows, unit):
    units = rows // unit
    if units < 2 or not HALVES:
        return [(0, rows)]
    return [(0, -(-units // 2) * unit), (-(-units // 2) * unit, units // 2 * unit)]


HALVES = False


def sum_plan(n, up_rows, down_rows, own_rows, dp, tail_rows):
    unit = 16 * dp
    chunks, starts = [], []

    def pad(rows):
        return -(-rows // unit) * unit

    def add(pair, rows_pair):
        cuts = [pieces(pad(rows), unit) for rows in rows_pair]
        for k in range(max(len(cut) for cut in cuts)):
            start = starts[-1] + 1 if starts else 0
            for (array, kind, result, layer, order), cut in zip(pair, cuts):
                if k < len(cut):
                    chunks.append(Chunk(array, cut[k][0], cut[k][1], order, kind, result, layer, False))
                    starts.append(start)

    add([(0, "wide", 0, 1, "cxyz"), (1, "stack", 1, 1, "cyxz")], (up_rows, down_rows))
    add([(4, "wide", 0, 0, "cxyz"), (5, "stack", 1, 0, "cyxz")], (up_rows, down_rows))
    add([(2, "own", 2, 1, "cxyz"), (3, "own", 3, 1, "cyxz")], (own_rows, own_rows))
    add([(6, "own", 2, 0, "cxyz"), (7, "own", 3, 0, "cyxz")], (own_rows, own_rows))
    chunks.append(Chunk(8, 0, tail_rows, "cxyz", "stack", 4, 0, False))
    starts.append(0)
    return chunks, starts


def reduce_all(arrays, chunks, starts, result_shapes, small, sizes, collective_id):
    scratch, sems = sum_scratch(chunks, [array.shape for array in arrays], sizes)
    counts = (len(arrays), len(result_shapes), len(scratch))
    anywhere = pl.BlockSpec(memory_space=pl.ANY)
    return pl.pallas_call(
        partial(reduce_kernel, chunks, starts, counts),
        out_shape=[jax.ShapeDtypeStruct(shape, BF16) for shape in result_shapes] + [jax.ShapeDtypeStruct(small.shape, F32)],
        in_specs=[anywhere] * len(arrays) + [vmem()],
        out_specs=[anywhere] * len(result_shapes) + [vmem()],
        scratch_shapes=scratch + sems + small_scratch(small.shape, sizes),
        compiler_params=pltpu.CompilerParams(
            collective_id=collective_id, has_side_effects=True, vmem_limit_bytes=VMEM_LIMIT
        ),
        name="sum_gradients",
    )(*arrays, small)


def gather_kernel(orders, *refs):
    count = len(orders)
    mine, results, sems = refs[:2], refs[2 : 2 + count], refs[2 + count :]
    mine = [mine[i % 2].at[i // 2] for i in range(count)]
    send_sem, recv_sem, own_sem = sems
    at, size = place_of()
    greet("cxyz", at, size)
    waiting = {}

    def region(i, s):
        first, rows = 0, mine[i].shape[0]
        for axis in reversed(orders[i][s:]):
            rows = rows // size[axis]
            first = first + at[axis] * rows
        return pl.ds(pl.multiple_of(first, rows), rows)

    def send(i, s):
        axis = orders[i][s]
        copies = []
        if s == 0:
            where = region(i, 1)
            own = pltpu.make_async_copy(mine[i], results[i].at[at["z"]], own_sem.at[i])
            own.start()
            copies.append(own)
        else:
            where = region(i, s)
        for step, (_, device) in enumerate(peers_of(axis, at, size)):
            for other in range(1 if s == 0 else size["z"] - 1):
                block = at["z"] if s == 0 else lax.rem(at["z"] + 1 + other, size["z"])
                source = mine[i].at[where, :] if s == 0 else results[i].at[block, where, :]
                copy = pltpu.make_async_remote_copy(
                    src_ref=source,
                    dst_ref=results[i].at[block, where, :],
                    send_sem=send_sem.at[i, s, step, other],
                    recv_sem=recv_sem.at[i, s, step, other],
                    device_id=device,
                    device_id_type=pl.DeviceIdType.MESH,
                )
                copy.start()
                copies.append(copy)
        waiting[i] = copies

    for t in range(count // 2 + max(len(order) for order in orders)):
        for i in range(count):
            stage = t - i // 2
            if 0 <= stage <= len(orders[i]):
                if stage > 0:
                    for copy in waiting[i]:
                        copy.wait()
                if stage < len(orders[i]):
                    send(i, stage)


def gather_all(arrays, sizes, collective_id):
    layers, rows, width = arrays[0].shape
    n = sizes["z"]
    orders = []
    for i in range(2 * layers):
        left, axes = rows // 16, ""
        for axis in "cxy" if i % 2 else "cyx":
            if left % sizes[axis] == 0:
                left, axes = left // sizes[axis], axis + axes
        orders.append("z" + axes)
    anywhere = pl.BlockSpec(memory_space=pl.ANY)
    most = max(sizes.values()) - 1
    sems = pltpu.SemaphoreType.DMA((len(orders), 4, most, n - 1))
    return pl.pallas_call(
        partial(gather_kernel, orders),
        out_shape=[jax.ShapeDtypeStruct((n, rows, width), BF16) for _ in orders],
        in_specs=[vmem()] * 2,
        out_specs=[vmem()] * len(orders),
        scratch_shapes=[sems, sems, pltpu.SemaphoreType.DMA((len(orders),))],
        compiler_params=pltpu.CompilerParams(collective_id=collective_id, has_side_effects=True),
        name="gather_experts",
    )(*arrays)


def layer_spec(array, layer):
    block = (None,) + array.shape[1:]
    return pl.BlockSpec(block, lambda *_: (layer,) + (0,) * (array.ndim - 1), pipeline_mode=pl.Buffered(1))


def share(mine, n, scatter, collective_id, name):
    rows = mine.shape[0] // n if scatter else mine.shape[0]
    return pl.pallas_call(
        partial(share_kernel, n, scatter),
        out_shape=jax.ShapeDtypeStruct((n, rows, mine.shape[1]), mine.dtype),
        in_specs=[vmem()],
        out_specs=vmem(),
        scratch_shapes=[pltpu.SemaphoreType.DMA((n - 1,)), pltpu.SemaphoreType.DMA((n - 1,))],
        compiler_params=pltpu.CompilerParams(collective_id=collective_id, has_side_effects=True),
        name=name,
    )(mine)


class KeyvalSum:
    def __init__(self, mine, got, send, recv):
        self.mine, self.got, self.send, self.recv = mine, got, send, recv
        self.at, self.size = place_of()

    def part(self, place):
        rows = self.got.shape[1]
        return self.mine.at[pl.ds(pl.multiple_of(place * rows, rows), rows), :]

    def start(self):
        self.copies = []
        for step, (place, device) in enumerate(peers_of("z", self.at, self.size)):
            copy = pltpu.make_async_remote_copy(
                src_ref=self.part(place), dst_ref=self.got.at[step], send_sem=self.send.at[step],
                recv_sem=self.recv.at[step], device_id=device, device_id_type=pl.DeviceIdType.MESH,
            )
            copy.start()
            self.copies.append(copy)

    def total(self):
        for copy in self.copies:
            copy.wait()
        total = self.part(self.at["z"])[...].astype(F32)
        for step in range(self.got.shape[0]):
            total = total + self.got[step].astype(F32)
        return total.astype(BF16)


def finish_chunks(n, up_rows, down_rows, own_rows, tail_rows):
    groups = [
        [Chunk(0, 0, up_rows, "cxyz", "wide", 0, 1, False), Chunk(1, 0, down_rows, "cyxz", "stack", 1, 1, False)],
        [Chunk(2, 0, own_rows, "cxyz", "own", 2, 1, False), Chunk(3, 0, own_rows, "cyxz", "own", 3, 1, False)],
        [Chunk(4, 0, up_rows, "cxyz", "wide", 0, 0, True), Chunk(5, 0, down_rows, "cyxz", "stack", 1, 0, True)],
        [Chunk(6, 0, own_rows, "cxyz", "own", 2, 0, True), Chunk(7, 0, own_rows, "cyxz", "own", 3, 0, True)],
        [Chunk(8, 0, tail_rows, "cxyz", "stack", 4, 0, True)],
    ]
    chunks, numbers = [], []
    for group in groups:
        numbers.append(list(range(len(chunks), len(chunks) + len(group))))
        chunks += group
    return chunks, numbers


def finish_kernel(chunks, groups, counts, *refs):
    weights, refs = weights_of(0, refs)
    later, refs = named(LATER[:2] + ("part",) + LATER[3:] + ("router",), refs)
    (x, normed, routes, lengths, keep, small), refs = refs[:6], refs[6:]
    kept, refs = named(KEPT, refs)
    last_grads, refs = refs[:4], refs[4:]
    input_grad, refs = refs[0], refs[1:]
    results, refs = refs[:5], refs[5:]
    small_out, refs = refs[0], refs[1:]
    out, refs = named(OUT, refs)
    sums, refs = named(SUMS, refs)
    (mask, spread, dense, gated), refs = refs[:4], refs[4:]
    (tail, small_in, got1, got0), refs = refs[:4], refs[4:]
    scratch, refs = refs[:counts], refs[counts:]
    small_got, refs = refs[:4], refs[4:]
    sems, small_sems, (send1, recv1, send0, recv0) = refs[:5], refs[5:7], refs[7:]
    sources = list(last_grads) + [out.up, out.down, out.w_query, out.w_out, tail]
    total = Sums(chunks, sources, results, scratch, sems)
    little = SmallSum(small_in, small_out, small_got, *small_sems)
    keyval1 = KeyvalSum(later.part, got1, send1, recv1)
    keyval0 = KeyvalSum(out.keyval, got0, send0, recv0)
    done = [0] * len(groups)

    def begin(group):
        for i in groups[group]:
            total.send_down(i, 0)

    def advance(group):
        if done[group] < total.stages(groups[group][0]):
            for i in groups[group]:
                total.advance(i, done[group])
            done[group] += 1

    greet("cxyz", total.at, total.size)
    keyval1.start()
    begin(0)
    begin(1)
    fill_mask(lengths, keep, mask)
    spread_routes(routes, spread)
    tail[...] = jnp.zeros(tail.shape, BF16)
    rows = small.shape[0]
    experts = weights.w_router.shape[0]
    small_in[0:rows, :] = small[...]
    small_in[rows : 2 * rows, :] = later.small[...]
    small0, small1 = small_in.at[0:rows, :], small_in.at[rows : 2 * rows, :]
    out.small = small0
    tail[3, 0:experts, :] = later.router[...].astype(BF16)
    advance(0)
    stream_grad = layer_finish(
        later.x[...], later.normed, keyval1.total(), later.gain1[1:2, :], later.w_kv[...],
        later.middle_grad, later.normed_grad, tail.at[2, 0 : later.w_kv.shape[1]], small1,
    )

    def between(place, k=None):
        if place == "hidden":
            begin(2)
            advance(0)
            advance(1)
        elif place == "slot":

            @pl.when(k == 2)
            def _():
                advance(0)

            @pl.when(k == 5)
            def _():
                advance(1)
                advance(2)

        elif place == "keyval":
            keyval0.start()
            advance(0)

    layer_back(stream_grad, normed, weights, mask, spread, dense, gated, kept, sums, out, between)
    tail[1, 0:experts, :] = out.router[...].astype(BF16)
    begin(3)
    advance(1)
    input_grad[...] = layer_finish(
        x[...].astype(F32), normed, keyval0.total(), weights.gain1[...], weights.w_kv[...],
        out.middle_grad, out.normed_grad, tail.at[0, 0 : weights.w_kv.shape[1]], small0,
    )
    begin(4)
    little.start(0)
    for step in range(2 * len(chunks[-1].order)):
        for group in range(len(groups)):
            advance(group)
        if step < 4:
            little.advance(step)


def finish_all(args, last_grads, out_shapes, work, result_shapes, sizes):
    specs, arrays = specs_of(args)
    n, up_rows, _ = last_grads[0].shape
    tail_shape = result_shapes[4][1:]
    chunks, groups = finish_chunks(n, up_rows, last_grads[1].shape[1], last_grads[2].shape[1], tail_shape[1])
    shapes = [array.shape for array in last_grads] * 2 + [tail_shape]
    scratch, sems = sum_scratch(chunks, shapes, sizes)
    count, width = out_shapes[-1][0]
    small_shape = (2 * out_shapes[6][0][0], width)
    group, pair = out_shapes[5][0]
    got = pltpu.VMEM((n - 1, group // n, pair), BF16)
    anywhere = pl.BlockSpec(memory_space=pl.ANY)
    return pl.pallas_call(
        partial(finish_kernel, chunks, groups, len(scratch)),
        out_shape=[jax.ShapeDtypeStruct((count, width), F32)]
        + [jax.ShapeDtypeStruct(shape, BF16) for shape in result_shapes]
        + [jax.ShapeDtypeStruct(small_shape, F32)],
        grid=(1,),
        in_specs=specs + [anywhere] * len(last_grads),
        out_specs=[vmem()] + [anywhere] * len(result_shapes) + [vmem()],
        scratch_shapes=[pltpu.VMEM(shape, dtype) for shape, dtype in out_shapes + work]
        + [pltpu.VMEM(tail_shape, BF16), pltpu.VMEM(small_shape, F32), got, got]
        + scratch + small_scratch(small_shape, sizes)[:4] + sems + small_scratch(small_shape, sizes)[4:]
        + [pltpu.SemaphoreType.DMA((n - 1,))] * 4,
        compiler_params=pltpu.CompilerParams(
            collective_id=4, has_side_effects=True, vmem_limit_bytes=62 << 20
        ),
        name="first_block_back_and_sums",
    )(*arrays, *last_grads)


class Gather:
    def __init__(self, sources, targets, orders, send, recv, own_sem):
        self.sources, self.targets, self.orders = sources, targets, orders
        self.send, self.recv, self.own_sem = send, recv, own_sem
        self.at, self.size = place_of()
        self.stage = [0] * len(sources)

    def copies(self, i, s):
        rows, order = self.sources[i].shape[0], self.orders[i]
        first, part = 0, rows
        for axis in reversed(order[max(s, 1) :]):
            part = part // self.size[axis]
            first = first + self.at[axis] * part
        here = self.at["z"]
        out = []
        if s == 0:
            place = pl.ds(pl.multiple_of(here * rows, rows), rows)
            out.append(pltpu.make_async_copy(self.sources[i], self.targets[i].at[place, :], self.own_sem.at[i]))
        for step, (_, device) in enumerate(peers_of(order[s], self.at, self.size)):
            for other in range(1 if s == 0 else self.size["z"] - 1):
                block = here if s == 0 else lax.rem(here + 1 + other, self.size["z"])
                target = self.targets[i].at[pl.ds(pl.multiple_of(block * rows + first, part), part), :]
                source = self.sources[i].at[pl.ds(pl.multiple_of(first, part), part), :] if s == 0 else target
                index = (i, s, step, other)
                out.append(
                    pltpu.make_async_remote_copy(
                        src_ref=source, dst_ref=target, send_sem=self.send.at[index], recv_sem=self.recv.at[index],
                        device_id=device, device_id_type=pl.DeviceIdType.MESH,
                    )
                )
        return out

    def begin(self, i):
        for copy in self.copies(i, 0):
            copy.start()

    def advance(self, i):
        s = self.stage[i]
        for copy in self.copies(i, s):
            copy.wait()
        self.stage[i] = s + 1
        if s + 1 < len(self.orders[i]):
            for copy in self.copies(i, s + 1):
                copy.start()


def share_orders(rows, count, size):
    orders = []
    for i in range(count):
        left, axes = rows // 16, ""
        for axis in "cxy" if i % 2 else "cyx":
            if left % size[axis] == 0:
                left, axes = left // size[axis], axis + axes
        orders.append("z" + axes)
    return orders


class KeyvalGather:
    def __init__(self, keyval, count, send, recv):
        self.keyval, self.count, self.send, self.recv = keyval, count, send, recv
        self.at, self.size = place_of()

    def own(self):
        return self.keyval.at[pl.ds(pl.multiple_of(self.at["z"] * self.count, self.count), self.count), :]

    def copies(self):
        return [
            pltpu.make_async_remote_copy(
                src_ref=self.own(), dst_ref=self.own(), send_sem=self.send.at[step], recv_sem=self.recv.at[step],
                device_id=device, device_id_type=pl.DeviceIdType.MESH,
            )
            for step, (_, device) in enumerate(peers_of("z", self.at, self.size))
        ]

    def start(self):
        for copy in self.copies():
            copy.start()

    def wait(self):
        for copy in self.copies():
            copy.wait()


INPUTS = ("x", "cotangent", "routes", "lengths", "keep", "gain1", "bias1", "w_kv", "w_router", "gain2", "bias2")
GRADS = ("up", "down", "w_query", "w_out")


def whole_kernel(chunks, groups, counts, *refs):
    given, refs = named(INPUTS, refs)
    (queries, outs, w_up, w_down), refs = refs[:4], refs[4:]
    (activations, input_grad), refs = refs[:2], refs[2:]
    results, small_out, refs = refs[:5], refs[5], refs[6:]
    experts_in, refs = refs[:4], refs[4:]
    (up_here, down_here), refs = refs[:2], refs[2:]
    kept, normed = [], []
    for _ in range(2):
        normed.append(refs[0])
        one, refs = named(KEPT, refs[1:])
        kept.append(one)
    grads = []
    for _ in range(2):
        one, refs = named(GRADS, refs)
        grads.append(one)
    (stream, router, middle_grad, normed_grad, part1, part0, tail, small_in), refs = refs[:8], refs[8:]
    sums, refs = named(SUMS, refs)
    (mask, spread, dense, gated, got1, got0), refs = refs[:6], refs[6:]
    scratch, refs = refs[:counts], refs[counts:]
    small_got, refs = refs[:4], refs[4:]
    sems, small_sems, refs = refs[:5], refs[5:7], refs[7:]
    gather_sems, keyval_sems, load_sem = refs[:3], refs[3:11], refs[11]

    count, width = given.x.shape
    rows = small_in.shape[0] // 2
    experts = given.w_router.shape[1]
    pair = given.w_kv.shape[2]
    sources = []
    for l in (1, 0):
        sources += [getattr(grads[l], name) for name in GRADS]
    total = Sums(chunks, sources + [tail], results, scratch, sems)
    little = SmallSum(small_in, small_out, small_got, *small_sems)
    smalls = [small_in.at[0:rows, :], small_in.at[rows : 2 * rows, :]]
    gather = Gather(
        [queries.at[0], outs.at[0], queries.at[1], outs.at[1]], experts_in,
        share_orders(queries.shape[1], 4, total.size), *gather_sems,
    )
    keyval_gather = [KeyvalGather(kept[l].keyval, count, *keyval_sems[2 * l : 2 * l + 2]) for l in range(2)]
    keyval_sum = [KeyvalSum(part0, got0, *keyval_sems[4:6]), KeyvalSum(part1, got1, *keyval_sems[6:8])]
    weights = []
    for l in range(2):
        row = pl.ds(l, 1)
        weights.append(
            Refs(
                gain1=given.gain1.at[row, :], bias1=given.bias1.at[row, :], gain2=given.gain2.at[row, :],
                bias2=given.bias2.at[row, :], w_kv=given.w_kv.at[l], w_router=given.w_router.at[l],
                w_query=experts_in[2 * l], w_out=experts_in[2 * l + 1], w_up=up_here, w_down=down_here,
            )
        )
    outputs = [
        Refs(
            up=grads[l].up, down=grads[l].down, w_out=grads[l].w_out, w_query=grads[l].w_query, router=router,
            keyval=(part0, part1)[l], small=smalls[l], middle_grad=middle_grad, normed_grad=normed_grad,
        )
        for l in range(2)
    ]

    def loads(l):
        return [
            pltpu.make_async_copy(w_up.at[l], up_here, load_sem.at[l, 0]),
            pltpu.make_async_copy(w_down.at[l], down_here, load_sem.at[l, 1]),
        ]

    def load(l):
        for copy in loads(l):
            copy.start()

    def loaded(l):
        for copy in loads(l):
            copy.wait()

    done = [0] * len(groups)

    def begin(group):
        for i in groups[group]:
            total.send_down(i, 0)

    def advance(group):
        if done[group] < total.stages(groups[group][0]):
            for i in groups[group]:
                total.advance(i, done[group])
            done[group] += 1

    def pre(l, x):
        pre_layer(x, weights[l].gain1[...], weights[l].bias1[...], weights[l].w_kv[...], normed[l], keyval_gather[l].own())
        keyval_gather[l].start()

    load(0)
    greet("cxyz", total.at, total.size)
    gather.begin(0)
    gather.begin(1)
    x = given.x[...].astype(F32)
    pre(0, x)
    gather.begin(2)
    gather.begin(3)
    fill_mask(given.lengths, given.keep, mask)
    spread_routes(given.routes.at[0], spread)
    small_in[...] = jnp.zeros(small_in.shape, F32)
    tail[...] = jnp.zeros(tail.shape, BF16)
    for i in (0, 1, 0, 1, 0, 1, 0):
        gather.advance(i)
    keyval_gather[0].wait()

    def first_between(place, k=None):
        if place == "slot":
            for when in (1, 4):

                @pl.when(k == when)
                def _():
                    gather.advance(2)
                    gather.advance(3)

        elif place == "attended":
            gather.advance(1)
            gather.advance(2)
            gather.advance(3)
        elif place == "middle":
            loaded(0)

    result, picked = layer_forward(x, normed[0], weights[0], mask, spread, dense, gated, kept[0], first_between)
    load(1)
    count_chosen(picked, given.keep, smalls[0])
    stream[...] = result
    pre(1, result)
    spread_routes(given.routes.at[1], spread)

    def second_between(place, k=None):
        if place == "queries":
            keyval_gather[1].wait()
        elif place == "middle":
            loaded(1)

    gather.advance(2)
    gather.advance(3)
    result, picked = layer_forward(
        stream[...], normed[1], weights[1], mask, spread, dense, gated, kept[1], second_between
    )
    count_chosen(picked, given.keep, smalls[1])
    activations[...] = result.astype(BF16)
    kept_col = jnp.broadcast_to(own_columns(given.keep, count).astype(F32), (LANES, count)).T
    kept_col = jnp.concatenate([kept_col] * (width // LANES), axis=1)

    def last_between(place, k=None):
        if place == "hidden":
            load(0)
            begin(0)
        elif place == "out":
            pass
        elif place == "slot":

            @pl.when(k == 1)
            def _():
                advance(0)

        elif place == "keyval":
            keyval_sum[1].start()
            advance(0)

    layer_back(
        given.cotangent[...].astype(F32) * kept_col, normed[1], weights[1], mask, spread, dense, gated, kept[1],
        sums, outputs[1], last_between,
    )
    tail[3, 0:experts, :] = router[...].astype(BF16)
    begin(1)
    stream_grad = layer_finish(
        stream[...], normed[1], keyval_sum[1].total(), weights[1].gain1[...], weights[1].w_kv[...], middle_grad,
        normed_grad, tail.at[2, 0:pair], smalls[1],
    )
    advance(0)
    advance(1)
    spread_routes(given.routes.at[0], spread)
    loaded(0)

    def between(place, k=None):
        if place == "hidden":
            begin(2)
            advance(0)
            advance(1)
        elif place == "slot":

            @pl.when(k == 2)
            def _():
                advance(0)
                advance(2)

            @pl.when(k == 5)
            def _():
                advance(1)

        elif place == "keyval":
            keyval_sum[0].start()
            advance(0)
            advance(2)

    layer_back(
        stream_grad, normed[0], weights[0], mask, spread, dense, gated, kept[0], sums, outputs[0], between
    )
    tail[1, 0:experts, :] = router[...].astype(BF16)
    begin(3)
    advance(1)
    input_grad[...] = layer_finish(
        given.x[...].astype(F32), normed[0], keyval_sum[0].total(), weights[0].gain1[...], weights[0].w_kv[...],
        middle_grad, normed_grad, tail.at[0, 0:pair], smalls[0],
    )
    begin(4)
    little.start(0)
    for step in range(2 * len(chunks[-1].order)):
        for group in range(len(groups)):
            advance(group)
        if step < 4:
            little.advance(step)


def run_whole(args, weights_out, shapes, sizes):
    specs, arrays = specs_of(args)
    queries, _, w_up, w_down = weights_out
    layers, own, width = queries.shape
    n = sizes["z"]
    count, flat, hidden = args[0][0].shape[0], n * own, w_up.shape[2]
    chunks, groups = finish_chunks(n, shapes.up[1], shapes.down[1], shapes.own[1], shapes.tail[1])
    scratch, sems = sum_scratch(chunks, [shapes.up, shapes.down, shapes.own, shapes.own] * 2 + [shapes.tail], sizes)
    small_shape = (16, width)
    results = [
        (layers, shapes.up[1], hidden), (layers,) + shapes.down, (layers,) + shapes.own[1:], (layers,) + shapes.own[1:],
        (1,) + shapes.tail,
    ]
    most = max(sizes.values()) - 1
    gather_sem = pltpu.SemaphoreType.DMA((4, 4, most, n - 1))
    got = pltpu.VMEM((n - 1, shapes.group // n, shapes.pair), BF16)
    part = pltpu.VMEM((shapes.group, shapes.pair), BF16)
    one = pltpu.VMEM((count, width), F32)
    local = [pltpu.VMEM((flat, width), BF16)] * 4
    local += [pltpu.VMEM(w_up.shape[1:], BF16), pltpu.VMEM(w_down.shape[1:], BF16)]
    for _ in range(2):
        local += [pltpu.VMEM((count, width), BF16), part]
        local += [pltpu.VMEM(shape, dtype) for shape, dtype in shapes.kept]
    local += [pltpu.VMEM(shape, BF16) for shape in (shapes.up, shapes.down, shapes.own, shapes.own)] * 2
    local += [one, pltpu.VMEM((shapes.experts, width), F32), one, one, part, part]
    local += [pltpu.VMEM(shapes.tail, BF16), pltpu.VMEM(small_shape, F32)]
    local += [pltpu.VMEM(shape, dtype) for shape, dtype in shapes.sums]
    mask, spread, dense, gated = [pltpu.VMEM(shape, dtype) for shape, dtype in shapes.work]
    local += [mask, spread, dense, gated, got, got]
    small_refs = small_scratch(small_shape, sizes)
    anywhere = pl.BlockSpec(memory_space=pl.ANY)
    return pl.pallas_call(
        partial(whole_kernel, chunks, groups, len(scratch)),
        out_shape=[jax.ShapeDtypeStruct((count, width), BF16), jax.ShapeDtypeStruct((count, width), F32)]
        + [jax.ShapeDtypeStruct(shape, BF16) for shape in results]
        + [jax.ShapeDtypeStruct(small_shape, F32)],
        grid=(1,),
        in_specs=specs + [anywhere] * 4,
        out_specs=[vmem(), vmem()] + [anywhere] * 5 + [vmem()],
        scratch_shapes=local + scratch + small_refs[:4] + sems + small_refs[4:]
        + [gather_sem, gather_sem, pltpu.SemaphoreType.DMA((4,))]
        + [pltpu.SemaphoreType.DMA((n - 1,))] * 8
        + [pltpu.SemaphoreType.DMA((2, 2))],
        compiler_params=pltpu.CompilerParams(
            collective_id=5, has_side_effects=True, vmem_limit_bytes=63 << 20
        ),
        name="both_blocks",
    )(*arrays, *weights_out)


def specs_of(args):
    specs, arrays = [], []
    for array, layer in args:
        arrays.append(array)
        if layer == "smem":
            specs.append(pl.BlockSpec(memory_space=pltpu.SMEM))
        elif layer is None:
            specs.append(pl.BlockSpec(array.shape, lambda *_, nd=array.ndim: (0,) * nd, pipeline_mode=pl.Buffered(1)))
        else:
            specs.append(layer_spec(array, layer))
    return specs, arrays


def call(kernel, args, outs, scratch, name):
    specs, arrays = specs_of(args)
    return pl.pallas_call(
        kernel,
        out_shape=[jax.ShapeDtypeStruct(shape, dtype) for shape, dtype in outs],
        grid=(1,),
        in_specs=specs,
        out_specs=[pl.BlockSpec(shape, lambda *_, nd=len(shape): (0,) * nd, pipeline_mode=pl.Buffered(1)) for shape, _ in outs],
        scratch_shapes=[pltpu.VMEM(shape, dtype) for shape, dtype in scratch],
        compiler_params=pltpu.CompilerParams(vmem_limit_bytes=VMEM_LIMIT),
        name=name,
    )(*arrays)


def body(
    tokens, cotangent, routes, keep, lengths, norm1_gain, norm1_bias, w_kv, w_router, w_query, w_out,
    norm2_gain, norm2_bias, w_up, w_down,
):
    n = lax.axis_size("exp")
    dp = lax.axis_size("dp")
    layers, width, pair = w_kv.shape
    count = tokens.shape[1]
    group = routes.shape[2]
    topk = routes.shape[3]
    experts = w_router.shape[2]
    head = w_query.shape[3]
    local = w_query.shape[1]
    hidden = w_up.shape[2]
    flat = experts * head
    own = local * head
    x0 = tokens[0]
    routes_t = jnp.swapaxes(routes[:, 0], 1, 2)
    router_t = jnp.swapaxes(w_router, 1, 2)
    gain1, bias1, gain2, bias2 = norm1_gain, norm1_bias, norm2_gain, norm2_bias
    queries_t = jnp.swapaxes(w_query, 2, 3).reshape(layers, own, width)
    outs = w_out.reshape(layers, own, width)
    sizes = axis_sizes()

    def rows_of(least):
        return -(-least // (16 * dp)) * 16 * dp

    kept_shapes = [
        ((count, experts), F32), ((topk, count, LANES), BF16), ((topk, 8, count), F32),
        ((topk, count, LANES), BF16), ((count, flat), BF16), ((count, width), F32),
    ]
    work = [((group, count), F32), ((topk, count, LANES), jnp.int32), ((count, flat), F32), ((count, flat), F32)]
    sum_shapes = [((count, width), F32), ((group, pair), F32), ((group, pair), F32), ((count, experts), F32)]
    out_shapes = [
        ((n, rows_of(width), hidden // n), BF16), ((n, rows_of(hidden // n), width), BF16),
        ((n, rows_of(own), width), BF16), ((n, rows_of(own), width), BF16),
        ((experts, width), F32), ((group, pair), BF16), ((8, width), F32), ((count, width), F32), ((count, width), F32),
    ]
    if n * dp == 32 and layers == 2:
        all_shapes = Refs(
            up=out_shapes[0][0], down=out_shapes[1][0], own=out_shapes[2][0], tail=(n, rows_of(pair), width), group=group,
            pair=pair, experts=experts, kept=kept_shapes, sums=sum_shapes, work=work,
        )
        given = [
            (x0, None), (cotangent[0], None), (routes_t, None), (lengths, "smem"), (keep, None), (gain1, None),
            (bias1, None), (w_kv, None), (router_t, None), (gain2, None), (bias2, None),
        ]
        activations, input_grad, up, down, expert_query, expert_out, tail, small = run_whole(
            given, (queries_t, outs, w_up, w_down), all_shapes, sizes
        )
    else:
        gathered = [array.reshape(flat, width) for array in gather_all((queries_t, outs), sizes, 2)]
        wq, wo = gathered[0::2], gathered[1::2]
        def weights(l):
            return [(gain1, None), (bias1, None), (w_kv, l), (router_t, l), (wq[l], None), (wo[l], None), (gain2, None), (bias2, None), (w_up, l), (w_down, l)]


        normed0, keyval0 = call(
            pre_kernel, [(x0, None), (gain1, None), (bias1, None), (w_kv, 0)],
            [((count, width), BF16), ((count, pair), BF16)], [], "pre",
        )
        keyval0 = share(keyval0, n, False, 0, "gather_keyval").reshape(group, pair)
        *kept0, x1, normed1, keyval1, small0 = call(
            first_kernel,
            weights(0) + [(x0, None), (normed0, None), (keyval0, None), (routes_t, 0), (lengths, "smem"), (keep, None), (gain1, None), (bias1, None), (w_kv, 1)],
            kept_shapes + [((count, width), F32), ((count, width), BF16), ((count, pair), BF16), ((8, width), F32)],
            work, "first_block",
        )
        keyval1 = share(keyval1, n, False, 0, "gather_keyval").reshape(group, pair)
        activations, up1, down1, out1, query1, router1, part1, small1, mid1, ngrad1 = call(
            turn_kernel,
            weights(1) + [(x1, None), (normed1, None), (keyval1, None), (routes_t, 1), (lengths, "smem"), (keep, None), (cotangent[0], None)],
            [((count, width), BF16)] + out_shapes, kept_shapes + sum_shapes + work, "second_block",
        )
        tail_rows = rows_of(pair)
        result_shapes = [
            (layers,) + up1.shape[1:2] + (hidden,), (layers,) + down1.shape, (layers,) + query1.shape[1:],
            (layers,) + out1.shape[1:], (1, n, tail_rows, width),
        ]
        received1 = share(part1, n, True, 1, "scatter_keyval")
        kv1, small1, up0, down0, out0, query0, router0, part0, small0, mid0, ngrad0 = call(
            back_kernel,
            weights(0) + [(x1, None), (normed1, None), (received1, None), (gain1, None), (w_kv, 1), (mid1, None), (ngrad1, None), (small1, None),
             (normed0, None), (routes_t, 0), (lengths, "smem"), (keep, None), (small0, None), (keyval0, None)] + [(v, None) for v in kept0],
            [((pair, width), BF16), ((8, width), F32)] + out_shapes, sum_shapes + work, "first_block_back",
        )
        received0 = share(part0, n, True, 1, "scatter_keyval")
        kv0, small0, input_grad = call(
            end_kernel,
            [(x0, None), (normed0, None), (received0, None), (gain1, None), (w_kv, 0), (mid0, None), (ngrad0, None), (small0, None)],
            [((pair, width), BF16), ((8, width), F32), ((count, width), F32)], [], "end",
        )
        tail = jnp.zeros((n, tail_rows, width), BF16)
        for block, rows in enumerate((kv0, router0, kv1, router1)):
            tail = tail.at[block, : rows.shape[0]].set(rows.astype(BF16))
        chunks, starts = sum_plan(n, width, hidden // n, own, dp, tail_rows)
        arrays = [up1, down1, query1, out1, up0, down0, query0, out0, tail]
        up, down, expert_query, expert_out, tail, small = reduce_all(
            arrays, chunks, starts,
            result_shapes,
            jnp.concatenate([small0, small1]), sizes, 3,
        )
    down = down[:, :, : hidden // n].reshape(layers, hidden, width).astype(F32)
    kv = jnp.swapaxes(tail[0, 0:4:2, :pair].astype(F32), 1, 2)
    router = jnp.swapaxes(tail[0, 1:4:2, :experts].astype(F32), 1, 2)
    norms = small.reshape(layers, -1, width)
    expert_query = jnp.swapaxes(expert_query[:, :own].reshape(layers, local, head, width), 2, 3).astype(F32)
    expert_out = expert_out[:, :own].reshape(layers, local, head, width).astype(F32)
    return (
        activations[None], input_grad[None], norms[:, 0], norms[:, 1], kv, router, expert_query, expert_out,
        norms[:, 2], norms[:, 3], up[:, :width].astype(F32), down, norms[:, 4, :experts],
    )


def solution(mesh):
    return jax.shard_map(
        body,
        mesh=mesh,
        in_specs=(
            P("dp", "exp", None), P("dp", "exp", None), P(None, "dp", None, None), P("dp", None), P("dp", None),
            P(), P(), P(), P(), P(None, "exp", None, None), P(None, "exp", None, None), P(), P(), P(), P(),
        ),
        out_specs=(
            P("dp", "exp", None), P("dp", "exp", None), P(), P(), P(), P(),
            P(None, "exp", None, None), P(None, "exp", None, None), P(), P(), P(), P(), P(),
        ),
        check_vma=False,
    )
```

```python
from functools import partial
import math

import jax
import jax.numpy as jnp
from jax import lax
from jax.experimental import pallas as pl
from jax.experimental.pallas import tpu as pltpu
from jax.sharding import PartitionSpec as P

F32 = jnp.float32
EXP = "exp"
CLHXY = "clhxy"
CLHYX = "clhyx"
CXLHY = "cxlhy"
CXYLH = "cxylh"
CXYZ = "cxyz"
CYLHX = "cylhx"
CYXLH = "cyxlh"
CYXZ = "cyxz"
ZXYC = "zxyc"
ZYXC = "zyxc"
WIDE, STACK, OWN = range(3)
BF16 = jnp.bfloat16
LANES = 128
epsilon = 1e-05
neg_big = -1e30
never = 1 << 30
gelu_c = 0.7978845608028654
gelu_a = 0.044715
VMEM_LIMIT = 56 << 20


def nn(a, b):
    return jnp.dot(a, b, preferred_element_type=F32)


def nt(a, b):
    return lax.dot_general(a, b, (((1,), (1,)), ((), ())), preferred_element_type=F32)


def tn(a, b):
    return lax.dot_general(a, b, (((0,), (0,)), ((), ())), preferred_element_type=F32)


def iota(shape, axis):
    return lax.broadcasted_iota(jnp.int32, shape, axis)


def norm_parts(values):
    center = values - jnp.mean(values, axis=-1, keepdims=True)
    spread = jnp.mean(center * center, axis=-1, keepdims=True)
    scale = lax.rsqrt(spread + epsilon)
    return center * scale, scale


def norm_back(hat, scale, gain, grad):
    scaled = grad * gain
    first = jnp.mean(scaled, axis=-1, keepdims=True)
    second = jnp.mean(scaled * hat, axis=-1, keepdims=True)
    back = scale * (scaled - first - hat * second)
    return back, jnp.sum(grad * hat, axis=0, keepdims=True), jnp.sum(grad, axis=0, keepdims=True)


def gelu_parts(v):
    inner = jnp.tanh(gelu_c * (v + gelu_a * v * v * v))
    half = 0.5 * (1.0 + inner)
    return v * half, half + 0.5 * v * (1.0 - inner * inner) * gelu_c * (1.0 + 3.0 * gelu_a * v * v)


def lane_half(shape):
    return (iota(shape, 1) >= LANES // 2).astype(jnp.int32)


def select_tiles(dense, chosen):
    out = jnp.zeros(chosen.shape, F32)
    for tile in range(dense.shape[1] // LANES):
        out = jnp.where(chosen == 2 * tile, dense[:, tile * LANES : (tile + 1) * LANES], out)
    return out


def place_tiles(dense, chosen, values):
    for tile in range(dense.shape[1] // LANES):
        where = slice(tile * LANES, (tile + 1) * LANES)
        dense[:, where] = jnp.where(chosen == 2 * tile, values, dense[:, where])


def own_columns(ref, count):
    start = lax.axis_index(EXP) * count
    return ref[:, pl.ds(pl.multiple_of(start, count), count)]


def spread_routes(routes, spread):
    topk, count, lanes = spread.shape
    own = own_columns(routes, count)
    for k in range(topk):
        spread[k] = jnp.broadcast_to(own[k : k + 1, :], (lanes, count)).T


def fill_mask(lengths, keep, mask):
    group, count = mask.shape
    start = lax.axis_index(EXP) * count
    position = start + iota((1, count), 1)
    low = jnp.zeros((1, count), jnp.int32)
    end = 0
    for s in range(lengths.shape[1] - 1):
        end = end + lengths[0, s]
        low = jnp.where(position >= end, end, low)
    kept = jnp.broadcast_to(keep[...], (LANES, group)).T
    kept = jnp.concatenate([kept] * (count // LANES), axis=1)
    key = iota((group, count), 0)
    usable = jnp.where(kept > 0, key, never)
    allowed = ((usable >= low) & (usable <= position)) | (key == position)
    mask[...] = jnp.where(allowed, 0.0, neg_big)


def split_keyval(keyval):
    both = keyval.astype(F32)
    swapped = pltpu.roll(both, LANES // 2, 1)
    first = iota(both.shape, 1) < LANES // 2
    return jnp.where(first, both, swapped), jnp.where(first, swapped, both)


def pre_layer(x, gain1, bias1, w_kv, normed, keyval_own):
    hat, _ = norm_parts(x)
    normed[...] = (hat * gain1 + bias1).astype(BF16)
    keyval_own[...] = nn(normed[...], w_kv).astype(BF16)


def make_gates(normed, w_router, spread):
    logits = nt(normed, w_router)
    experts = logits.shape[1]
    lanes = iota(logits.shape, 1)
    picked = spread[0][:, :experts] == lanes
    for k in range(1, spread.shape[0]):
        picked = picked | (spread[k][:, :experts] == lanes)
    top = jnp.max(jnp.where(picked, logits, neg_big), axis=1, keepdims=True)
    shares = jnp.where(picked, jnp.exp(jnp.minimum(logits - top, 0.0)), 0.0)
    return shares / jnp.sum(shares, axis=1, keepdims=True), picked


def gate_column(gates, spread_k):
    lanes = iota(gates.shape, 1)
    return jnp.sum(
        jnp.where(spread_k[:, : gates.shape[1]] == lanes, gates, 0.0), axis=1, keepdims=True
    )


def layer_forward(x, normed, weights, mask, spread, dense, gated, kept, between=None):
    between = between or (lambda *place: None)
    count = normed.shape[0]
    gates, picked = make_gates(normed[...], weights.w_router[...], spread)
    kept.gates[...] = gates
    dense[...] = nt(normed[...], weights.w_query[...]).astype(BF16).astype(F32) * 0.125
    gated[...] = jnp.zeros(gated.shape, F32)
    between("queries")
    keys, values = split_keyval(kept.keyval[...])
    keys = keys.astype(BF16)
    values_t = values.T.astype(BF16)

    def pair(step, carry):
        slots = [2 * step, 2 * step + 1]
        which = [spread[k] for k in slots]
        chosen = [w - lane_half((count, LANES)) for w in which]
        queries = [select_tiles(dense, c).astype(BF16) for c in chosen]
        scores = [nt(keys, query) + mask[...] for query in queries]
        tops = [jnp.max(score, axis=0, keepdims=True) for score in scores]
        shares = [jnp.exp(score - top) for score, top in zip(scores, tops)]
        totals = [jnp.sum(share, axis=0, keepdims=True) for share in shares]
        rounded = [(share * (1.0 / total)).astype(BF16) for share, total in zip(shares, totals)]
        attended = [nn(values_t, share).T.astype(BF16) for share in rounded]
        for i, k in enumerate(slots):
            kept.query[k] = queries[i]
            kept.lse[k] = jnp.broadcast_to(tops[i] + jnp.log(totals[i]), kept.lse.shape[1:])
            kept.attended[k] = attended[i]
            gate = gate_column(kept.gates[...], which[i])
            place_tiles(gated, chosen[i], gate * attended[i].astype(F32))
        between("slot", step)
        return carry

    lax.fori_loop(0, spread.shape[0] // 2, pair, 0)
    kept.gated[...] = gated[...].astype(BF16)
    between("attended")
    middle = x + nn(kept.gated[...], weights.w_out[...])
    kept.middle[...] = middle
    between("middle")
    return middle, picked


def feed_forward(middle, weights):
    hat, _ = norm_parts(middle)
    normed2 = (hat * weights.gain2[...] + weights.bias2[...]).astype(BF16)
    active = gelu_parts(nn(normed2, weights.w_up[...]))[0].astype(BF16)
    return middle + nn(active, weights.w_down[...])


def layer_back(stream_grad, normed, weights, mask, spread, dense, gated, kept, sums, out, between=None, result=None):
    between = between or (lambda *place: None)
    count, width = normed.shape
    hidden = weights.w_up.shape[1]
    branch = stream_grad.astype(BF16)
    hat2, scale2 = norm_parts(kept.middle[...])
    normed2 = (hat2 * weights.gain2[...] + weights.bias2[...]).astype(BF16)
    normed2_t = normed2.astype(F32).T.astype(BF16)
    sums.total[...] = jnp.zeros(sums.total.shape, F32)
    if result is not None:
        result[...] = jnp.zeros(result.shape, F32)

    blocks = out.up.shape[0]
    piece = hidden // blocks
    own = weights.w_query.shape[0] // blocks

    def part(c, carry):
        cols = pl.ds(pl.multiple_of(c * piece, piece), piece)
        active, slope = gelu_parts(nn(normed2, weights.w_up[:, cols]))
        if result is not None:
            result[...] += nn(active.astype(BF16), weights.w_down[cols, :])
        out.down[c, 0:piece, :] = nn(active.T.astype(BF16), branch).astype(BF16)
        upper_grad = (nt(branch, weights.w_down[cols, :]) * slope).astype(BF16)
        out.up[c, 0:width, :] = nn(normed2_t, upper_grad).astype(BF16)
        sums.total[...] += nt(upper_grad, weights.w_up[:, cols])
        between("part", c)
        return carry

    lax.fori_loop(0, blocks, part, 0)
    between("hidden")
    back, gain2_grad, bias2_grad = norm_back(hat2, scale2, weights.gain2[...], sums.total[...])
    out.small[2:3, :] = gain2_grad
    out.small[3:4, :] = bias2_grad
    middle_grad = stream_grad + back
    out.middle_grad[...] = middle_grad
    rounded = middle_grad.astype(BF16)
    gated_t = kept.gated[...].astype(F32).T.astype(BF16)
    for block in range(blocks):
        rows = slice(block * own, (block + 1) * own)
        out.w_out[block, 0:own, :] = nn(gated_t[rows], rounded).astype(BF16)
    dense[...] = nt(rounded, weights.w_out[...])
    between("out")
    gated[...] = jnp.zeros(gated.shape, F32)
    keys, values = split_keyval(kept.keyval[...])
    keys_t = keys.T.astype(BF16)
    keys = keys.astype(BF16)
    values = values.astype(BF16)
    sums.keys[...] = jnp.zeros(sums.keys.shape, F32)
    sums.values[...] = jnp.zeros(sums.values.shape, F32)
    sums.gates[...] = jnp.zeros(sums.gates.shape, F32)
    lanes = iota(sums.gates.shape, 1)

    def pair(step, carry):
        slots = [2 * step, 2 * step + 1]
        which = [spread[k] for k in slots]
        chosen = [w - lane_half((count, LANES)) for w in which]
        grads = [select_tiles(dense, c) for c in chosen]
        weighted, att_grads = [], []
        for k, w, grad in zip(slots, which, grads):
            gate = gate_column(kept.gates[...], w)
            gate_grad = jnp.sum(grad * kept.attended[k].astype(F32), axis=1, keepdims=True)
            weighted.append(jnp.where(w[:, : lanes.shape[1]] == lanes, gate * gate_grad, 0.0))
            att_grads.append((gate * grad).astype(BF16))
        sums.gates[...] += weighted[0] + weighted[1]
        queries = [kept.query[k] for k in slots]
        scores = [nt(keys, query) + mask[...] for query in queries]
        shares = [jnp.exp(score - kept.lse[k, 0:1, :]) for k, score in zip(slots, scores)]
        share_grads = [nt(values, grad) for grad in att_grads]
        sums.values[...] += nn(shares[0].astype(BF16), att_grads[0]) + nn(shares[1].astype(BF16), att_grads[1])
        score_grads = [
            (share * (grad - jnp.sum(grad * share, axis=0, keepdims=True))).astype(BF16)
            for share, grad in zip(shares, share_grads)
        ]
        sums.keys[...] += nn(score_grads[0], queries[0]) + nn(score_grads[1], queries[1])
        for c, score_grad in zip(chosen, score_grads):
            query_grad = nn(keys_t, score_grad).T * 0.125
            place_tiles(gated, c, query_grad.astype(BF16).astype(F32))
        between("slot", step)
        return carry

    lax.fori_loop(0, kept.query.shape[0] // 2, pair, 0)
    both_keys = sums.keys[...] + pltpu.roll(sums.keys[...], LANES // 2, 1)
    both_values = sums.values[...] + pltpu.roll(sums.values[...], LANES // 2, 1)
    first = iota(both_keys.shape, 1) < LANES // 2
    out.keyval[...] = jnp.where(first, both_keys, both_values).astype(BF16)
    between("keyval")
    weighted = sums.gates[...]
    logit_grad = weighted - kept.gates[...] * jnp.sum(weighted, axis=1, keepdims=True)
    logit_grad = logit_grad.astype(BF16)
    out.router[...] = tn(logit_grad, normed[...])
    query_grad = gated[...].astype(BF16)
    query_grad_t = gated[...].T.astype(BF16)
    for block in range(blocks):
        rows = slice(block * own, (block + 1) * own)
        out.w_query[block, 0:own, :] = nn(query_grad_t[rows], normed[...]).astype(BF16)
    out.normed_grad[...] = nn(query_grad, weights.w_query[...]) + nn(logit_grad, weights.w_router[...])


def add_received(received):
    total = received[0].astype(F32)
    for j in range(1, received.shape[0]):
        total = total + received[j].astype(F32)
    return total.astype(BF16)


def layer_finish(x, normed, total, gain1, w_kv, middle_grad, normed_grad, keyval_out, small):
    keyval_out[...] = nn(total.astype(F32).T.astype(BF16), normed[...]).astype(BF16)
    grad = normed_grad[...] + nt(total, w_kv)
    hat, scale = norm_parts(x)
    back, gain1_grad, bias1_grad = norm_back(hat, scale, gain1, grad)
    small[0:1, :] = gain1_grad
    small[1:2, :] = bias1_grad
    return middle_grad[...] + back


def count_chosen(picked, keep, small):
    count, experts = picked.shape
    kept = jnp.broadcast_to(own_columns(keep, count).astype(F32), (LANES, count)).T[:, :experts]
    small[4:5, 0:experts] = jnp.sum(jnp.where(picked, kept, 0.0), axis=0, keepdims=True)


class Refs:
    def __init__(self, **refs):
        self.__dict__.update(refs)


def named(names, refs):
    return Refs(**dict(zip(names, refs[: len(names)]))), refs[len(names) :]


def weights_of(layer, refs):
    weights, refs = named(WEIGHTS, refs)
    for name in ("gain1", "bias1", "gain2", "bias2"):
        setattr(weights, name, getattr(weights, name).at[pl.ds(layer, 1), :])
    return weights, refs


WEIGHTS = ("gain1", "bias1", "w_kv", "w_router", "w_query", "w_out", "gain2", "bias2", "w_up", "w_down")
KEPT = ("keyval", "gates", "query", "lse", "attended", "gated", "middle")
SUMS = ("total", "keys", "values", "gates")
OUT = ("up", "down", "w_out", "w_query", "router", "keyval", "small", "middle_grad", "normed_grad")
LATER = ("x", "normed", "received", "gain1", "w_kv", "middle_grad", "normed_grad", "small")


def pre_kernel(x, gain1, bias1, w_kv, normed, keyval_own):
    pre_layer(x[...].astype(F32), gain1[0:1, :], bias1[0:1, :], w_kv[...], normed, keyval_own)


def first_kernel(*refs):
    weights, refs = weights_of(0, refs)
    (x, normed, keyval, routes, lengths, keep, next_gain1, next_bias1, next_w_kv), refs = refs[:9], refs[9:]
    kept, refs = named(KEPT[1:], refs)
    kept.keyval = keyval
    (stream, next_normed, next_keyval, small), refs = refs[:4], refs[4:]
    mask, spread, dense, gated = refs
    fill_mask(lengths, keep, mask)
    spread_routes(routes, spread)
    middle, picked = layer_forward(
        x[...].astype(F32), normed, weights, mask, spread, dense, gated, kept
    )
    result = feed_forward(middle, weights)
    small[...] = jnp.zeros(small.shape, F32)
    count_chosen(picked, keep, small)
    stream[...] = result
    pre_layer(result, next_gain1[1:2, :], next_bias1[1:2, :], next_w_kv[...], next_normed, next_keyval)


def turn_kernel(*refs):
    weights, refs = weights_of(1, refs)
    (x, normed, keyval, routes, lengths, keep, cotangent), refs = refs[:7], refs[7:]
    (activations,), refs = refs[:1], refs[1:]
    out, refs = named(OUT, refs)
    kept, refs = named(KEPT[1:], refs)
    kept.keyval = keyval
    sums, refs = named(SUMS, refs)
    mask, spread, dense, gated = refs
    fill_mask(lengths, keep, mask)
    spread_routes(routes, spread)
    middle, picked = layer_forward(x[...], normed, weights, mask, spread, dense, gated, kept)
    activations[...] = feed_forward(middle, weights).astype(BF16)
    count = x.shape[0]
    kept_col = jnp.broadcast_to(own_columns(keep, count).astype(F32), (LANES, count)).T
    kept_col = jnp.concatenate([kept_col] * (x.shape[1] // LANES), axis=1)
    out.small[...] = jnp.zeros(out.small.shape, F32)
    count_chosen(picked, keep, out.small)
    stream_grad = cotangent[...].astype(F32) * kept_col
    layer_back(stream_grad, normed, weights, mask, spread, dense, gated, kept, sums, out)


def back_kernel(*refs):
    weights, refs = weights_of(0, refs)
    later, refs = named(LATER, refs)
    (normed, routes, lengths, keep, small), refs = refs[:5], refs[5:]
    kept, refs = named(KEPT, refs)
    (later_keyval, later_small), refs = refs[:2], refs[2:]
    out, refs = named(OUT, refs)
    sums, refs = named(SUMS, refs)
    mask, spread, dense, gated = refs
    later_small[...] = later.small[...]
    out.small[...] = small[...]
    stream_grad = layer_finish(
        later.x[...], later.normed, add_received(later.received), later.gain1[1:2, :], later.w_kv[...],
        later.middle_grad, later.normed_grad, later_keyval, later_small,
    )
    fill_mask(lengths, keep, mask)
    spread_routes(routes, spread)
    layer_back(stream_grad, normed, weights, mask, spread, dense, gated, kept, sums, out)


def end_kernel(x, normed, received, gain1, w_kv, middle_grad, normed_grad, small_in, keyval_out, small, grad):
    small[...] = small_in[...]
    grad[...] = layer_finish(
        x[...].astype(F32), normed, add_received(received), gain1[0:1, :], w_kv[...], middle_grad, normed_grad,
        keyval_out, small,
    )


def share_kernel(n, scatter, mine, everyones, send_sem, recv_sem):
    me = lax.axis_index(EXP)
    rows = everyones.shape[1]
    barrier = pltpu.get_barrier_semaphore()
    others = [lax.rem(me + step, n) for step in range(1, n)]
    for other in others:
        pl.semaphore_signal(
            barrier, inc=1, device_id={EXP: other}, device_id_type=pl.DeviceIdType.MESH
        )

    def part(owner):
        return mine.at[pl.ds(pl.multiple_of(owner * rows, rows), rows)] if scatter else mine

    pl.semaphore_wait(barrier, n - 1)
    copies = []
    for step, other in enumerate(others):
        copy = pltpu.make_async_remote_copy(
            src_ref=part(other),
            dst_ref=everyones.at[me],
            send_sem=send_sem.at[step],
            recv_sem=recv_sem.at[step],
            device_id={EXP: other},
            device_id_type=pl.DeviceIdType.MESH,
        )
        copy.start()
        copies.append(copy)
    everyones[me] = part(me)[...]
    for copy in copies:
        copy.wait()


def vmem():
    return pl.BlockSpec(memory_space=pltpu.VMEM)


def axis_sizes():
    chips = lax.axis_size("dp") // 2
    across = math.isqrt(chips)
    across = across if across * across == chips else chips
    n = lax.axis_size(EXP)
    return {"c": 2, "x": across, "y": chips // across, "z": n, "l": 2, "h": n // 2}


def place_of():
    size = axis_sizes()
    d = lax.axis_index("dp")
    z = lax.axis_index(EXP)
    at = {"c": lax.rem(d, 2), "x": lax.rem(d // 2, size["x"]), "y": d // (2 * size["x"])}
    return {**at, "z": z, "l": lax.rem(z, 2), "h": z // 2}, size


def peers_of(axis, at, size):
    out = []
    for step in range(1, size[axis]):
        where = dict(at)
        where[axis] = lax.rem(at[axis] + step, size[axis])
        if axis in "lh":
            where["z"] = where["h"] * 2 + where["l"]
        out.append((where[axis], {EXP: where["z"], "dp": (where["y"] * size["x"] + where["x"]) * 2 + where["c"]}))
    return out


def greet(axes, at, size):
    barrier = pltpu.get_barrier_semaphore()
    total = 0
    for axis in axes:
        for _, device in peers_of(axis, at, size):
            pl.semaphore_signal(barrier, inc=1, device_id=device, device_id_type=pl.DeviceIdType.MESH)
            total += 1
    pl.semaphore_wait(barrier, total)


class Chunk:
    def __init__(self, array, first, rows, order, kind, result, layer, held_here):
        self.array, self.first, self.rows, self.order = array, first, rows, order
        self.kind, self.result, self.layer, self.held_here = kind, result, layer, held_here

    def shapes(self, blocks, width, size):
        own = (blocks, self.rows // size[self.order[0]], width)
        z, rows = blocks, self.rows
        got = []
        for axis in self.order:
            if axis in "zlh":
                z = z // size[axis]
            else:
                rows = rows // size[axis]
            got.append((size[axis] - 1, z, rows, width))
        return ([] if self.held_here else [own]) + got


class Sums:
    def __init__(self, chunks, sources, results, scratch, sems):
        self.chunks, self.sources, self.results = chunks, sources, results
        self.send_sem, self.recv_sem, self.own_sem = sems
        self.first_down, self.first_up, _ = arrivals(chunks, axis_sizes())
        self.at, self.size = place_of()
        self.own, self.base, self.got = [], [], []
        scratch = list(scratch)
        for chunk in chunks:
            part = chunk.rows // self.size[chunk.order[0]]
            if chunk.held_here:
                self.own.append(sources[chunk.array])
                self.base.append(chunk.first + self.at[chunk.order[0]] * part)
            else:
                self.own.append(scratch.pop(0))
                self.base.append(0)
            self.got.append([scratch.pop(0) for _ in chunk.order])

    def region(self, i, stages):
        chunk = self.chunks[i]
        first, rows, z = 0, chunk.rows, None
        for k, axis in enumerate(chunk.order[:stages]):
            if axis in "zlh":
                z = axis if axis == "l" else self.at["z"]
            else:
                rows = rows // self.size[axis]
                if k > 0:
                    first = first + self.at[axis] * rows
        return z, first, rows

    def copy_to(self, source, target, send, recv, device):
        copy = pltpu.make_async_remote_copy(
            src_ref=source, dst_ref=target, send_sem=send, recv_sem=recv, device_id=device,
            device_id_type=pl.DeviceIdType.MESH,
        )
        return copy

    def send_down(self, i, s):
        for copy in self.down_copies(i, s):
            copy.start()

    def down_copies(self, i, s):
        chunk, axis = self.chunks[i], self.chunks[i].order[s]
        copies = []
        z, first, rows = self.region(i, s)
        part = rows if axis in "zlh" else rows // self.size[axis]
        number = 0
        for step, (place, device) in enumerate(peers_of(axis, self.at, self.size)):
            start = self.base[i] + first
            blocks, into = [slice(None) if z is None else pl.ds(z, 1)], [self.got[i][s].at[step]]
            if s == 0:
                start = chunk.first + place * part
            elif axis == "z":
                blocks = [pl.ds(place, 1)]
            elif axis == "h":
                blocks = [pl.ds(place * 2 + self.at["l"], 1)]
            elif axis == "l":
                halves = range(self.size["h"])
                blocks = [pl.ds(2 * half + place, 1) for half in halves]
                into = [self.got[i][s].at[step, pl.ds(half, 1)] for half in halves]
            else:
                start = start + place * part
            source = self.sources[chunk.array] if s == 0 else self.own[i]
            for block, there in zip(blocks, into):
                piece = source.at[block, pl.ds(pl.multiple_of(start, 16), part), :]
                recv = self.recv_sem.at[self.first_down[i][s] + number]
                copies.append(self.copy_to(piece, there, self.send_sem.at[i, number], recv, device))
                number += 1
        if s == 0 and not chunk.held_here:
            start = pl.multiple_of(chunk.first + self.at[axis] * part, 16)
            load = pltpu.make_async_copy(
                self.sources[chunk.array].at[:, pl.ds(start, part), :], self.own[i], self.own_sem.at[i]
            )
            copies.append(load)
        return copies

    def add_up(self, i, s):
        chunk, axis = self.chunks[i], self.chunks[i].order[s]
        for copy in self.down_copies(i, s):
            copy.wait()
        z, first, rows = self.region(i, s + 1)
        blocks = self.got[i][s].shape[1]
        piece = math.gcd(rows, 64)
        own, got = self.own[i], self.got[i][s]

        def one(t, carry):
            block, row = t // (rows // piece), lax.rem(t, rows // piece) * piece
            where = pl.ds(pl.multiple_of(self.base[i] + first + row, 16), piece)
            arrived = pl.ds(pl.multiple_of(row, 16), piece)
            held = block if z is None else 2 * block + self.at["l"] if axis == "l" else z
            total = own[held, where, :].astype(F32)
            for step in range(self.size[axis] - 1):
                total = total + got[step, block, arrived, :].astype(F32)
            own[held, where, :] = total.astype(BF16)
            return carry

        lax.fori_loop(0, blocks * (rows // piece), one, 0)

    def targets(self, i, stages):
        chunk = self.chunks[i]
        z, first, rows = self.region(i, stages)
        start = chunk.first + self.at[chunk.order[0]] * (chunk.rows // self.size[chunk.order[0]]) + first
        where = pl.ds(pl.multiple_of(start, 16), rows)
        result = self.results[chunk.result].at[chunk.layer]
        width = self.own[i].shape[2]
        if chunk.kind == OWN:
            return [result.at[where, :]]
        if z is None:
            return [result.at[where, :] if chunk.kind == WIDE else result.at[:, where, :]]
        blocks = [2 * half + self.at["l"] for half in range(self.size["h"])] if isinstance(z, str) else [z]
        if chunk.kind == STACK:
            return [result.at[block, where, :] for block in blocks]
        return [result.at[where, pl.ds(pl.multiple_of(block * width, width), width)] for block in blocks]

    def send_up(self, i, s):
        for copy in self.up_copies(i, s):
            copy.start()

    def ups(self, i):
        chunk = self.chunks[i]
        return [s for s in reversed(range(len(chunk.order))) if chunk.kind != OWN or chunk.order[s] not in "zlh"]

    def up_copies(self, i, s):
        chunk, axis = self.chunks[i], self.chunks[i].order[s]
        targets = self.targets(i, s + 1)
        copies = []
        sources = targets
        if s == self.ups(i)[0]:
            z, first, rows = self.region(i, len(chunk.order))
            where = pl.ds(pl.multiple_of(self.base[i] + first, 16), rows)
            sources = [self.own[i].at[z, where, :]]
            copies.append(pltpu.make_async_copy(sources[0], targets[0], self.own_sem.at[i]))
        number = 0
        for _, device in peers_of(axis, self.at, self.size):
            for source, target in zip(sources, targets):
                recv = self.recv_sem.at[self.first_up[i][s] + number]
                copies.append(self.copy_to(source, target, self.send_sem.at[i, number], recv, device))
                number += 1
        return copies

    def stages(self, i):
        return len(self.chunks[i].order) + len(self.ups(i))

    def advance(self, i, stage):
        depth, ups = len(self.chunks[i].order), self.ups(i)
        if stage < depth:
            self.add_up(i, stage)
            if stage + 1 < depth:
                self.send_down(i, stage + 1)
            else:
                self.send_up(i, ups[0])
        else:
            for copy in self.up_copies(i, ups[stage - depth]):
                copy.wait()
            if stage - depth + 1 < len(ups):
                self.send_up(i, ups[stage - depth + 1])


class SmallSum:
    def __init__(self, array, result, got, send, recv):
        self.array, self.result, self.got, self.send, self.recv = array, result, got, send, recv
        self.at, self.size = place_of()

    def start(self, s):
        axis = CXYZ[s]
        source = self.array if s == 0 else self.result
        self.copies = []
        for step, (_, device) in enumerate(peers_of(axis, self.at, self.size)):
            copy = pltpu.make_async_remote_copy(
                src_ref=source, dst_ref=self.got[s].at[self.at[axis]], send_sem=self.send.at[step],
                recv_sem=self.recv.at[s, step], device_id=device, device_id_type=pl.DeviceIdType.MESH,
            )
            copy.start()
            self.copies.append(copy)
        self.got[s][self.at[axis]] = source[...]

    def advance(self, s):
        for copy in self.copies:
            copy.wait()
        total = self.got[s][0]
        for j in range(1, self.size[CXYZ[s]]):
            total = total + self.got[s][j]
        self.result[...] = total
        if s < 3:
            self.start(s + 1)


def arrivals(chunks, size):
    down, up, total = [], [], 0
    for chunk in chunks:
        for firsts in (down, up):
            firsts.append([])
            for axis in chunk.order:
                firsts[-1].append(total)
                if firsts is down or chunk.kind != OWN or axis not in "zlh":
                    total += arriving(axis, size)
    return down, up, total


def arriving(axis, size):
    return (size[axis] - 1) * (size["h"] if axis == "l" else 1)


def sum_scratch(chunks, shapes, size):
    scratch = []
    for chunk in chunks:
        blocks, _, width = shapes[chunk.array]
        scratch += [pltpu.VMEM(shape, BF16) for shape in chunk.shapes(blocks, width, size)]
    most = max(arriving(axis, size) for chunk in chunks for axis in chunk.order)
    sems = [(len(chunks), most), (arrivals(chunks, size)[2],), (len(chunks),)]
    return scratch, [pltpu.SemaphoreType.DMA(shape) for shape in sems]


def small_scratch(shape, size):
    most = max(size.values()) - 1
    sems = [pltpu.SemaphoreType.DMA((most,)), pltpu.SemaphoreType.DMA((4, most))]
    return [pltpu.VMEM((size[axis],) + shape, F32) for axis in CXYZ] + sems


def reduce_kernel(chunks, starts, counts, *refs):
    sources, refs = refs[: counts[0]], refs[counts[0] :]
    small_in, refs = refs[0], refs[1:]
    results, refs = refs[: counts[1]], refs[counts[1] :]
    small_out, refs = refs[0], refs[1:]
    scratch, sems, refs = refs[: counts[2]], refs[counts[2] : counts[2] + 3], refs[counts[2] + 3 :]
    small = SmallSum(small_in, small_out, refs[:4], refs[4], refs[5])
    sums = Sums(chunks, sources, results, scratch, sems)
    greet(CXYZ, sums.at, sums.size)
    ahead = AHEAD
    for i, start in enumerate(starts):
        if start < ahead:
            sums.send_down(i, 0)
    small.start(0)
    for t in range(max(start + sums.stages(i) for i, start in enumerate(starts))):
        order = range(len(chunks))
        for i in (reversed(order) if NEWEST else order):
            if 0 <= t - starts[i] < sums.stages(i):
                sums.advance(i, t - starts[i])
        for i, start in enumerate(starts):
            if start == t + ahead:
                sums.send_down(i, 0)
        if t < 4:
            small.advance(t)


AHEAD = 2
NEWEST = False


def pieces(rows, unit):
    units = rows // unit
    if units < 2 or not HALVES:
        return [(0, rows)]
    return [(0, -(-units // 2) * unit), (-(-units // 2) * unit, units // 2 * unit)]


HALVES = False


def sum_plan(n, up_rows, down_rows, own_rows, dp, tail_rows):
    unit = 16 * dp
    chunks, starts = [], []

    def pad(rows):
        return -(-rows // unit) * unit

    def add(pair, rows_pair):
        cuts = [pieces(pad(rows), unit) for rows in rows_pair]
        for k in range(max(len(cut) for cut in cuts)):
            start = starts[-1] + 1 if starts else 0
            for (array, kind, result, layer, order), cut in zip(pair, cuts):
                if k < len(cut):
                    chunks.append(Chunk(array, cut[k][0], cut[k][1], order, kind, result, layer, False))
                    starts.append(start)

    add([(0, WIDE, 0, 1, CXYZ), (1, STACK, 1, 1, CYXZ)], (up_rows, down_rows))
    add([(4, WIDE, 0, 0, CXYZ), (5, STACK, 1, 0, CYXZ)], (up_rows, down_rows))
    add([(2, OWN, 2, 1, CXYZ), (3, OWN, 3, 1, CYXZ)], (own_rows, own_rows))
    add([(6, OWN, 2, 0, CXYZ), (7, OWN, 3, 0, CYXZ)], (own_rows, own_rows))
    chunks.append(Chunk(8, 0, tail_rows, CXYZ, STACK, 4, 0, False))
    starts.append(0)
    return chunks, starts


def reduce_all(arrays, chunks, starts, result_shapes, small, sizes, collective_id):
    scratch, sems = sum_scratch(chunks, [array.shape for array in arrays], sizes)
    counts = (len(arrays), len(result_shapes), len(scratch))
    anywhere = pl.BlockSpec(memory_space=pl.ANY)
    return pl.pallas_call(
        partial(reduce_kernel, chunks, starts, counts),
        out_shape=[jax.ShapeDtypeStruct(shape, BF16) for shape in result_shapes] + [jax.ShapeDtypeStruct(small.shape, F32)],
        in_specs=[anywhere] * len(arrays) + [vmem()],
        out_specs=[anywhere] * len(result_shapes) + [vmem()],
        scratch_shapes=scratch + sems + small_scratch(small.shape, sizes),
        compiler_params=pltpu.CompilerParams(
            collective_id=collective_id, has_side_effects=True, vmem_limit_bytes=VMEM_LIMIT
        ),
        name="sums",
    )(*arrays, small)


def layer_spec(array, layer):
    block = (None,) + array.shape[1:]
    return pl.BlockSpec(block, lambda *_: (layer,) + (0,) * (array.ndim - 1), pipeline_mode=pl.Buffered(1))


def share(mine, n, scatter, collective_id, name):
    rows = mine.shape[0] // n if scatter else mine.shape[0]
    return pl.pallas_call(
        partial(share_kernel, n, scatter),
        out_shape=jax.ShapeDtypeStruct((n, rows, mine.shape[1]), mine.dtype),
        in_specs=[vmem()],
        out_specs=vmem(),
        scratch_shapes=[pltpu.SemaphoreType.DMA((n - 1,)), pltpu.SemaphoreType.DMA((n - 1,))],
        compiler_params=pltpu.CompilerParams(collective_id=collective_id, has_side_effects=True),
        name=name,
    )(mine)


class KeyvalSum:
    def __init__(self, mine, got, send, recv):
        self.mine, self.got, self.send, self.recv = mine, got, send, recv
        self.at, self.size = place_of()

    def part(self, place):
        rows = self.got.shape[1]
        return self.mine.at[pl.ds(pl.multiple_of(place * rows, rows), rows), :]

    def start(self):
        self.copies = []
        for step, (place, device) in enumerate(peers_of("z", self.at, self.size)):
            copy = pltpu.make_async_remote_copy(
                src_ref=self.part(place), dst_ref=self.got.at[step], send_sem=self.send.at[step],
                recv_sem=self.recv.at[step], device_id=device, device_id_type=pl.DeviceIdType.MESH,
            )
            copy.start()
            self.copies.append(copy)

    def total(self):
        for copy in self.copies:
            copy.wait()
        total = self.part(self.at["z"])[...].astype(F32)
        for step in range(self.got.shape[0]):
            total = total + self.got[step].astype(F32)
        return total.astype(BF16)


class Part:
    def __init__(self, array, layer, first, rows, order):
        self.array, self.layer, self.first, self.rows, self.order = array, layer, first, rows, order


class Gather:
    def __init__(self, parts, sources, targets, send, recv, own_sem):
        self.parts, self.sources, self.targets = parts, sources, targets
        self.send, self.recv, self.own_sem = send, recv, own_sem
        self.at, self.size = place_of()
        self.firsts = gather_arrivals(parts, axis_sizes())[0]
        self.stage = [-1] * len(parts)

    def copies(self, i, s):
        part = self.parts[i]
        source, target = self.sources[part.array].at[part.layer], self.targets[2 * part.layer + part.array]
        all_rows, rows, first = source.shape[0], part.rows, part.first
        for axis in reversed(part.order[max(s, 1) :]):
            rows = rows // self.size[axis]
            first = first + self.at[axis] * rows
        here = self.at["z"]
        out = []
        if s == 0:
            start = pl.multiple_of(here * all_rows + part.first, 16)
            out.append(
                pltpu.make_async_copy(
                    source.at[pl.ds(part.first, part.rows), :], target.at[pl.ds(start, part.rows), :], self.own_sem.at[i]
                )
            )
        number = 0
        for _, device in peers_of(part.order[s], self.at, self.size):
            for other in range(1 if s == 0 else self.size["z"] - 1):
                block = here if s == 0 else lax.rem(here + 1 + other, self.size["z"])
                into = target.at[pl.ds(pl.multiple_of(block * all_rows + first, 16), rows), :]
                out.append(
                    pltpu.make_async_remote_copy(
                        src_ref=source.at[pl.ds(pl.multiple_of(first, 16), rows), :] if s == 0 else into,
                        dst_ref=into, send_sem=self.send.at[i, number],
                        recv_sem=self.recv.at[self.firsts[i][s] + number], device_id=device,
                        device_id_type=pl.DeviceIdType.MESH,
                    )
                )
                number += 1
        return out

    def move(self, i):
        s = self.stage[i]
        if s >= 0:
            for copy in self.copies(i, s):
                copy.wait()
        self.stage[i] = s + 1
        if s + 1 < len(self.parts[i].order):
            for copy in self.copies(i, s + 1):
                copy.start()


def gather_arrivals(parts, size):
    firsts, total, most = [], 0, 0
    for part in parts:
        firsts.append([])
        for axis in part.order:
            number = (size[axis] - 1) * (1 if axis == "z" else size["z"] - 1)
            firsts[-1].append(total)
            total += number
            most = max(most, number)
    return firsts, total, most


def gather_sems(parts, size):
    _, total, most = gather_arrivals(parts, size)
    return [pltpu.SemaphoreType.DMA(shape) for shape in ((len(parts), most), (total,), (len(parts),))]


def gather_kernel(parts, *refs):
    gather = Gather(parts, refs[:2], refs[2:-3], *refs[-3:])
    greet(CXYZ, gather.at, gather.size)
    for _ in range(1 + max(len(part.order) for part in parts)):
        for i, part in enumerate(parts):
            if gather.stage[i] < len(part.order):
                gather.move(i)


def gather_all(arrays, sizes, collective_id):
    layers, rows, width = arrays[0].shape
    parts = []
    for layer in range(layers):
        for array in range(2):
            left, axes = rows // 16, ""
            for axis in "cyx":
                if left % sizes[axis] == 0:
                    left, axes = left // sizes[axis], axis + axes
            parts.append(Part(array, layer, 0, rows, "z" + axes))
    return pl.pallas_call(
        partial(gather_kernel, parts),
        out_shape=[jax.ShapeDtypeStruct((sizes["z"] * rows, width), BF16) for _ in parts],
        in_specs=[pl.BlockSpec(memory_space=pl.ANY)] * 2,
        out_specs=[vmem()] * len(parts),
        scratch_shapes=gather_sems(parts, sizes),
        compiler_params=pltpu.CompilerParams(
            collective_id=collective_id, has_side_effects=True, vmem_limit_bytes=VMEM_LIMIT
        ),
        name="gather",
    )(*arrays)


class KeyvalGather:
    def __init__(self, keyval, count, send, recv):
        self.keyval, self.count, self.send, self.recv = keyval, count, send, recv
        self.at, self.size = place_of()

    def own(self):
        return self.keyval.at[pl.ds(pl.multiple_of(self.at["z"] * self.count, self.count), self.count), :]

    def copies(self):
        return [
            pltpu.make_async_remote_copy(
                src_ref=self.own(), dst_ref=self.own(), send_sem=self.send.at[step], recv_sem=self.recv.at[step],
                device_id=device, device_id_type=pl.DeviceIdType.MESH,
            )
            for step, (_, device) in enumerate(peers_of("z", self.at, self.size))
        ]

    def start(self):
        for copy in self.copies():
            copy.start()

    def wait(self):
        for copy in self.copies():
            copy.wait()


INPUTS = ("x", "cotangent", "routes", "lengths", "keep", "gain1", "bias1", "w_kv", "w_router", "gain2", "bias2")
GRADS = ("up", "down", "w_query", "w_out")


PARTS = (
    (0, 0, 0, 256, ZYXC),
    (0, 0, 256, 128, ZXYC),
    (1, 0, 0, 256, ZXYC),
    (1, 0, 256, 128, ZYXC),
    (0, 1, 0, 384, ZYXC),
    (1, 1, 0, 384, ZXYC),
)
MOVES = {
    "start0": {None: (0, 1, 3, 2)},
    "pre0": {None: (4, 0, 1, 0, 1, 3)},
    "keyval0": {None: (2, 4, 1, 3, 0, 5, 2, 1)},
    "mask0": {None: (0, 3)},
    "arrived0": {None: (4,)},
    "slot0": {2: (2,), 6: (5, 3, 2)},
    "keyval1": {None: (4, 5, 4)},
    "slot1": {2: (5,), 6: (5,)},
}
CHUNKS = (
    (0, 0, 256, CXYLH, WIDE, 0, 1),
    (0, 256, 256, CLHXY, WIDE, 0, 1),
    (1, 0, 256, CYXLH, STACK, 1, 1),
    (1, 256, 256, CLHYX, STACK, 1, 1),
    (2, 0, 384, CYLHX, OWN, 2, 1),
    (3, 0, 384, CXYLH, OWN, 3, 1),
    (4, 0, 512, CXYLH, WIDE, 0, 0),
    (5, 0, 512, CYXLH, STACK, 1, 0),
    (6, 0, 384, CXYLH, OWN, 2, 0),
    (7, 0, 384, CYXLH, OWN, 3, 0),
    (8, 0, 128, CXLHY, STACK, 4, 0),
)
SCHEDULE = {
    "hidden1": {None: (1, 2, 0)},
    "slot1": {0: (5,), 2: (1, 0), 3: (2,), 5: (3,)},
    "keyval1": {None: (0, 5)},
    "back1": {None: (4, 2, 0, 1, 3, 4)},
    "hidden0": {None: (6,)},
    "out0": {None: (7, 5)},
    "slot0": {1: (6, 3, 7), 3: (4,), 4: (0,), 5: (2,), 7: (1,)},
    "keyval0": {None: (3,)},
    "back0": {None: (9, 8, 4, 7, 6, 5, 2, 0, 3, 9, 1, 8, 6, 3, 5, 4)},
}
REST = (2, 10, 7, 10, 6, 5, 8, 0, 2, 1, 7, 9, 0, 6, 4, 5, 10, 3, 1, 7, 10, 2, 4, 0, 6, 7, 5, 8, 10, 1, 5, 6, 10, 9, 3, 2, 7, 0, 10, 8, 6, 7, 9, 1, 10, 2, 8, 3, 4, 1, 9, 6, 10, 4, 7, 9, 2, 1, 8, 0, 10, 3, 6, 8, 7, 9, 3, 10, 8, 9)


def whole_kernel(chunks, parts, counts, *refs):
    given, refs = named(INPUTS, refs)
    (queries, outs, w_up, w_down), refs = refs[:4], refs[4:]
    (activations, input_grad), refs = refs[:2], refs[2:]
    results, small_out, refs = refs[:5], refs[5], refs[6:]
    experts_in, refs = refs[:4], refs[4:]
    (up_here, down_here), refs = refs[:2], refs[2:]
    kept, normed = [], []
    for _ in range(2):
        normed.append(refs[0])
        one, refs = named(KEPT, refs[1:])
        kept.append(one)
    grads = []
    for _ in range(2):
        one, refs = named(GRADS, refs)
        grads.append(one)
    (stream, router, middle_grad, normed_grad, part1, part0, tail, small_in), refs = refs[:8], refs[8:]
    sums, refs = named(SUMS, refs)
    (mask, spread, dense, gated, got1, got0), refs = refs[:6], refs[6:]
    scratch, refs = refs[:counts], refs[counts:]
    small_got, refs = refs[:4], refs[4:]
    sems, small_sems, refs = refs[:3], refs[3:5], refs[5:]
    gather_sems, keyval_sems, load_sem = refs[:3], refs[3:11], refs[11]

    count, width = given.x.shape
    rows = small_in.shape[0] // 2
    experts = given.w_router.shape[1]
    pair = given.w_kv.shape[2]
    sources = []
    for l in (1, 0):
        sources += [getattr(grads[l], name) for name in GRADS]
    total = Sums(chunks, sources + [tail], results, scratch, sems)
    little = SmallSum(small_in, small_out, small_got, *small_sems)
    smalls = [small_in.at[0:rows, :], small_in.at[rows : 2 * rows, :]]
    gather = Gather(parts, (queries, outs), experts_in, *gather_sems)
    keyval_gather = [KeyvalGather(kept[l].keyval, count, *keyval_sems[2 * l : 2 * l + 2]) for l in range(2)]
    keyval_sum = [KeyvalSum(part0, got0, *keyval_sems[4:6]), KeyvalSum(part1, got1, *keyval_sems[6:8])]
    weights = []
    for l in range(2):
        row = pl.ds(l, 1)
        weights.append(
            Refs(
                gain1=given.gain1.at[row, :], bias1=given.bias1.at[row, :], gain2=given.gain2.at[row, :],
                bias2=given.bias2.at[row, :], w_kv=given.w_kv.at[l], w_router=given.w_router.at[l],
                w_query=experts_in[2 * l], w_out=experts_in[2 * l + 1], w_up=up_here, w_down=down_here,
            )
        )
    outputs = [
        Refs(
            up=grads[l].up, down=grads[l].down, w_out=grads[l].w_out, w_query=grads[l].w_query, router=router,
            keyval=(part0, part1)[l], small=smalls[l], middle_grad=middle_grad, normed_grad=normed_grad,
        )
        for l in range(2)
    ]

    def loads(l):
        return [
            pltpu.make_async_copy(w_up.at[l], up_here, load_sem.at[l, 0]),
            pltpu.make_async_copy(w_down.at[l], down_here, load_sem.at[l, 1]),
        ]

    def load(l):
        for copy in loads(l):
            copy.start()

    def loaded(l):
        for copy in loads(l):
            copy.wait()

    done = [-1] * len(chunks)

    def listed_moves(table, act, place, k):
        for when, listed in table.get(place, {None: ()}).items():
            if when is None:
                for i in listed:
                    act(i)
            else:
                at = when // 2 if place.startswith("slot") else when
                pl.when(k == at)(lambda listed=listed: [act(i) for i in listed] and None)

    def move(place, k=None):
        listed_moves(SCHEDULE, step, place, k)

    def fetch(place, k=None):
        listed_moves(MOVES, gather.move, place, k)

    def step(i):
        if done[i] < 0:
            total.send_down(i, 0)
        else:
            total.advance(i, done[i])
        done[i] += 1

    def pre(l, x):
        pre_layer(x, weights[l].gain1[...], weights[l].bias1[...], weights[l].w_kv[...], normed[l], keyval_gather[l].own())
        fetch("pre" + str(l))
        keyval_gather[l].start()
        fetch("keyval" + str(l))

    load(0)
    greet(CXYZ, total.at, total.size)
    fetch("start0")
    x = given.x[...].astype(F32)
    pre(0, x)
    fill_mask(given.lengths, given.keep, mask)
    fetch("mask0")
    spread_routes(given.routes.at[0], spread)
    fetch("spread0")
    small_in[...] = jnp.zeros(small_in.shape, F32)
    tail[...] = jnp.zeros(tail.shape, BF16)
    keyval_gather[0].wait()
    fetch("arrived0")

    def first_between(place, k=None):
        if place == "middle":
            loaded(0)
        fetch(place + "0", k)

    middle, picked = layer_forward(x, normed[0], weights[0], mask, spread, dense, gated, kept[0], first_between)
    result = feed_forward(middle, weights[0])
    fetch("hidden0")
    load(1)
    count_chosen(picked, given.keep, smalls[0])
    stream[...] = result
    pre(1, result)
    spread_routes(given.routes.at[1], spread)
    fetch("spread1")

    def second_between(place, k=None):
        if place == "queries":
            keyval_gather[1].wait()
        elif place == "middle":
            loaded(1)
        fetch(place + "1", k)

    _, picked = layer_forward(
        stream[...], normed[1], weights[1], mask, spread, dense, gated, kept[1], second_between
    )
    count_chosen(picked, given.keep, smalls[1])
    kept_col = jnp.broadcast_to(own_columns(given.keep, count).astype(F32), (LANES, count)).T
    kept_col = jnp.concatenate([kept_col] * (width // LANES), axis=1)

    def last_between(place, k=None):
        if place == "hidden":
            load(0)
            activations[...] = (kept[1].middle[...] + normed_grad[...]).astype(BF16)
        elif place == "keyval":
            keyval_sum[1].start()
        move(place + "1", k)

    layer_back(
        given.cotangent[...].astype(F32) * kept_col, normed[1], weights[1], mask, spread, dense, gated, kept[1],
        sums, outputs[1], last_between, normed_grad,
    )
    tail[3, 0:experts, :] = router[...].astype(BF16)
    move("back1")
    stream_grad = layer_finish(
        stream[...], normed[1], keyval_sum[1].total(), weights[1].gain1[...], weights[1].w_kv[...], middle_grad,
        normed_grad, tail.at[2, 0:pair], smalls[1],
    )
    move("finish1")
    spread_routes(given.routes.at[0], spread)
    loaded(0)

    def between(place, k=None):
        if place == "keyval":
            keyval_sum[0].start()
        move(place + "0", k)

    layer_back(
        stream_grad, normed[0], weights[0], mask, spread, dense, gated, kept[0], sums, outputs[0], between
    )
    tail[1, 0:experts, :] = router[...].astype(BF16)
    move("back0")
    input_grad[...] = layer_finish(
        given.x[...].astype(F32), normed[0], keyval_sum[0].total(), weights[0].gain1[...], weights[0].w_kv[...],
        middle_grad, normed_grad, tail.at[0, 0:pair], smalls[0],
    )
    little.start(0)
    move("finish0")
    every = len(REST) // 4
    for number, i in enumerate(REST):
        step(i)
        if number % every == every - 1 and number // every < 4:
            little.advance(number // every)


def run_whole(args, weights_out, shapes, sizes):
    specs, arrays = specs_of(args)
    queries, _, w_up, w_down = weights_out
    layers, own, width = queries.shape
    n = sizes["z"]
    count, flat, hidden = args[0][0].shape[0], n * own, w_up.shape[2]
    chunks = [
        Chunk(array, first, rows, order, kind, result, layer, True) for array, first, rows, order, kind, result, layer in CHUNKS
    ]
    parts = [Part(*part) for part in PARTS]
    scratch, sems = sum_scratch(chunks, [shapes.up, shapes.down, shapes.own, shapes.own] * 2 + [shapes.tail], sizes)
    small_shape = (16, width)
    results = [
        (layers, shapes.up[1], hidden), (layers,) + shapes.down, (layers,) + shapes.own[1:], (layers,) + shapes.own[1:],
        (1,) + shapes.tail,
    ]
    got = pltpu.VMEM((n - 1, shapes.group // n, shapes.pair), BF16)
    part = pltpu.VMEM((shapes.group, shapes.pair), BF16)
    one = pltpu.VMEM((count, width), F32)
    local = [pltpu.VMEM((flat, width), BF16)] * 4
    local += [pltpu.VMEM(w_up.shape[1:], BF16), pltpu.VMEM(w_down.shape[1:], BF16)]
    for _ in range(2):
        local += [pltpu.VMEM((count, width), BF16), part]
        local += [pltpu.VMEM(shape, dtype) for shape, dtype in shapes.kept]
    local += [pltpu.VMEM(shape, BF16) for shape in (shapes.up, shapes.down, shapes.own, shapes.own)] * 2
    local += [one, pltpu.VMEM((shapes.experts, width), F32), one, one, part, part]
    local += [pltpu.VMEM(shapes.tail, BF16), pltpu.VMEM(small_shape, F32)]
    local += [pltpu.VMEM(shape, dtype) for shape, dtype in shapes.sums]
    mask, spread, dense, gated = [pltpu.VMEM(shape, dtype) for shape, dtype in shapes.work]
    local += [mask, spread, dense, gated, got, got]
    small_refs = small_scratch(small_shape, sizes)
    anywhere = pl.BlockSpec(memory_space=pl.ANY)
    return pl.pallas_call(
        partial(whole_kernel, chunks, parts, len(scratch)),
        out_shape=[jax.ShapeDtypeStruct((count, width), BF16), jax.ShapeDtypeStruct((count, width), F32)]
        + [jax.ShapeDtypeStruct(shape, BF16) for shape in results]
        + [jax.ShapeDtypeStruct(small_shape, F32)],
        grid=(1,),
        in_specs=specs + [anywhere] * 4,
        out_specs=[vmem(), vmem()] + [anywhere] * 5 + [vmem()],
        scratch_shapes=local + scratch + small_refs[:4] + sems + small_refs[4:]
        + gather_sems(parts, sizes)
        + [pltpu.SemaphoreType.DMA((n - 1,))] * 8
        + [pltpu.SemaphoreType.DMA((2, 2))],
        compiler_params=pltpu.CompilerParams(
            collective_id=5, has_side_effects=True, vmem_limit_bytes=63 << 20
        ),
        name="both_blocks",
    )(*arrays, *weights_out)


def widen_kernel(*refs):
    up, down, query, out, result, grad, tail, small = refs[:8]
    up_out, down_out, query_out, out_out, result_out, grad_out, kv, router, gain1, bias1, gain2, bias2, counts = refs[8:]
    for source, target in ((up, up_out), (down, down_out), (query, query_out), (out, out_out), (grad, grad_out)):
        target[...] = source[...].astype(F32)
    result_out[...] = result[...]

    @pl.when(pl.program_id(0) == 0)
    def _():
        rows = small.shape[0] // 2
        for l in range(2):
            kv[l] = tail[2 * l].astype(F32).T
            router[l] = tail[2 * l + 1, 0 : router.shape[1], :].astype(F32)
            row = slice(l, l + 1)
            for i, target in enumerate((gain1, bias1, gain2, bias2)):
                target[row, :] = small[l * rows + i : l * rows + i + 1, :]
            counts[row, :] = small[l * rows + 4 : l * rows + 5, 0 : counts.shape[1]]


def widen(result, grad, up, down, query, out, tail, small, experts):
    layers, n, rows, width = down.shape
    steps = layers * n
    blocked, whole = [], []
    for array in (up, down, query, out):
        if array.ndim == 4:
            blocked.append(pl.BlockSpec((None, 1, rows, width), lambda i: (i // n, i % n, 0, 0)))
        else:
            blocked.append(pl.BlockSpec((None, array.shape[1] // n, array.shape[2]), lambda i: (i // n, i % n, 0)))
    for array in (result, grad):
        blocked.append(pl.BlockSpec((array.shape[0] // steps, array.shape[1]), lambda i: (i, 0)))
    tail = tail.reshape(tail.shape[1:])
    shapes = [(layers, width, tail.shape[1]), (layers, experts, width)] + [(layers, width)] * 4 + [(layers, experts)]

    def fixed(shape):
        return pl.BlockSpec(shape, lambda i: (0,) * len(shape))

    return pl.pallas_call(
        widen_kernel,
        out_shape=[jax.ShapeDtypeStruct(a.shape, F32) for a in (up, down, query, out)]
        + [jax.ShapeDtypeStruct(a.shape, a.dtype) for a in (result, grad)]
        + [jax.ShapeDtypeStruct(shape, F32) for shape in shapes],
        grid=(steps,),
        in_specs=blocked + [fixed(tail.shape), fixed(small.shape)],
        out_specs=blocked + [fixed(shape) for shape in shapes],
        compiler_params=pltpu.CompilerParams(vmem_limit_bytes=VMEM_LIMIT),
        name="widen",
    )(up, down, query, out, result, grad, tail, small)


def specs_of(args):
    specs, arrays = [], []
    for array, layer in args:
        arrays.append(array)
        if layer == "smem":
            specs.append(pl.BlockSpec(memory_space=pltpu.SMEM))
        elif layer is None:
            specs.append(pl.BlockSpec(array.shape, lambda *_, nd=array.ndim: (0,) * nd, pipeline_mode=pl.Buffered(1)))
        else:
            specs.append(layer_spec(array, layer))
    return specs, arrays


def call(kernel, args, outs, scratch, name):
    specs, arrays = specs_of(args)
    return pl.pallas_call(
        kernel,
        out_shape=[jax.ShapeDtypeStruct(shape, dtype) for shape, dtype in outs],
        grid=(1,),
        in_specs=specs,
        out_specs=[pl.BlockSpec(shape, lambda *_, nd=len(shape): (0,) * nd, pipeline_mode=pl.Buffered(1)) for shape, _ in outs],
        scratch_shapes=[pltpu.VMEM(shape, dtype) for shape, dtype in scratch],
        compiler_params=pltpu.CompilerParams(vmem_limit_bytes=VMEM_LIMIT),
        name=name,
    )(*arrays)


def body(
    tokens, cotangent, routes, keep, lengths, norm1_gain, norm1_bias, w_kv, w_router, w_query, w_out,
    norm2_gain, norm2_bias, w_up, w_down,
):
    n = lax.axis_size(EXP)
    dp = lax.axis_size("dp")
    layers, width, pair = w_kv.shape
    count = tokens.shape[1]
    group = routes.shape[2]
    topk = routes.shape[3]
    experts = w_router.shape[2]
    head = w_query.shape[3]
    local = w_query.shape[1]
    hidden = w_up.shape[2]
    flat = experts * head
    own = local * head
    x0 = tokens[0]
    routes_t = jnp.swapaxes(routes[:, 0], 1, 2)
    router_t = jnp.swapaxes(w_router, 1, 2)
    gain1, bias1, gain2, bias2 = norm1_gain, norm1_bias, norm2_gain, norm2_bias
    queries_t = jnp.swapaxes(w_query, 2, 3).reshape(layers, own, width)
    outs = w_out.reshape(layers, own, width)
    sizes = axis_sizes()

    def rows_of(least):
        return -(-least // (16 * dp)) * 16 * dp

    kept_shapes = [
        ((count, experts), F32), ((topk, count, LANES), BF16), ((topk, 8, count), F32),
        ((topk, count, LANES), BF16), ((count, flat), BF16), ((count, width), F32),
    ]
    work = [((group, count), F32), ((topk, count, LANES), jnp.int32), ((count, flat), F32), ((count, flat), F32)]
    sum_shapes = [((count, width), F32), ((group, pair), F32), ((group, pair), F32), ((count, experts), F32)]
    out_shapes = [
        ((n, rows_of(width), hidden // n), BF16), ((n, rows_of(hidden // n), width), BF16),
        ((n, rows_of(own), width), BF16), ((n, rows_of(own), width), BF16),
        ((experts, width), F32), ((group, pair), BF16), ((8, width), F32), ((count, width), F32), ((count, width), F32),
    ]
    if n * dp == 32 and layers == 2:
        all_shapes = Refs(
            up=out_shapes[0][0], down=out_shapes[1][0], own=out_shapes[2][0], tail=(n, rows_of(pair), width), group=group,
            pair=pair, experts=experts, kept=kept_shapes, sums=sum_shapes, work=work,
        )
        given = [
            (x0, None), (cotangent[0], None), (routes_t, None), (lengths, "smem"), (keep, None), (gain1, None),
            (bias1, None), (w_kv, None), (router_t, None), (gain2, None), (bias2, None),
        ]
        results = run_whole(given, (queries_t, outs, w_up, w_down), all_shapes, sizes)
        up, down, expert_query, expert_out, activations, input_grad, kv, router, *norms, counts = widen(*results, experts)
        expert_query = jnp.swapaxes(expert_query.reshape(layers, local, head, width), 2, 3)
        return (
            activations[None], input_grad[None], norms[0], norms[1], kv, jnp.swapaxes(router, 1, 2), expert_query,
            expert_out.reshape(layers, local, head, width), norms[2], norms[3], up, down.reshape(layers, hidden, width), counts,
        )
    else:
        gathered = gather_all((queries_t, outs), sizes, 2)
        wq, wo = gathered[0::2], gathered[1::2]
        def weights(l):
            return [(gain1, None), (bias1, None), (w_kv, l), (router_t, l), (wq[l], None), (wo[l], None), (gain2, None), (bias2, None), (w_up, l), (w_down, l)]


        normed0, keyval0 = call(
            pre_kernel, [(x0, None), (gain1, None), (bias1, None), (w_kv, 0)],
            [((count, width), BF16), ((count, pair), BF16)], [], "pre",
        )
        keyval0 = share(keyval0, n, False, 0, "share").reshape(group, pair)
        *kept0, x1, normed1, keyval1, small0 = call(
            first_kernel,
            weights(0) + [(x0, None), (normed0, None), (keyval0, None), (routes_t, 0), (lengths, "smem"), (keep, None), (gain1, None), (bias1, None), (w_kv, 1)],
            kept_shapes + [((count, width), F32), ((count, width), BF16), ((count, pair), BF16), ((8, width), F32)],
            work, "first",
        )
        keyval1 = share(keyval1, n, False, 0, "share").reshape(group, pair)
        activations, up1, down1, out1, query1, router1, part1, small1, mid1, ngrad1 = call(
            turn_kernel,
            weights(1) + [(x1, None), (normed1, None), (keyval1, None), (routes_t, 1), (lengths, "smem"), (keep, None), (cotangent[0], None)],
            [((count, width), BF16)] + out_shapes, kept_shapes + sum_shapes + work, "turn",
        )
        tail_rows = rows_of(pair)
        result_shapes = [
            (layers,) + up1.shape[1:2] + (hidden,), (layers,) + down1.shape, (layers,) + query1.shape[1:],
            (layers,) + out1.shape[1:], (1, n, tail_rows, width),
        ]
        received1 = share(part1, n, True, 1, "scatter")
        kv1, small1, up0, down0, out0, query0, router0, part0, small0, mid0, ngrad0 = call(
            back_kernel,
            weights(0) + [(x1, None), (normed1, None), (received1, None), (gain1, None), (w_kv, 1), (mid1, None), (ngrad1, None), (small1, None),
             (normed0, None), (routes_t, 0), (lengths, "smem"), (keep, None), (small0, None), (keyval0, None)] + [(v, None) for v in kept0],
            [((pair, width), BF16), ((8, width), F32)] + out_shapes, sum_shapes + work, "back",
        )
        received0 = share(part0, n, True, 1, "scatter")
        kv0, small0, input_grad = call(
            end_kernel,
            [(x0, None), (normed0, None), (received0, None), (gain1, None), (w_kv, 0), (mid0, None), (ngrad0, None), (small0, None)],
            [((pair, width), BF16), ((8, width), F32), ((count, width), F32)], [], "end",
        )
        tail = jnp.zeros((n, tail_rows, width), BF16)
        for block, rows in enumerate((kv0, router0, kv1, router1)):
            tail = tail.at[block, : rows.shape[0]].set(rows.astype(BF16))
        chunks, starts = sum_plan(n, width, hidden // n, own, dp, tail_rows)
        arrays = [up1, down1, query1, out1, up0, down0, query0, out0, tail]
        up, down, expert_query, expert_out, tail, small = reduce_all(
            arrays, chunks, starts,
            result_shapes,
            jnp.concatenate([small0, small1]), sizes, 3,
        )
    down = down[:, :, : hidden // n].reshape(layers, hidden, width).astype(F32)
    kv = jnp.swapaxes(tail[0, 0:4:2, :pair].astype(F32), 1, 2)
    router = jnp.swapaxes(tail[0, 1:4:2, :experts].astype(F32), 1, 2)
    norms = small.reshape(layers, -1, width)
    expert_query = jnp.swapaxes(expert_query[:, :own].reshape(layers, local, head, width), 2, 3).astype(F32)
    expert_out = expert_out[:, :own].reshape(layers, local, head, width).astype(F32)
    return (
        activations[None], input_grad[None], norms[:, 0], norms[:, 1], kv, router, expert_query, expert_out,
        norms[:, 2], norms[:, 3], up[:, :width].astype(F32), down, norms[:, 4, :experts],
    )


def solution(mesh):
    return jax.shard_map(
        body,
        mesh=mesh,
        in_specs=(
            P("dp", EXP, None), P("dp", EXP, None), P(None, "dp", None, None), P("dp", None), P("dp", None),
            P(), P(), P(), P(), P(None, EXP, None, None), P(None, EXP, None, None), P(), P(), P(), P(),
        ),
        out_specs=(
            P("dp", EXP, None), P("dp", EXP, None), P(), P(), P(), P(),
            P(None, EXP, None, None), P(None, EXP, None, None), P(), P(), P(), P(), P(),
        ),
        check_vma=False,
    )
```

```python
from functools import partial
import math

import jax
import jax.numpy as jnp
from jax import lax
from jax.experimental import pallas as pl
from jax.experimental.pallas import tpu as pltpu
from jax.sharding import PartitionSpec as P

F32 = jnp.float32
EXP = "exp"
CLHXY = "clhxy"
CLHYX = "clhyx"
CXYLH = "cxylh"
CXYZ = "cxyz"
CYLHX = "cylhx"
CYXLH = "cyxlh"
CYXZ = "cyxz"
ZXYC = "zxyc"
ZYXC = "zyxc"
WIDE, STACK, OWN = range(3)
BF16 = jnp.bfloat16
LANES = 128
epsilon = 1e-05
neg_big = -1e30
never = 1 << 30
gelu_c = 0.7978845608028654
gelu_a = 0.044715
VMEM_LIMIT = 56 << 20


def nn(a, b):
    return jnp.dot(a, b, preferred_element_type=F32)


def nt(a, b):
    return lax.dot_general(a, b, (((1,), (1,)), ((), ())), preferred_element_type=F32)


def tn(a, b):
    return lax.dot_general(a, b, (((0,), (0,)), ((), ())), preferred_element_type=F32)


def iota(shape, axis):
    return lax.broadcasted_iota(jnp.int32, shape, axis)


def norm_parts(values):
    center = values - jnp.mean(values, axis=-1, keepdims=True)
    spread = jnp.mean(center * center, axis=-1, keepdims=True)
    scale = lax.rsqrt(spread + epsilon)
    return center * scale, scale


def norm_back(hat, scale, gain, grad):
    scaled = grad * gain
    first = jnp.mean(scaled, axis=-1, keepdims=True)
    second = jnp.mean(scaled * hat, axis=-1, keepdims=True)
    back = scale * (scaled - first - hat * second)
    return back, jnp.sum(grad * hat, axis=0, keepdims=True), jnp.sum(grad, axis=0, keepdims=True)


def gelu_parts(v):
    inner = jnp.tanh(gelu_c * (v + gelu_a * v * v * v))
    half = 0.5 * (1.0 + inner)
    return v * half, half + 0.5 * v * (1.0 - inner * inner) * gelu_c * (1.0 + 3.0 * gelu_a * v * v)


def lane_half(shape):
    return (iota(shape, 1) >= LANES // 2).astype(jnp.int32)


def select_tiles(dense, chosen):
    out = jnp.zeros(chosen.shape, F32)
    for tile in range(dense.shape[1] // LANES):
        out = jnp.where(chosen == 2 * tile, dense[:, tile * LANES : (tile + 1) * LANES], out)
    return out


def place_tiles(dense, chosen, values):
    for tile in range(dense.shape[1] // LANES):
        where = slice(tile * LANES, (tile + 1) * LANES)
        dense[:, where] = jnp.where(chosen == 2 * tile, values, dense[:, where])


def own_columns(ref, count):
    start = lax.axis_index(EXP) * count
    return ref[:, pl.ds(pl.multiple_of(start, count), count)]


def spread_routes(routes, spread):
    topk, count, lanes = spread.shape
    own = own_columns(routes, count)
    for k in range(topk):
        spread[k] = jnp.broadcast_to(own[k : k + 1, :], (lanes, count)).T


def fill_mask(lengths, keep, mask):
    group, count = mask.shape
    start = lax.axis_index(EXP) * count
    position = start + iota((1, count), 1)
    low = jnp.zeros((1, count), jnp.int32)
    end = 0
    for s in range(lengths.shape[1] - 1):
        end = end + lengths[0, s]
        low = jnp.where(position >= end, end, low)
    kept = jnp.broadcast_to(keep[...], (LANES, group)).T
    kept = jnp.concatenate([kept] * (count // LANES), axis=1)
    key = iota((group, count), 0)
    usable = jnp.where(kept > 0, key, never)
    allowed = ((usable >= low) & (usable <= position)) | (key == position)
    mask[...] = jnp.where(allowed, 0.0, neg_big)


def split_keyval(keyval):
    both = keyval.astype(F32)
    swapped = pltpu.roll(both, LANES // 2, 1)
    first = iota(both.shape, 1) < LANES // 2
    return jnp.where(first, both, swapped), jnp.where(first, swapped, both)


def pre_layer(x, gain1, bias1, w_kv, normed, keyval_own):
    hat, _ = norm_parts(x)
    normed[...] = (hat * gain1 + bias1).astype(BF16)
    keyval_own[...] = nn(normed[...], w_kv).astype(BF16)


def make_gates(normed, w_router, spread):
    logits = nt(normed, w_router)
    experts = logits.shape[1]
    lanes = iota(logits.shape, 1)
    picked = spread[0][:, :experts] == lanes
    for k in range(1, spread.shape[0]):
        picked = picked | (spread[k][:, :experts] == lanes)
    top = jnp.max(jnp.where(picked, logits, neg_big), axis=1, keepdims=True)
    shares = jnp.where(picked, jnp.exp(jnp.minimum(logits - top, 0.0)), 0.0)
    return shares / jnp.sum(shares, axis=1, keepdims=True), picked


def gate_column(gates, spread_k):
    lanes = iota(gates.shape, 1)
    return jnp.sum(
        jnp.where(spread_k[:, : gates.shape[1]] == lanes, gates, 0.0), axis=1, keepdims=True
    )


def layer_forward(x, normed, weights, mask, spread, dense, gated, kept, between=None):
    between = between or (lambda *place: None)
    count = normed.shape[0]
    gates, picked = make_gates(normed[...], weights.w_router[...], spread)
    kept.gates[...] = gates
    dense[...] = nt(normed[...], weights.w_query[...]).astype(BF16).astype(F32) * 0.125
    gated[...] = jnp.zeros(gated.shape, F32)
    between("queries")
    keys, values = split_keyval(kept.keyval[...])
    keys = keys.astype(BF16)
    values_t = values.T.astype(BF16)

    def pair(step, carry):
        slots = [2 * step, 2 * step + 1]
        which = [spread[k] for k in slots]
        chosen = [w - lane_half((count, LANES)) for w in which]
        queries = [select_tiles(dense, c).astype(BF16) for c in chosen]
        scores = [nt(keys, query) + mask[...] for query in queries]
        tops = [jnp.max(score, axis=0, keepdims=True) for score in scores]
        shares = [jnp.exp(score - top) for score, top in zip(scores, tops)]
        totals = [jnp.sum(share, axis=0, keepdims=True) for share in shares]
        rounded = [(share * (1.0 / total)).astype(BF16) for share, total in zip(shares, totals)]
        attended = [nn(values_t, share).T.astype(BF16) for share in rounded]
        for i, k in enumerate(slots):
            kept.query[k] = queries[i]
            kept.lse[k] = jnp.broadcast_to(tops[i] + jnp.log(totals[i]), kept.lse.shape[1:])
            kept.attended[k] = attended[i]
            gate = gate_column(kept.gates[...], which[i])
            place_tiles(gated, chosen[i], gate * attended[i].astype(F32))
        between("slot", step)
        return carry

    lax.fori_loop(0, spread.shape[0] // 2, pair, 0)
    kept.gated[...] = gated[...].astype(BF16)
    between("attended")
    middle = x + nn(kept.gated[...], weights.w_out[...])
    kept.middle[...] = middle
    between("middle")
    return middle, picked


def feed_forward(middle, weights):
    hat, _ = norm_parts(middle)
    normed2 = (hat * weights.gain2[...] + weights.bias2[...]).astype(BF16)
    active = gelu_parts(nn(normed2, weights.w_up[...]))[0].astype(BF16)
    return middle + nn(active, weights.w_down[...])


def layer_back(stream_grad, normed, weights, mask, spread, dense, gated, kept, sums, out, between=None, result=None):
    between = between or (lambda *place: None)
    count, width = normed.shape
    hidden = weights.w_up.shape[1]
    branch = stream_grad.astype(BF16)
    hat2, scale2 = norm_parts(kept.middle[...])
    normed2 = (hat2 * weights.gain2[...] + weights.bias2[...]).astype(BF16)
    normed2_t = normed2.astype(F32).T.astype(BF16)
    sums.total[...] = jnp.zeros(sums.total.shape, F32)
    if result is not None:
        result[...] = jnp.zeros(result.shape, F32)

    blocks = out.up.shape[0]
    piece = hidden // blocks
    own = weights.w_query.shape[0] // blocks

    def part(c, carry):
        cols = pl.ds(pl.multiple_of(c * piece, piece), piece)
        active, slope = gelu_parts(nn(normed2, weights.w_up[:, cols]))
        if result is not None:
            result[...] += nn(active.astype(BF16), weights.w_down[cols, :])
        out.down[c, 0:piece, :] = nn(active.T.astype(BF16), branch).astype(BF16)
        upper_grad = (nt(branch, weights.w_down[cols, :]) * slope).astype(BF16)
        out.up[c, 0:width, :] = nn(normed2_t, upper_grad).astype(BF16)
        sums.total[...] += nt(upper_grad, weights.w_up[:, cols])
        between("part", c)
        return carry

    lax.fori_loop(0, blocks, part, 0)
    between("hidden")
    back, gain2_grad, bias2_grad = norm_back(hat2, scale2, weights.gain2[...], sums.total[...])
    out.small[2:3, :] = gain2_grad
    out.small[3:4, :] = bias2_grad
    middle_grad = stream_grad + back
    out.middle_grad[...] = middle_grad
    rounded = middle_grad.astype(BF16)
    gated_t = kept.gated[...].astype(F32).T.astype(BF16)
    for block in range(blocks):
        rows = slice(block * own, (block + 1) * own)
        out.w_out[block, 0:own, :] = nn(gated_t[rows], rounded).astype(BF16)
    dense[...] = nt(rounded, weights.w_out[...])
    between("out")
    gated[...] = jnp.zeros(gated.shape, F32)
    keys, values = split_keyval(kept.keyval[...])
    keys_t = keys.T.astype(BF16)
    keys = keys.astype(BF16)
    values = values.astype(BF16)
    sums.keys[...] = jnp.zeros(sums.keys.shape, F32)
    sums.values[...] = jnp.zeros(sums.values.shape, F32)
    sums.gates[...] = jnp.zeros(sums.gates.shape, F32)
    lanes = iota(sums.gates.shape, 1)

    def pair(step, carry):
        slots = [2 * step, 2 * step + 1]
        which = [spread[k] for k in slots]
        chosen = [w - lane_half((count, LANES)) for w in which]
        grads = [select_tiles(dense, c) for c in chosen]
        weighted, att_grads = [], []
        for k, w, grad in zip(slots, which, grads):
            gate = gate_column(kept.gates[...], w)
            gate_grad = jnp.sum(grad * kept.attended[k].astype(F32), axis=1, keepdims=True)
            weighted.append(jnp.where(w[:, : lanes.shape[1]] == lanes, gate * gate_grad, 0.0))
            att_grads.append((gate * grad).astype(BF16))
        sums.gates[...] += weighted[0] + weighted[1]
        queries = [kept.query[k] for k in slots]
        scores = [nt(keys, query) + mask[...] for query in queries]
        shares = [jnp.exp(score - kept.lse[k, 0:1, :]) for k, score in zip(slots, scores)]
        share_grads = [nt(values, grad) for grad in att_grads]
        sums.values[...] += nn(shares[0].astype(BF16), att_grads[0]) + nn(shares[1].astype(BF16), att_grads[1])
        score_grads = [
            (share * (grad - jnp.sum(grad * share, axis=0, keepdims=True))).astype(BF16)
            for share, grad in zip(shares, share_grads)
        ]
        sums.keys[...] += nn(score_grads[0], queries[0]) + nn(score_grads[1], queries[1])
        for c, score_grad in zip(chosen, score_grads):
            query_grad = nn(keys_t, score_grad).T * 0.125
            place_tiles(gated, c, query_grad.astype(BF16).astype(F32))
        between("slot", step)
        return carry

    lax.fori_loop(0, kept.query.shape[0] // 2, pair, 0)
    both_keys = sums.keys[...] + pltpu.roll(sums.keys[...], LANES // 2, 1)
    both_values = sums.values[...] + pltpu.roll(sums.values[...], LANES // 2, 1)
    first = iota(both_keys.shape, 1) < LANES // 2
    out.keyval[...] = jnp.where(first, both_keys, both_values).astype(BF16)
    between("keyval")
    weighted = sums.gates[...]
    logit_grad = weighted - kept.gates[...] * jnp.sum(weighted, axis=1, keepdims=True)
    logit_grad = logit_grad.astype(BF16)
    out.router[...] = tn(logit_grad, normed[...])
    query_grad = gated[...].astype(BF16)
    query_grad_t = gated[...].T.astype(BF16)
    for block in range(blocks):
        rows = slice(block * own, (block + 1) * own)
        out.w_query[block, 0:own, :] = nn(query_grad_t[rows], normed[...]).astype(BF16)
    out.normed_grad[...] = nn(query_grad, weights.w_query[...]) + nn(logit_grad, weights.w_router[...])


def add_received(received):
    total = received[0].astype(F32)
    for j in range(1, received.shape[0]):
        total = total + received[j].astype(F32)
    return total.astype(BF16)


def layer_finish(x, normed, total, gain1, w_kv, middle_grad, normed_grad, keyval_out, small):
    keyval_out[...] = nn(total.astype(F32).T.astype(BF16), normed[...]).astype(BF16)
    grad = normed_grad[...] + nt(total, w_kv)
    hat, scale = norm_parts(x)
    back, gain1_grad, bias1_grad = norm_back(hat, scale, gain1, grad)
    small[0:1, :] = gain1_grad
    small[1:2, :] = bias1_grad
    return middle_grad[...] + back


def count_chosen(picked, keep, small):
    count, experts = picked.shape
    kept = jnp.broadcast_to(own_columns(keep, count).astype(F32), (LANES, count)).T[:, :experts]
    small[4:5, 0:experts] = jnp.sum(jnp.where(picked, kept, 0.0), axis=0, keepdims=True)


class Refs:
    def __init__(self, **refs):
        self.__dict__.update(refs)


def named(names, refs):
    return Refs(**dict(zip(names, refs[: len(names)]))), refs[len(names) :]


def weights_of(layer, refs):
    weights, refs = named(WEIGHTS, refs)
    for name in ("gain1", "bias1", "gain2", "bias2"):
        setattr(weights, name, getattr(weights, name).at[pl.ds(layer, 1), :])
    return weights, refs


WEIGHTS = ("gain1", "bias1", "w_kv", "w_router", "w_query", "w_out", "gain2", "bias2", "w_up", "w_down")
KEPT = ("keyval", "gates", "query", "lse", "attended", "gated", "middle")
SUMS = ("total", "keys", "values", "gates")
OUT = ("up", "down", "w_out", "w_query", "router", "keyval", "small", "middle_grad", "normed_grad")
LATER = ("x", "normed", "received", "gain1", "w_kv", "middle_grad", "normed_grad", "small")


def pre_kernel(x, gain1, bias1, w_kv, normed, keyval_own):
    pre_layer(x[...].astype(F32), gain1[0:1, :], bias1[0:1, :], w_kv[...], normed, keyval_own)


def first_kernel(*refs):
    weights, refs = weights_of(0, refs)
    (x, normed, keyval, routes, lengths, keep, next_gain1, next_bias1, next_w_kv), refs = refs[:9], refs[9:]
    kept, refs = named(KEPT[1:], refs)
    kept.keyval = keyval
    (stream, next_normed, next_keyval, small), refs = refs[:4], refs[4:]
    mask, spread, dense, gated = refs
    fill_mask(lengths, keep, mask)
    spread_routes(routes, spread)
    middle, picked = layer_forward(
        x[...].astype(F32), normed, weights, mask, spread, dense, gated, kept
    )
    result = feed_forward(middle, weights)
    small[...] = jnp.zeros(small.shape, F32)
    count_chosen(picked, keep, small)
    stream[...] = result
    pre_layer(result, next_gain1[1:2, :], next_bias1[1:2, :], next_w_kv[...], next_normed, next_keyval)


def turn_kernel(*refs):
    weights, refs = weights_of(1, refs)
    (x, normed, keyval, routes, lengths, keep, cotangent), refs = refs[:7], refs[7:]
    (activations,), refs = refs[:1], refs[1:]
    out, refs = named(OUT, refs)
    kept, refs = named(KEPT[1:], refs)
    kept.keyval = keyval
    sums, refs = named(SUMS, refs)
    mask, spread, dense, gated = refs
    fill_mask(lengths, keep, mask)
    spread_routes(routes, spread)
    middle, picked = layer_forward(x[...], normed, weights, mask, spread, dense, gated, kept)
    activations[...] = feed_forward(middle, weights).astype(BF16)
    count = x.shape[0]
    kept_col = jnp.broadcast_to(own_columns(keep, count).astype(F32), (LANES, count)).T
    kept_col = jnp.concatenate([kept_col] * (x.shape[1] // LANES), axis=1)
    out.small[...] = jnp.zeros(out.small.shape, F32)
    count_chosen(picked, keep, out.small)
    stream_grad = cotangent[...].astype(F32) * kept_col
    layer_back(stream_grad, normed, weights, mask, spread, dense, gated, kept, sums, out)


def back_kernel(*refs):
    weights, refs = weights_of(0, refs)
    later, refs = named(LATER, refs)
    (normed, routes, lengths, keep, small), refs = refs[:5], refs[5:]
    kept, refs = named(KEPT, refs)
    (later_keyval, later_small), refs = refs[:2], refs[2:]
    out, refs = named(OUT, refs)
    sums, refs = named(SUMS, refs)
    mask, spread, dense, gated = refs
    later_small[...] = later.small[...]
    out.small[...] = small[...]
    stream_grad = layer_finish(
        later.x[...], later.normed, add_received(later.received), later.gain1[1:2, :], later.w_kv[...],
        later.middle_grad, later.normed_grad, later_keyval, later_small,
    )
    fill_mask(lengths, keep, mask)
    spread_routes(routes, spread)
    layer_back(stream_grad, normed, weights, mask, spread, dense, gated, kept, sums, out)


def end_kernel(x, normed, received, gain1, w_kv, middle_grad, normed_grad, small_in, keyval_out, small, grad):
    small[...] = small_in[...]
    grad[...] = layer_finish(
        x[...].astype(F32), normed, add_received(received), gain1[0:1, :], w_kv[...], middle_grad, normed_grad,
        keyval_out, small,
    )


def share_kernel(n, scatter, mine, everyones, send_sem, recv_sem):
    me = lax.axis_index(EXP)
    rows = everyones.shape[1]
    barrier = pltpu.get_barrier_semaphore()
    others = [lax.rem(me + step, n) for step in range(1, n)]
    for other in others:
        pl.semaphore_signal(
            barrier, inc=1, device_id={EXP: other}, device_id_type=pl.DeviceIdType.MESH
        )

    def part(owner):
        return mine.at[pl.ds(pl.multiple_of(owner * rows, rows), rows)] if scatter else mine

    pl.semaphore_wait(barrier, n - 1)
    copies = []
    for step, other in enumerate(others):
        copy = pltpu.make_async_remote_copy(
            src_ref=part(other),
            dst_ref=everyones.at[me],
            send_sem=send_sem.at[step],
            recv_sem=recv_sem.at[step],
            device_id={EXP: other},
            device_id_type=pl.DeviceIdType.MESH,
        )
        copy.start()
        copies.append(copy)
    everyones[me] = part(me)[...]
    for copy in copies:
        copy.wait()


def vmem():
    return pl.BlockSpec(memory_space=pltpu.VMEM)


def axis_sizes():
    chips = lax.axis_size("dp") // 2
    across = math.isqrt(chips)
    across = across if across * across == chips else chips
    n = lax.axis_size(EXP)
    return {"c": 2, "x": across, "y": chips // across, "z": n, "l": 2, "h": n // 2}


def place_of():
    size = axis_sizes()
    d = lax.axis_index("dp")
    z = lax.axis_index(EXP)
    at = {"c": lax.rem(d, 2), "x": lax.rem(d // 2, size["x"]), "y": d // (2 * size["x"])}
    return {**at, "z": z, "l": lax.rem(z, 2), "h": z // 2}, size


def peers_of(axis, at, size):
    out = []
    for step in range(1, size[axis]):
        where = dict(at)
        where[axis] = lax.rem(at[axis] + step, size[axis])
        if axis in "lh":
            where["z"] = where["h"] * 2 + where["l"]
        out.append((where[axis], {EXP: where["z"], "dp": (where["y"] * size["x"] + where["x"]) * 2 + where["c"]}))
    return out


def greet(axes, at, size):
    barrier = pltpu.get_barrier_semaphore()
    total = 0
    for axis in axes:
        for _, device in peers_of(axis, at, size):
            pl.semaphore_signal(barrier, inc=1, device_id=device, device_id_type=pl.DeviceIdType.MESH)
            total += 1
    pl.semaphore_wait(barrier, total)


class Chunk:
    def __init__(self, array, first, rows, order, kind, result, layer, held_here):
        self.array, self.first, self.rows, self.order = array, first, rows, order
        self.kind, self.result, self.layer, self.held_here = kind, result, layer, held_here

    def shapes(self, blocks, width, size):
        own = (blocks, self.rows // size[self.order[0]], width)
        z, rows = blocks, self.rows
        got = []
        for axis in self.order:
            if axis in "zlh":
                z = z // size[axis]
            else:
                rows = rows // size[axis]
            got.append((size[axis] - 1, z, rows, width))
        return ([] if self.held_here else [own]) + got


class Sums:
    def __init__(self, chunks, sources, results, scratch, sems):
        self.chunks, self.sources, self.results = chunks, sources, results
        self.send_sem, self.recv_sem, self.own_sem = sems
        self.first_down, self.first_up, _ = arrivals(chunks, axis_sizes())
        self.at, self.size = place_of()
        self.own, self.base, self.got = [], [], []
        scratch = list(scratch)
        for chunk in chunks:
            part = chunk.rows // self.size[chunk.order[0]]
            if chunk.held_here:
                self.own.append(sources[chunk.array])
                self.base.append(chunk.first + self.at[chunk.order[0]] * part)
            else:
                self.own.append(scratch.pop(0))
                self.base.append(0)
            self.got.append([scratch.pop(0) for _ in chunk.order])

    def region(self, i, stages):
        chunk = self.chunks[i]
        first, rows, z = 0, chunk.rows, None
        for k, axis in enumerate(chunk.order[:stages]):
            if axis in "zlh":
                z = axis if axis == "l" else self.at["z"]
            else:
                rows = rows // self.size[axis]
                if k > 0:
                    first = first + self.at[axis] * rows
        return z, first, rows

    def copy_to(self, source, target, send, recv, device):
        copy = pltpu.make_async_remote_copy(
            src_ref=source, dst_ref=target, send_sem=send, recv_sem=recv, device_id=device,
            device_id_type=pl.DeviceIdType.MESH,
        )
        return copy

    def send_down(self, i, s):
        for copy in self.down_copies(i, s):
            copy.start()

    def down_copies(self, i, s):
        chunk, axis = self.chunks[i], self.chunks[i].order[s]
        copies = []
        z, first, rows = self.region(i, s)
        part = rows if axis in "zlh" else rows // self.size[axis]
        number = 0
        for step, (place, device) in enumerate(peers_of(axis, self.at, self.size)):
            start = self.base[i] + first
            blocks, into = [slice(None) if z is None else pl.ds(z, 1)], [self.got[i][s].at[step]]
            if s == 0:
                start = chunk.first + place * part
            elif axis == "z":
                blocks = [pl.ds(place, 1)]
            elif axis == "h":
                blocks = [pl.ds(place * 2 + self.at["l"], 1)]
            elif axis == "l":
                halves = range(self.size["h"])
                blocks = [pl.ds(2 * half + place, 1) for half in halves]
                into = [self.got[i][s].at[step, pl.ds(half, 1)] for half in halves]
            else:
                start = start + place * part
            source = self.sources[chunk.array] if s == 0 else self.own[i]
            for block, there in zip(blocks, into):
                piece = source.at[block, pl.ds(pl.multiple_of(start, 16), part), :]
                recv = self.recv_sem.at[self.first_down[i][s] + number]
                copies.append(self.copy_to(piece, there, self.send_sem.at[i, number], recv, device))
                number += 1
        if s == 0 and not chunk.held_here:
            start = pl.multiple_of(chunk.first + self.at[axis] * part, 16)
            load = pltpu.make_async_copy(
                self.sources[chunk.array].at[:, pl.ds(start, part), :], self.own[i], self.own_sem.at[i]
            )
            copies.append(load)
        return copies

    def add_up(self, i, s):
        chunk, axis = self.chunks[i], self.chunks[i].order[s]
        for copy in self.down_copies(i, s):
            copy.wait()
        z, first, rows = self.region(i, s + 1)
        blocks = self.got[i][s].shape[1]
        piece = math.gcd(rows, 64)
        own, got = self.own[i], self.got[i][s]

        def one(t, carry):
            block, row = t // (rows // piece), lax.rem(t, rows // piece) * piece
            where = pl.ds(pl.multiple_of(self.base[i] + first + row, 16), piece)
            arrived = pl.ds(pl.multiple_of(row, 16), piece)
            held = block if z is None else 2 * block + self.at["l"] if axis == "l" else z
            total = own[held, where, :].astype(F32)
            for step in range(self.size[axis] - 1):
                total = total + got[step, block, arrived, :].astype(F32)
            own[held, where, :] = total.astype(BF16)
            return carry

        lax.fori_loop(0, blocks * (rows // piece), one, 0)

    def targets(self, i, stages):
        chunk = self.chunks[i]
        z, first, rows = self.region(i, stages)
        start = chunk.first + self.at[chunk.order[0]] * (chunk.rows // self.size[chunk.order[0]]) + first
        where = pl.ds(pl.multiple_of(start, 16), rows)
        result = self.results[chunk.result].at[chunk.layer]
        width = self.own[i].shape[2]
        if chunk.kind == OWN:
            return [result.at[where, :]]
        if z is None:
            return [result.at[where, :] if chunk.kind == WIDE else result.at[:, where, :]]
        blocks = [2 * half + self.at["l"] for half in range(self.size["h"])] if isinstance(z, str) else [z]
        if chunk.kind == STACK:
            return [result.at[block, where, :] for block in blocks]
        return [result.at[where, pl.ds(pl.multiple_of(block * width, width), width)] for block in blocks]

    def send_up(self, i, s):
        for copy in self.up_copies(i, s):
            copy.start()

    def ups(self, i):
        chunk = self.chunks[i]
        return [s for s in reversed(range(len(chunk.order))) if chunk.kind != OWN or chunk.order[s] not in "zlh"]

    def up_copies(self, i, s):
        chunk, axis = self.chunks[i], self.chunks[i].order[s]
        targets = self.targets(i, s + 1)
        copies = []
        sources = targets
        if s == self.ups(i)[0]:
            z, first, rows = self.region(i, len(chunk.order))
            where = pl.ds(pl.multiple_of(self.base[i] + first, 16), rows)
            sources = [self.own[i].at[z, where, :]]
            copies.append(pltpu.make_async_copy(sources[0], targets[0], self.own_sem.at[i]))
        number = 0
        for _, device in peers_of(axis, self.at, self.size):
            for source, target in zip(sources, targets):
                recv = self.recv_sem.at[self.first_up[i][s] + number]
                copies.append(self.copy_to(source, target, self.send_sem.at[i, number], recv, device))
                number += 1
        return copies

    def stages(self, i):
        return len(self.chunks[i].order) + len(self.ups(i))

    def advance(self, i, stage):
        depth, ups = len(self.chunks[i].order), self.ups(i)
        if stage < depth:
            self.add_up(i, stage)
            if stage + 1 < depth:
                self.send_down(i, stage + 1)
            else:
                self.send_up(i, ups[0])
        else:
            for copy in self.up_copies(i, ups[stage - depth]):
                copy.wait()
            if stage - depth + 1 < len(ups):
                self.send_up(i, ups[stage - depth + 1])


class SmallSum:
    def __init__(self, array, result, got, send, recv):
        self.array, self.result, self.got, self.send, self.recv = array, result, got, send, recv
        self.at, self.size = place_of()

    def start(self, s):
        axis = CXYZ[s]
        source = self.array if s == 0 else self.result
        self.copies = []
        for step, (_, device) in enumerate(peers_of(axis, self.at, self.size)):
            copy = pltpu.make_async_remote_copy(
                src_ref=source, dst_ref=self.got[s].at[self.at[axis]], send_sem=self.send.at[step],
                recv_sem=self.recv.at[s, step], device_id=device, device_id_type=pl.DeviceIdType.MESH,
            )
            copy.start()
            self.copies.append(copy)
        self.got[s][self.at[axis]] = source[...]

    def advance(self, s):
        for copy in self.copies:
            copy.wait()
        total = self.got[s][0]
        for j in range(1, self.size[CXYZ[s]]):
            total = total + self.got[s][j]
        self.result[...] = total
        if s < 3:
            self.start(s + 1)


def arrivals(chunks, size):
    down, up, total = [], [], 0
    for chunk in chunks:
        for firsts in (down, up):
            firsts.append([])
            for axis in chunk.order:
                firsts[-1].append(total)
                if firsts is down or chunk.kind != OWN or axis not in "zlh":
                    total += arriving(axis, size)
    return down, up, total


def arriving(axis, size):
    return (size[axis] - 1) * (size["h"] if axis == "l" else 1)


def sum_scratch(chunks, shapes, size):
    scratch = []
    for chunk in chunks:
        blocks, _, width = shapes[chunk.array]
        scratch += [pltpu.VMEM(shape, BF16) for shape in chunk.shapes(blocks, width, size)]
    most = max(arriving(axis, size) for chunk in chunks for axis in chunk.order)
    sems = [(len(chunks), most), (arrivals(chunks, size)[2],), (len(chunks),)]
    return scratch, [pltpu.SemaphoreType.DMA(shape) for shape in sems]


def small_scratch(shape, size):
    most = max(size.values()) - 1
    sems = [pltpu.SemaphoreType.DMA((most,)), pltpu.SemaphoreType.DMA((4, most))]
    return [pltpu.VMEM((size[axis],) + shape, F32) for axis in CXYZ] + sems


def reduce_kernel(chunks, starts, counts, *refs):
    sources, refs = refs[: counts[0]], refs[counts[0] :]
    small_in, refs = refs[0], refs[1:]
    results, refs = refs[: counts[1]], refs[counts[1] :]
    small_out, refs = refs[0], refs[1:]
    scratch, sems, refs = refs[: counts[2]], refs[counts[2] : counts[2] + 3], refs[counts[2] + 3 :]
    small = SmallSum(small_in, small_out, refs[:4], refs[4], refs[5])
    sums = Sums(chunks, sources, results, scratch, sems)
    greet(CXYZ, sums.at, sums.size)
    ahead = AHEAD
    for i, start in enumerate(starts):
        if start < ahead:
            sums.send_down(i, 0)
    small.start(0)
    for t in range(max(start + sums.stages(i) for i, start in enumerate(starts))):
        order = range(len(chunks))
        for i in (reversed(order) if NEWEST else order):
            if 0 <= t - starts[i] < sums.stages(i):
                sums.advance(i, t - starts[i])
        for i, start in enumerate(starts):
            if start == t + ahead:
                sums.send_down(i, 0)
        if t < 4:
            small.advance(t)


AHEAD = 2
NEWEST = False


def pieces(rows, unit):
    units = rows // unit
    if units < 2 or not HALVES:
        return [(0, rows)]
    return [(0, -(-units // 2) * unit), (-(-units // 2) * unit, units // 2 * unit)]


HALVES = False


def sum_plan(n, up_rows, down_rows, own_rows, dp, tail_rows):
    unit = 16 * dp
    chunks, starts = [], []

    def pad(rows):
        return -(-rows // unit) * unit

    def add(pair, rows_pair):
        cuts = [pieces(pad(rows), unit) for rows in rows_pair]
        for k in range(max(len(cut) for cut in cuts)):
            start = starts[-1] + 1 if starts else 0
            for (array, kind, result, layer, order), cut in zip(pair, cuts):
                if k < len(cut):
                    chunks.append(Chunk(array, cut[k][0], cut[k][1], order, kind, result, layer, False))
                    starts.append(start)

    add([(0, WIDE, 0, 1, CXYZ), (1, STACK, 1, 1, CYXZ)], (up_rows, down_rows))
    add([(4, WIDE, 0, 0, CXYZ), (5, STACK, 1, 0, CYXZ)], (up_rows, down_rows))
    add([(2, OWN, 2, 1, CXYZ), (3, OWN, 3, 1, CYXZ)], (own_rows, own_rows))
    add([(6, OWN, 2, 0, CXYZ), (7, OWN, 3, 0, CYXZ)], (own_rows, own_rows))
    chunks.append(Chunk(8, 0, tail_rows, CXYZ, STACK, 4, 0, False))
    starts.append(0)
    return chunks, starts


def reduce_all(arrays, chunks, starts, result_shapes, small, sizes, collective_id):
    scratch, sems = sum_scratch(chunks, [array.shape for array in arrays], sizes)
    counts = (len(arrays), len(result_shapes), len(scratch))
    anywhere = pl.BlockSpec(memory_space=pl.ANY)
    return pl.pallas_call(
        partial(reduce_kernel, chunks, starts, counts),
        out_shape=[jax.ShapeDtypeStruct(shape, BF16) for shape in result_shapes] + [jax.ShapeDtypeStruct(small.shape, F32)],
        in_specs=[anywhere] * len(arrays) + [vmem()],
        out_specs=[anywhere] * len(result_shapes) + [vmem()],
        scratch_shapes=scratch + sems + small_scratch(small.shape, sizes),
        compiler_params=pltpu.CompilerParams(
            collective_id=collective_id, has_side_effects=True, vmem_limit_bytes=VMEM_LIMIT
        ),
        name="sums",
    )(*arrays, small)


def layer_spec(array, layer):
    block = (None,) + array.shape[1:]
    return pl.BlockSpec(block, lambda *_: (layer,) + (0,) * (array.ndim - 1), pipeline_mode=pl.Buffered(1))


def share(mine, n, scatter, collective_id, name):
    rows = mine.shape[0] // n if scatter else mine.shape[0]
    return pl.pallas_call(
        partial(share_kernel, n, scatter),
        out_shape=jax.ShapeDtypeStruct((n, rows, mine.shape[1]), mine.dtype),
        in_specs=[vmem()],
        out_specs=vmem(),
        scratch_shapes=[pltpu.SemaphoreType.DMA((n - 1,)), pltpu.SemaphoreType.DMA((n - 1,))],
        compiler_params=pltpu.CompilerParams(collective_id=collective_id, has_side_effects=True),
        name=name,
    )(mine)


class KeyvalSum:
    def __init__(self, mine, got, send, recv):
        self.mine, self.got, self.send, self.recv = mine, got, send, recv
        self.at, self.size = place_of()

    def part(self, place):
        rows = self.got.shape[1]
        return self.mine.at[pl.ds(pl.multiple_of(place * rows, rows), rows), :]

    def start(self):
        self.copies = []
        for step, (place, device) in enumerate(peers_of("z", self.at, self.size)):
            copy = pltpu.make_async_remote_copy(
                src_ref=self.part(place), dst_ref=self.got.at[step], send_sem=self.send.at[step],
                recv_sem=self.recv.at[step], device_id=device, device_id_type=pl.DeviceIdType.MESH,
            )
            copy.start()
            self.copies.append(copy)

    def total(self):
        for copy in self.copies:
            copy.wait()
        total = self.part(self.at["z"])[...].astype(F32)
        for step in range(self.got.shape[0]):
            total = total + self.got[step].astype(F32)
        return total.astype(BF16)


class Part:
    def __init__(self, array, layer, first, rows, order):
        self.array, self.layer, self.first, self.rows, self.order = array, layer, first, rows, order


class Gather:
    def __init__(self, parts, sources, targets, send, recv, own_sem):
        self.parts, self.sources, self.targets = parts, sources, targets
        self.send, self.recv, self.own_sem = send, recv, own_sem
        self.at, self.size = place_of()
        self.firsts = gather_arrivals(parts, axis_sizes())[0]
        self.stage = [-1] * len(parts)

    def copies(self, i, s):
        part = self.parts[i]
        source, target = self.sources[part.array].at[part.layer], self.targets[2 * part.layer + part.array]
        all_rows, rows, first = source.shape[0], part.rows, part.first
        for axis in reversed(part.order[max(s, 1) :]):
            rows = rows // self.size[axis]
            first = first + self.at[axis] * rows
        here = self.at["z"]
        out = []
        if s == 0:
            start = pl.multiple_of(here * all_rows + part.first, 16)
            out.append(
                pltpu.make_async_copy(
                    source.at[pl.ds(part.first, part.rows), :], target.at[pl.ds(start, part.rows), :], self.own_sem.at[i]
                )
            )
        number = 0
        for _, device in peers_of(part.order[s], self.at, self.size):
            for other in range(1 if s == 0 else self.size["z"] - 1):
                block = here if s == 0 else lax.rem(here + 1 + other, self.size["z"])
                into = target.at[pl.ds(pl.multiple_of(block * all_rows + first, 16), rows), :]
                out.append(
                    pltpu.make_async_remote_copy(
                        src_ref=source.at[pl.ds(pl.multiple_of(first, 16), rows), :] if s == 0 else into,
                        dst_ref=into, send_sem=self.send.at[i, number],
                        recv_sem=self.recv.at[self.firsts[i][s] + number], device_id=device,
                        device_id_type=pl.DeviceIdType.MESH,
                    )
                )
                number += 1
        return out

    def move(self, i):
        s = self.stage[i]
        if s >= 0:
            for copy in self.copies(i, s):
                copy.wait()
        self.stage[i] = s + 1
        if s + 1 < len(self.parts[i].order):
            for copy in self.copies(i, s + 1):
                copy.start()


def gather_arrivals(parts, size):
    firsts, total, most = [], 0, 0
    for part in parts:
        firsts.append([])
        for axis in part.order:
            number = (size[axis] - 1) * (1 if axis == "z" else size["z"] - 1)
            firsts[-1].append(total)
            total += number
            most = max(most, number)
    return firsts, total, most


def gather_sems(parts, size):
    _, total, most = gather_arrivals(parts, size)
    return [pltpu.SemaphoreType.DMA(shape) for shape in ((len(parts), most), (total,), (len(parts),))]


def gather_kernel(parts, *refs):
    gather = Gather(parts, refs[:2], refs[2:-3], *refs[-3:])
    greet(CXYZ, gather.at, gather.size)
    for _ in range(1 + max(len(part.order) for part in parts)):
        for i, part in enumerate(parts):
            if gather.stage[i] < len(part.order):
                gather.move(i)


def gather_all(arrays, sizes, collective_id):
    layers, rows, width = arrays[0].shape
    parts = []
    for layer in range(layers):
        for array in range(2):
            left, axes = rows // 16, ""
            for axis in "cyx":
                if left % sizes[axis] == 0:
                    left, axes = left // sizes[axis], axis + axes
            parts.append(Part(array, layer, 0, rows, "z" + axes))
    return pl.pallas_call(
        partial(gather_kernel, parts),
        out_shape=[jax.ShapeDtypeStruct((sizes["z"] * rows, width), BF16) for _ in parts],
        in_specs=[pl.BlockSpec(memory_space=pl.ANY)] * 2,
        out_specs=[vmem()] * len(parts),
        scratch_shapes=gather_sems(parts, sizes),
        compiler_params=pltpu.CompilerParams(
            collective_id=collective_id, has_side_effects=True, vmem_limit_bytes=VMEM_LIMIT
        ),
        name="gather",
    )(*arrays)


class KeyvalGather:
    def __init__(self, keyval, count, send, recv):
        self.keyval, self.count, self.send, self.recv = keyval, count, send, recv
        self.at, self.size = place_of()

    def own(self):
        return self.keyval.at[pl.ds(pl.multiple_of(self.at["z"] * self.count, self.count), self.count), :]

    def copies(self):
        return [
            pltpu.make_async_remote_copy(
                src_ref=self.own(), dst_ref=self.own(), send_sem=self.send.at[step], recv_sem=self.recv.at[step],
                device_id=device, device_id_type=pl.DeviceIdType.MESH,
            )
            for step, (_, device) in enumerate(peers_of("z", self.at, self.size))
        ]

    def start(self):
        for copy in self.copies():
            copy.start()

    def wait(self):
        for copy in self.copies():
            copy.wait()


INPUTS = ("x", "cotangent", "routes", "lengths", "keep", "gain1", "bias1", "w_kv", "w_router", "gain2", "bias2")
LARGE = ("x", "cotangent", "routes", "w_kv", "w_router")
GRADS = ("up", "down", "w_query", "w_out")


PARTS = (
    (0, 0, 0, 256, ZYXC),
    (0, 0, 256, 128, ZXYC),
    (1, 0, 0, 256, ZXYC),
    (1, 0, 256, 128, ZYXC),
    (0, 1, 0, 384, ZYXC),
    (1, 1, 0, 384, ZXYC),
)
MOVES = {
    "start0": {None: (0, 1, 3, 2)},
    "pre0": {None: (4, 0, 1, 0, 1, 3)},
    "keyval0": {None: (2, 4, 1, 3, 0, 5, 2, 1)},
    "mask0": {None: (0, 3)},
    "arrived0": {None: (4,)},
    "slot0": {2: (2,), 6: (5, 3, 2)},
    "keyval1": {None: (4, 5, 4)},
    "slot1": {2: (5,), 6: (5,)},
}
CHUNKS = (
    (0, 0, 256, CXYLH, WIDE, 0, 1),
    (0, 256, 256, CLHXY, WIDE, 0, 1),
    (1, 0, 256, CYXLH, STACK, 1, 1),
    (1, 256, 256, CLHYX, STACK, 1, 1),
    (2, 0, 384, CYLHX, OWN, 2, 1),
    (3, 0, 384, CXYLH, OWN, 3, 1),
    (4, 0, 512, CXYLH, WIDE, 0, 0),
    (5, 0, 256, CYXLH, STACK, 1, 0),
    (5, 256, 256, CYLHX, STACK, 1, 0),
    (6, 0, 384, CXYLH, OWN, 2, 0),
    (7, 0, 384, CYXLH, OWN, 3, 0),
    (8, 0, 128, CXYLH, STACK, 4, 0),
)
SCHEDULE = {
    "hidden1": {None: (1, 0)},
    "slot1": {0: (2, 1), 2: (0, 2, 5), 4: (3,)},
    "back1": {None: (4, 0, 5, 2, 3, 1, 4, 0)},
    "hidden0": {None: (6, 8, 5, 3)},
    "out0": {None: (4, 0, 1, 2, 6, 7, 8)},
    "slot0": {0: (5,), 2: (7, 3, 1, 4), 4: (8,), 6: (10,)},
    "keyval0": {None: (0,)},
    "back0": {None: (6, 9, 7, 2, 3, 10, 9, 8, 7, 6, 2, 7)},
}
REST = (8, 0, 11, 1, 3, 6, 11, 2, 9, 8, 5, 4, 7, 11, 1, 6, 2, 8, 3, 9, 0, 11, 10, 4, 7, 2, 6, 11, 0, 8, 1, 7, 5, 6, 11, 9, 10, 8, 5, 3, 11, 6, 10, 4, 1, 5, 5, 11, 2, 0, 9, 7, 8, 4, 3, 0, 2, 10, 1, 11, 6, 9, 1, 10, 7, 11, 6, 8, 3, 4, 11, 10, 9, 10, 7, 3, 9)


def whole_kernel(chunks, parts, counts, *refs):
    given, refs = named(INPUTS, refs)
    (queries, outs, w_up, w_down), refs = refs[:4], refs[4:]
    written, refs = refs[:2], refs[2:]
    results, small_out, refs = refs[:5], refs[5], refs[6:]
    experts_in, refs = refs[:4], refs[4:]
    (up_here, down_here), refs = refs[:2], refs[2:]
    kept, normed = [], []
    for _ in range(2):
        normed.append(refs[0])
        one, refs = named(KEPT, refs[1:])
        kept.append(one)
    grads = []
    for _ in range(2):
        one, refs = named(GRADS, refs)
        grads.append(one)
    (stream, router, middle_grad, normed_grad, part1, part0, tail, small_in), refs = refs[:8], refs[8:]
    sums, refs = named(SUMS, refs)
    (mask, spread, dense, gated, got1, got0), refs = refs[:6], refs[6:]
    scratch, refs = refs[:counts], refs[counts:]
    small_got, refs = refs[:4], refs[4:]
    sems, small_sems, refs = refs[:3], refs[3:5], refs[5:]
    gather_sems, keyval_sems, load_sem, refs = refs[:3], refs[3:11], refs[11], refs[12:]
    (activations, input_grad), fetched, write_sem, fetch_sem = refs[:2], refs[2:-2], refs[-2], refs[-1]
    fetching = []
    for i, (name, here) in enumerate(zip(LARGE, fetched)):
        fetching.append(pltpu.make_async_copy(getattr(given, name), here, fetch_sem.at[i]))
        setattr(given, name, here)
    writing = [
        pltpu.make_async_copy(here, there, write_sem.at[i])
        for i, (here, there) in enumerate(zip((activations, input_grad), written))
    ]

    count, width = given.x.shape
    rows = small_in.shape[0] // 2
    experts = given.w_router.shape[1]
    pair = given.w_kv.shape[2]
    sources = []
    for l in (1, 0):
        sources += [getattr(grads[l], name) for name in GRADS]
    total = Sums(chunks, sources + [tail], results, scratch, sems)
    little = SmallSum(small_in, small_out, small_got, *small_sems)
    smalls = [small_in.at[0:rows, :], small_in.at[rows : 2 * rows, :]]
    gather = Gather(parts, (queries, outs), experts_in, *gather_sems)
    keyval_gather = [KeyvalGather(kept[l].keyval, count, *keyval_sems[2 * l : 2 * l + 2]) for l in range(2)]
    keyval_sum = [KeyvalSum(part0, got0, *keyval_sems[4:6]), KeyvalSum(part1, got1, *keyval_sems[6:8])]
    weights = []
    for l in range(2):
        row = pl.ds(l, 1)
        weights.append(
            Refs(
                gain1=given.gain1.at[row, :], bias1=given.bias1.at[row, :], gain2=given.gain2.at[row, :],
                bias2=given.bias2.at[row, :], w_kv=given.w_kv.at[l], w_router=given.w_router.at[l],
                w_query=experts_in[2 * l], w_out=experts_in[2 * l + 1], w_up=up_here, w_down=down_here,
            )
        )
    outputs = [
        Refs(
            up=grads[l].up, down=grads[l].down, w_out=grads[l].w_out, w_query=grads[l].w_query, router=router,
            keyval=(part0, part1)[l], small=smalls[l], middle_grad=middle_grad, normed_grad=normed_grad,
        )
        for l in range(2)
    ]

    def loads(l):
        return [
            pltpu.make_async_copy(w_up.at[l], up_here, load_sem.at[l, 0]),
            pltpu.make_async_copy(w_down.at[l], down_here, load_sem.at[l, 1]),
        ]

    def load(l):
        for copy in loads(l):
            copy.start()

    def loaded(l):
        for copy in loads(l):
            copy.wait()

    done = [-1] * len(chunks)

    def listed_moves(table, act, place, k):
        for when, listed in table.get(place, {None: ()}).items():
            if when is None:
                for i in listed:
                    act(i)
            else:
                at = when // 2 if place.startswith("slot") else when
                pl.when(k == at)(lambda listed=listed: [act(i) for i in listed] and None)

    def move(place, k=None):
        listed_moves(SCHEDULE, step, place, k)

    def fetch(place, k=None):
        listed_moves(MOVES, gather.move, place, k)

    def step(i):
        if done[i] < 0:
            total.send_down(i, 0)
        else:
            total.advance(i, done[i])
        done[i] += 1

    def pre(l, x):
        pre_layer(x, weights[l].gain1[...], weights[l].bias1[...], weights[l].w_kv[...], normed[l], keyval_gather[l].own())
        fetch("pre" + str(l))
        keyval_gather[l].start()
        fetch("keyval" + str(l))

    for copy in fetching:
        copy.start()
    greet(CXYZ, total.at, total.size)
    fetch("start0")
    load(0)
    for copy in fetching:
        copy.wait()
    x = given.x[...].astype(F32)
    pre(0, x)
    fill_mask(given.lengths, given.keep, mask)
    fetch("mask0")
    spread_routes(given.routes.at[0], spread)
    fetch("spread0")
    small_in[...] = jnp.zeros(small_in.shape, F32)
    tail[...] = jnp.zeros(tail.shape, BF16)
    keyval_gather[0].wait()
    fetch("arrived0")

    def first_between(place, k=None):
        if place == "middle":
            loaded(0)
        fetch(place + "0", k)

    middle, picked = layer_forward(x, normed[0], weights[0], mask, spread, dense, gated, kept[0], first_between)
    result = feed_forward(middle, weights[0])
    fetch("hidden0")
    load(1)
    count_chosen(picked, given.keep, smalls[0])
    stream[...] = result
    pre(1, result)
    spread_routes(given.routes.at[1], spread)
    fetch("spread1")

    def second_between(place, k=None):
        if place == "queries":
            keyval_gather[1].wait()
        elif place == "middle":
            loaded(1)
        fetch(place + "1", k)

    _, picked = layer_forward(
        stream[...], normed[1], weights[1], mask, spread, dense, gated, kept[1], second_between
    )
    count_chosen(picked, given.keep, smalls[1])
    kept_col = jnp.broadcast_to(own_columns(given.keep, count).astype(F32), (LANES, count)).T
    kept_col = jnp.concatenate([kept_col] * (width // LANES), axis=1)

    def last_between(place, k=None):
        if place == "hidden":
            load(0)
            activations[...] = (kept[1].middle[...] + normed_grad[...]).astype(BF16)
            writing[0].start()
        elif place == "keyval":
            keyval_sum[1].start()
        move(place + "1", k)

    layer_back(
        given.cotangent[...].astype(F32) * kept_col, normed[1], weights[1], mask, spread, dense, gated, kept[1],
        sums, outputs[1], last_between, normed_grad,
    )
    tail[3, 0:experts, :] = router[...].astype(BF16)
    move("back1")
    stream_grad = layer_finish(
        stream[...], normed[1], keyval_sum[1].total(), weights[1].gain1[...], weights[1].w_kv[...], middle_grad,
        normed_grad, tail.at[2, 0:pair], smalls[1],
    )
    move("finish1")
    spread_routes(given.routes.at[0], spread)
    loaded(0)

    def between(place, k=None):
        if place == "keyval":
            keyval_sum[0].start()
        move(place + "0", k)

    layer_back(
        stream_grad, normed[0], weights[0], mask, spread, dense, gated, kept[0], sums, outputs[0], between
    )
    tail[1, 0:experts, :] = router[...].astype(BF16)
    move("back0")
    input_grad[...] = layer_finish(
        given.x[...].astype(F32), normed[0], keyval_sum[0].total(), weights[0].gain1[...], weights[0].w_kv[...],
        middle_grad, normed_grad, tail.at[0, 0:pair], smalls[0],
    )
    writing[1].start()
    little.start(0)
    move("finish0")
    every = len(REST) // 4
    for number, i in enumerate(REST):
        step(i)
        if number % every == every - 1 and number // every < 4:
            little.advance(number // every)
    for copy in writing:
        copy.wait()


def run_whole(args, weights_out, shapes, sizes):
    specs, arrays = specs_of(args)
    large = [INPUTS.index(name) for name in LARGE]
    for i in large:
        specs[i] = pl.BlockSpec(memory_space=pl.ANY)
    queries, _, w_up, w_down = weights_out
    layers, own, width = queries.shape
    n = sizes["z"]
    count, flat, hidden = args[0][0].shape[0], n * own, w_up.shape[2]
    chunks = [
        Chunk(array, first, rows, order, kind, result, layer, True) for array, first, rows, order, kind, result, layer in CHUNKS
    ]
    parts = [Part(*part) for part in PARTS]
    scratch, sems = sum_scratch(chunks, [shapes.up, shapes.down, shapes.own, shapes.own] * 2 + [shapes.tail], sizes)
    small_shape = (16, width)
    results = [
        (layers, shapes.up[1], hidden), (layers,) + shapes.down, (layers,) + shapes.own[1:], (layers,) + shapes.own[1:],
        (1,) + shapes.tail,
    ]
    got = pltpu.VMEM((n - 1, shapes.group // n, shapes.pair), BF16)
    part = pltpu.VMEM((shapes.group, shapes.pair), BF16)
    one = pltpu.VMEM((count, width), F32)
    local = [pltpu.VMEM((flat, width), BF16)] * 4
    local += [pltpu.VMEM(w_up.shape[1:], BF16), pltpu.VMEM(w_down.shape[1:], BF16)]
    for _ in range(2):
        local += [pltpu.VMEM((count, width), BF16), part]
        local += [pltpu.VMEM(shape, dtype) for shape, dtype in shapes.kept]
    local += [pltpu.VMEM(shape, BF16) for shape in (shapes.up, shapes.down, shapes.own, shapes.own)] * 2
    local += [one, pltpu.VMEM((shapes.experts, width), F32), one, one, part, part]
    local += [pltpu.VMEM(shapes.tail, BF16), pltpu.VMEM(small_shape, F32)]
    local += [pltpu.VMEM(shape, dtype) for shape, dtype in shapes.sums]
    mask, spread, dense, gated = [pltpu.VMEM(shape, dtype) for shape, dtype in shapes.work]
    local += [mask, spread, dense, gated, got, got]
    small_refs = small_scratch(small_shape, sizes)
    anywhere = pl.BlockSpec(memory_space=pl.ANY)
    return pl.pallas_call(
        partial(whole_kernel, chunks, parts, len(scratch)),
        out_shape=[jax.ShapeDtypeStruct((count, width), BF16), jax.ShapeDtypeStruct((count, width), F32)]
        + [jax.ShapeDtypeStruct(shape, BF16) for shape in results]
        + [jax.ShapeDtypeStruct(small_shape, F32)],
        grid=(1,),
        in_specs=specs + [anywhere] * 4,
        out_specs=[anywhere] * 7 + [vmem()],
        scratch_shapes=local + scratch + small_refs[:4] + sems + small_refs[4:]
        + gather_sems(parts, sizes)
        + [pltpu.SemaphoreType.DMA((n - 1,))] * 8
        + [pltpu.SemaphoreType.DMA((2, 2)), pltpu.VMEM((count, width), BF16), one]
        + [pltpu.VMEM(arrays[i].shape, arrays[i].dtype) for i in large]
        + [pltpu.SemaphoreType.DMA((2,)), pltpu.SemaphoreType.DMA((len(large),))],
        compiler_params=pltpu.CompilerParams(
            collective_id=5, has_side_effects=True, vmem_limit_bytes=63 << 20
        ),
        name="both_blocks",
    )(*arrays, *weights_out)


def widen_kernel(*refs):
    up, down, query, out, result, grad, tail, small = refs[:8]
    up_out, down_out, query_out, out_out, result_out, grad_out, kv, router, gain1, bias1, gain2, bias2, counts = refs[8:]
    for source, target in ((up, up_out), (down, down_out), (query, query_out), (out, out_out), (grad, grad_out)):
        target[...] = source[...].astype(F32)
    result_out[...] = result[...]

    @pl.when(pl.program_id(0) == 0)
    def _():
        rows = small.shape[0] // 2
        for l in range(2):
            kv[l] = tail[2 * l].astype(F32).T
            router[l] = tail[2 * l + 1, 0 : router.shape[1], :].astype(F32)
            row = slice(l, l + 1)
            for i, target in enumerate((gain1, bias1, gain2, bias2)):
                target[row, :] = small[l * rows + i : l * rows + i + 1, :]
            counts[row, :] = small[l * rows + 4 : l * rows + 5, 0 : counts.shape[1]]


def widen(result, grad, up, down, query, out, tail, small, experts):
    layers, n, rows, width = down.shape
    cuts = n // 2
    steps = layers * cuts
    blocked, whole = [], []
    for array in (up, down, query, out):
        if array.ndim == 4:
            blocked.append(pl.BlockSpec((None, n // cuts, rows, width), lambda i: (i // cuts, i % cuts, 0, 0)))
        else:
            block = (None, array.shape[1] // cuts, array.shape[2])
            blocked.append(pl.BlockSpec(block, lambda i: (i // cuts, i % cuts, 0)))
    for array in (result, grad):
        blocked.append(pl.BlockSpec((array.shape[0] // steps, array.shape[1]), lambda i: (i, 0)))
    tail = tail.reshape(tail.shape[1:])
    shapes = [(layers, width, tail.shape[1]), (layers, experts, width)] + [(layers, width)] * 4 + [(layers, experts)]

    def fixed(shape):
        return pl.BlockSpec(shape, lambda i: (0,) * len(shape))

    return pl.pallas_call(
        widen_kernel,
        out_shape=[jax.ShapeDtypeStruct(a.shape, F32) for a in (up, down, query, out)]
        + [jax.ShapeDtypeStruct(a.shape, a.dtype) for a in (result, grad)]
        + [jax.ShapeDtypeStruct(shape, F32) for shape in shapes],
        grid=(steps,),
        in_specs=blocked + [fixed(tail.shape), fixed(small.shape)],
        out_specs=blocked + [fixed(shape) for shape in shapes],
        compiler_params=pltpu.CompilerParams(vmem_limit_bytes=VMEM_LIMIT),
        name="widen",
    )(up, down, query, out, result, grad, tail, small)


def specs_of(args):
    specs, arrays = [], []
    for array, layer in args:
        arrays.append(array)
        if layer == "smem":
            specs.append(pl.BlockSpec(memory_space=pltpu.SMEM))
        elif layer is None:
            specs.append(pl.BlockSpec(array.shape, lambda *_, nd=array.ndim: (0,) * nd, pipeline_mode=pl.Buffered(1)))
        else:
            specs.append(layer_spec(array, layer))
    return specs, arrays


def call(kernel, args, outs, scratch, name):
    specs, arrays = specs_of(args)
    return pl.pallas_call(
        kernel,
        out_shape=[jax.ShapeDtypeStruct(shape, dtype) for shape, dtype in outs],
        grid=(1,),
        in_specs=specs,
        out_specs=[pl.BlockSpec(shape, lambda *_, nd=len(shape): (0,) * nd, pipeline_mode=pl.Buffered(1)) for shape, _ in outs],
        scratch_shapes=[pltpu.VMEM(shape, dtype) for shape, dtype in scratch],
        compiler_params=pltpu.CompilerParams(vmem_limit_bytes=VMEM_LIMIT),
        name=name,
    )(*arrays)


def body(
    tokens, cotangent, routes, keep, lengths, norm1_gain, norm1_bias, w_kv, w_router, w_query, w_out,
    norm2_gain, norm2_bias, w_up, w_down,
):
    n = lax.axis_size(EXP)
    dp = lax.axis_size("dp")
    layers, width, pair = w_kv.shape
    count = tokens.shape[1]
    group = routes.shape[2]
    topk = routes.shape[3]
    experts = w_router.shape[2]
    head = w_query.shape[3]
    local = w_query.shape[1]
    hidden = w_up.shape[2]
    flat = experts * head
    own = local * head
    x0 = tokens[0]
    routes_t = jnp.swapaxes(routes[:, 0], 1, 2)
    router_t = jnp.swapaxes(w_router, 1, 2)
    gain1, bias1, gain2, bias2 = norm1_gain, norm1_bias, norm2_gain, norm2_bias
    queries_t = jnp.swapaxes(w_query, 2, 3).reshape(layers, own, width)
    outs = w_out.reshape(layers, own, width)
    sizes = axis_sizes()

    def rows_of(least):
        return -(-least // (16 * dp)) * 16 * dp

    kept_shapes = [
        ((count, experts), F32), ((topk, count, LANES), BF16), ((topk, 8, count), F32),
        ((topk, count, LANES), BF16), ((count, flat), BF16), ((count, width), F32),
    ]
    work = [((group, count), F32), ((topk, count, LANES), jnp.int32), ((count, flat), F32), ((count, flat), F32)]
    sum_shapes = [((count, width), F32), ((group, pair), F32), ((group, pair), F32), ((count, experts), F32)]
    out_shapes = [
        ((n, rows_of(width), hidden // n), BF16), ((n, rows_of(hidden // n), width), BF16),
        ((n, rows_of(own), width), BF16), ((n, rows_of(own), width), BF16),
        ((experts, width), F32), ((group, pair), BF16), ((8, width), F32), ((count, width), F32), ((count, width), F32),
    ]
    if n * dp == 32 and layers == 2:
        all_shapes = Refs(
            up=out_shapes[0][0], down=out_shapes[1][0], own=out_shapes[2][0], tail=(n, rows_of(pair), width), group=group,
            pair=pair, experts=experts, kept=kept_shapes, sums=sum_shapes, work=work,
        )
        given = [
            (x0, None), (cotangent[0], None), (routes_t, None), (lengths, "smem"), (keep, None), (gain1, None),
            (bias1, None), (w_kv, None), (router_t, None), (gain2, None), (bias2, None),
        ]
        results = run_whole(given, (queries_t, outs, w_up, w_down), all_shapes, sizes)
        up, down, expert_query, expert_out, activations, input_grad, kv, router, *norms, counts = widen(*results, experts)
        expert_query = jnp.swapaxes(expert_query.reshape(layers, local, head, width), 2, 3)
        return (
            activations[None], input_grad[None], norms[0], norms[1], kv, jnp.swapaxes(router, 1, 2), expert_query,
            expert_out.reshape(layers, local, head, width), norms[2], norms[3], up, down.reshape(layers, hidden, width), counts,
        )
    else:
        gathered = gather_all((queries_t, outs), sizes, 2)
        wq, wo = gathered[0::2], gathered[1::2]
        def weights(l):
            return [(gain1, None), (bias1, None), (w_kv, l), (router_t, l), (wq[l], None), (wo[l], None), (gain2, None), (bias2, None), (w_up, l), (w_down, l)]


        normed0, keyval0 = call(
            pre_kernel, [(x0, None), (gain1, None), (bias1, None), (w_kv, 0)],
            [((count, width), BF16), ((count, pair), BF16)], [], "pre",
        )
        keyval0 = share(keyval0, n, False, 0, "share").reshape(group, pair)
        *kept0, x1, normed1, keyval1, small0 = call(
            first_kernel,
            weights(0) + [(x0, None), (normed0, None), (keyval0, None), (routes_t, 0), (lengths, "smem"), (keep, None), (gain1, None), (bias1, None), (w_kv, 1)],
            kept_shapes + [((count, width), F32), ((count, width), BF16), ((count, pair), BF16), ((8, width), F32)],
            work, "first",
        )
        keyval1 = share(keyval1, n, False, 0, "share").reshape(group, pair)
        activations, up1, down1, out1, query1, router1, part1, small1, mid1, ngrad1 = call(
            turn_kernel,
            weights(1) + [(x1, None), (normed1, None), (keyval1, None), (routes_t, 1), (lengths, "smem"), (keep, None), (cotangent[0], None)],
            [((count, width), BF16)] + out_shapes, kept_shapes + sum_shapes + work, "turn",
        )
        tail_rows = rows_of(pair)
        result_shapes = [
            (layers,) + up1.shape[1:2] + (hidden,), (layers,) + down1.shape, (layers,) + query1.shape[1:],
            (layers,) + out1.shape[1:], (1, n, tail_rows, width),
        ]
        received1 = share(part1, n, True, 1, "scatter")
        kv1, small1, up0, down0, out0, query0, router0, part0, small0, mid0, ngrad0 = call(
            back_kernel,
            weights(0) + [(x1, None), (normed1, None), (received1, None), (gain1, None), (w_kv, 1), (mid1, None), (ngrad1, None), (small1, None),
             (normed0, None), (routes_t, 0), (lengths, "smem"), (keep, None), (small0, None), (keyval0, None)] + [(v, None) for v in kept0],
            [((pair, width), BF16), ((8, width), F32)] + out_shapes, sum_shapes + work, "back",
        )
        received0 = share(part0, n, True, 1, "scatter")
        kv0, small0, input_grad = call(
            end_kernel,
            [(x0, None), (normed0, None), (received0, None), (gain1, None), (w_kv, 0), (mid0, None), (ngrad0, None), (small0, None)],
            [((pair, width), BF16), ((8, width), F32), ((count, width), F32)], [], "end",
        )
        tail = jnp.zeros((n, tail_rows, width), BF16)
        for block, rows in enumerate((kv0, router0, kv1, router1)):
            tail = tail.at[block, : rows.shape[0]].set(rows.astype(BF16))
        chunks, starts = sum_plan(n, width, hidden // n, own, dp, tail_rows)
        arrays = [up1, down1, query1, out1, up0, down0, query0, out0, tail]
        up, down, expert_query, expert_out, tail, small = reduce_all(
            arrays, chunks, starts,
            result_shapes,
            jnp.concatenate([small0, small1]), sizes, 3,
        )
    down = down[:, :, : hidden // n].reshape(layers, hidden, width).astype(F32)
    kv = jnp.swapaxes(tail[0, 0:4:2, :pair].astype(F32), 1, 2)
    router = jnp.swapaxes(tail[0, 1:4:2, :experts].astype(F32), 1, 2)
    norms = small.reshape(layers, -1, width)
    expert_query = jnp.swapaxes(expert_query[:, :own].reshape(layers, local, head, width), 2, 3).astype(F32)
    expert_out = expert_out[:, :own].reshape(layers, local, head, width).astype(F32)
    return (
        activations[None], input_grad[None], norms[:, 0], norms[:, 1], kv, router, expert_query, expert_out,
        norms[:, 2], norms[:, 3], up[:, :width].astype(F32), down, norms[:, 4, :experts],
    )


def solution(mesh):
    return jax.shard_map(
        body,
        mesh=mesh,
        in_specs=(
            P("dp", EXP, None), P("dp", EXP, None), P(None, "dp", None, None), P("dp", None), P("dp", None),
            P(), P(), P(), P(), P(None, EXP, None, None), P(None, EXP, None, None), P(), P(), P(), P(),
        ),
        out_specs=(
            P("dp", EXP, None), P("dp", EXP, None), P(), P(), P(), P(),
            P(None, EXP, None, None), P(None, EXP, None, None), P(), P(), P(), P(), P(),
        ),
        check_vma=False,
    )
```
